32 devices in a mesh: ctx: 4 (over z), head: 8 (over y, x, core).
Axes of the slice: x: 2, y: 2, z: 4, core: 2. Of those that a mesh axis runs over, the one named last changes fastest.
Arguments:
- tokens_in: bfloat16 [1024, 4096], P('ctx', 'head'), may hold values from -6 to 6
- w_qkv: bfloat16 [4096, 8, 384], P(None, 'head'), may hold values from -0.125 to 0.125
- w_out: bfloat16 [8, 128, 4096], P('head'), may hold values from -0.75 to 0.75
- codebook: bfloat16 [8, 512, 128], P('head'), may hold values from -184 to 184
- codes: int32 [8, 1024], P('head', 'ctx'), may hold values from 0 to 511
- reach: int32 [4], P('ctx'), may hold values from 1 to 256, as said below
Outputs:
- mixed: bfloat16 [1024, 4096], P(('ctx', 'head'))
The draws below stay inside these ranges and needn't reach their ends.
Inputs may be any that keep to these rules, and one draw needn't show every extreme that they name: reach[g] is how many of the last positions of block g - 1 block g sees with exact keys; reach[0] has no effect.
All inputs are finite; a program needn't handle non-finite values.
Results may differ from the reference program's by a relative error of at most 0.015.
Values may be sent and summed in bfloat16 or wider, within the bound.
A program may use at most 64 MiB of HBM per device.

```python
import functools
import math
import jax
import jax.numpy as jnp
from jax import lax

D = 4096
HD = 128
CODES = 512
BLK = 256
HEADS = 8
SEQ = 1024
NBLK = 4


def draw_codebook(key, part):
    key_base = jax.random.fold_in(key, 0)
    base = 1.4 * jax.random.truncated_normal(key_base, -4.0, 4.0, (HEADS, CODES, HD), jnp.float32)
    return base.astype(jnp.bfloat16)


def draw_reach(key, part):
    key_base, key_high, key_low = jax.random.split(key, 3)
    base = jax.random.randint(key_base, (NBLK,), 1, BLK + 1, jnp.int32)
    high_pos = jax.random.randint(key_high, (), 0, NBLK, jnp.int32)
    low_pos = (high_pos + 1 + jax.random.randint(key_low, (), 0, NBLK - 1, jnp.int32)) % NBLK
    index_row = jnp.arange(NBLK, dtype=jnp.int32)
    return jnp.where(index_row == high_pos, BLK, jnp.where(index_row == low_pos, 1, base)).astype(jnp.int32)


def plant(array, rng, low, high):
    spot = [jax.random.randint(jax.random.fold_in(rng, axis), (), 0, length) for axis, length in enumerate(array.shape)]
    main_axis = array.shape.index(max(array.shape))
    neighbour = spot[:main_axis] + [(spot[main_axis] + 1) % array.shape[main_axis]] + spot[main_axis + 1:]
    return array.at[tuple(spot)].set(low).at[tuple(neighbour)].set(high)


def levels(key, extent, shards, smallest, top_value):
    def one(position, parts):
        draws = jax.random.uniform(jax.random.fold_in(jax.random.fold_in(key, 6), position), (parts,), jnp.float32, smallest / len(shards), top_value / len(shards))
        return jnp.repeat(jnp.exp(draws), extent[position] // parts).reshape((-1,) + (1,) * (len(extent) - position - 1))

    gain = one(*shards[0])
    for cut in shards[1:]:
        gain = gain * one(*cut)
    return gain


def noise(key, shape, spread, limit, pieces=(), held_as=jnp.bfloat16):
    result = jax.random.normal(key, shape, jnp.float32) * spread
    if len(pieces) > 0:
        result = levels(key, shape, pieces, -0.22, 0.18) * result
    return jnp.clip(result, min=-limit, max=limit).astype(held_as)


def setup_inputs(seed: int = 0) -> dict:
    key_of = jax.random.split(jax.random.key(seed), 7)
    tokens_in = noise(key_of[0], (SEQ, D), 1.0, 6.0, ((0, 4), (1, 8)))
    w_qkv = noise(key_of[1], (D, HEADS, 3 * HD), (D // 2) ** -0.5, 0.125, ((1, 8),))
    w_out = noise(key_of[2], (HEADS, HD, D), (HEADS * HD // 16) ** -0.5, 0.75, ((0, 8),))
    codebook = draw_codebook(jax.random.fold_in(key_of[6], 71), 0)
    codes = plant(jax.random.randint(key_of[4], (HEADS, SEQ), 0, CODES), jax.random.fold_in(key_of[4], 1), 0, CODES - 1).astype(jnp.int32)
    reach = draw_reach(jax.random.fold_in(key_of[6], 71), 0)
    return {"tokens_in": tokens_in, "w_qkv": w_qkv, "w_out": w_out, "codebook": codebook, "codes": codes, "reach": reach}


def attend_block(queries, keys_win, vals_win, cache_v, cache_c, book, reach_one, prev_flag, block_len, scale):
    exact = lax.dot_general(queries, keys_win, (((1,), (1,)), ((), ())), preferred_element_type=jnp.float32) * scale
    coded = lax.dot_general(queries, book, (((1,), (1,)), ((), ())), preferred_element_type=jnp.float32) * scale
    rows = lax.broadcasted_iota(jnp.int32, exact.shape, 0)
    cols = lax.broadcasted_iota(jnp.int32, exact.shape, 1)
    prev_ok = (cols < block_len) & (cols >= block_len - reach_one) & prev_flag
    curr_ok = (cols >= block_len) & (cols - block_len <= rows)
    allowed = prev_ok | curr_ok
    valid = cache_c > 0.5
    top = jnp.maximum(lax.optimization_barrier(jnp.max(jnp.where(allowed, exact, -jnp.inf), axis=1)), lax.optimization_barrier(jnp.max(jnp.where(valid[None, :], coded, -jnp.inf), axis=1)))
    probs = jnp.exp(jnp.where(allowed, exact - top[:, None], -jnp.inf))
    weights = jnp.exp(jnp.where(valid[None, :], coded - top[:, None], -jnp.inf))
    numer = jnp.dot(probs.astype(jnp.bfloat16), vals_win, preferred_element_type=jnp.float32)
    numer = numer + jnp.dot(weights, cache_v, precision=lax.Precision.HIGHEST)
    denom = lax.optimization_barrier(jnp.sum(probs, axis=1)) + jnp.dot(weights, cache_c, precision=lax.Precision.HIGHEST)
    return (numer / denom[:, None]).astype(jnp.bfloat16)

def shift_blocks(blocks):
    return jnp.concatenate([jnp.zeros_like(blocks[:1]), blocks[:-1]], axis=0)

def reference(tokens_in, w_qkv, w_out, codebook, codes, reach):
    scale = 1.0 / math.sqrt(HD)
    num_blocks = SEQ // BLK
    w_heads = jnp.moveaxis(w_qkv, 1, 0)
    code_ids = jnp.arange(CODES, dtype=jnp.int32)
    prev_flags = jnp.arange(num_blocks, dtype=jnp.int32) > 0
    offsets = jnp.arange(BLK, dtype=jnp.int32)
    cut = (offsets[None, :] < (BLK - reach)[:, None]).astype(jnp.float32)
    attend = jax.vmap(functools.partial(attend_block, block_len=BLK, scale=scale), in_axes=(0, 0, 0, 0, 0, None, 0, 0))

    def head_step(total, inputs):
        w_head, w_proj, book, code_row = inputs
        proj = jnp.dot(tokens_in, w_head, preferred_element_type=jnp.float32)
        queries = proj[:, :HD].astype(jnp.bfloat16)
        keys = proj[:, HD:2 * HD].astype(jnp.bfloat16)
        values = proj[:, 2 * HD:].astype(jnp.bfloat16)
        onehot = (code_row[:, None] == code_ids[None, :]).astype(jnp.float32).reshape(num_blocks, BLK, CODES)
        vals_f = values.astype(jnp.float32).reshape(num_blocks, BLK, HD)
        block_v = jnp.einsum('nbs,nbd->nsd', onehot, vals_f, precision=lax.Precision.HIGHEST)
        block_c = lax.optimization_barrier(jnp.sum(onehot, axis=1))
        before_v = shift_blocks(jnp.cumsum(block_v, axis=0) - block_v)
        before_c = shift_blocks(jnp.cumsum(block_c, axis=0) - block_c)
        masked = shift_blocks(onehot) * cut[:, :, None]
        cache_v = before_v + jnp.einsum('nbs,nbd->nsd', masked, shift_blocks(vals_f), precision=lax.Precision.HIGHEST)
        cache_c = before_c + lax.optimization_barrier(jnp.sum(masked, axis=1))
        keys_b = keys.reshape(num_blocks, BLK, HD)
        vals_b = values.reshape(num_blocks, BLK, HD)
        keys_win = jnp.concatenate([shift_blocks(keys_b), keys_b], axis=1)
        vals_win = jnp.concatenate([shift_blocks(vals_b), vals_b], axis=1)
        outs = attend(queries.reshape(num_blocks, BLK, HD), keys_win, vals_win, cache_v, cache_c, book, reach, prev_flags)
        attended = outs.reshape(SEQ, HD)
        term = jnp.dot(attended, w_proj, preferred_element_type=jnp.float32).astype(jnp.bfloat16)
        term = lax.optimization_barrier(term)
        return (total + term.astype(jnp.float32), None)
    start = jnp.zeros((SEQ, D), jnp.float32)
    total, unused = lax.scan(head_step, start, (w_heads, w_out, codebook, codes))
    return total.astype(jnp.bfloat16)
```

```python
import functools
import math

import jax
import jax.numpy as jnp
from jax import lax
from jax.experimental import pallas as pl
from jax.experimental.pallas import tpu as pltpu
from jax.sharding import PartitionSpec as P

MESH = pl.DeviceIdType.MESH
F32 = jnp.float32
BF16 = jnp.bfloat16
ROW_CHUNKS = 2
COL_CHUNKS = 4


def grid_of(chips):
    wide = 1 << ((chips.bit_length() - 1) // 2)
    return chips // wide, wide


def nt(a, b):
    return lax.dot_general(a, b, (((1,), (1,)), ((), ())), preferred_element_type=F32)


def kernel(
    sizes,
    tok, w_in, w_out, book, codes, reach, out,
    x, w, w2, book_v, codes_v, reach_s, kq, kz, vz, q_s, top_s, den_s, acc_s, att, att_p, term, got,
    local_sem, ag_send, ag_recv, fw_send, fw_recv, w2_sem, kq_send, kq_recv, k_send, k_recv,
    v_send, v_recv, att_sem, rs_send, rs_recv,
):
    ctxs, heads, blk, hd = sizes
    chips = heads // 2
    tall, wide = grid_of(chips)
    scale = 1.0 / math.sqrt(hd)
    rows = blk // ROW_CHUNKS
    cols = out.shape[1] // COL_CHUNKS
    rp = out.shape[0]
    ctx, head = lax.axis_index("ctx"), lax.axis_index("head")
    chip, core = head // 2, head % 2
    partner = (ctx, chip * 2 + 1 - core)

    def chip_at(d, sign):
        up, across = d // wide, d % wide
        row = lax.rem(chip // wide + (up if sign > 0 else tall - up), tall)
        col = lax.rem(chip % wide + (across if sign > 0 else wide - across), wide)
        return row * wide + col

    def remote(src, dst, send, recv, to):
        return pltpu.make_async_remote_copy(
            src_ref=src, dst_ref=dst, send_sem=send, recv_sem=recv, device_id=to, device_id_type=MESH
        )

    def arrived(dst, sem):
        remote(dst, dst, sem, sem, partner).wait_recv()

    copies = [
        pltpu.make_async_copy(codes, codes_v, local_sem.at[0]),
        pltpu.make_async_copy(book, book_v, local_sem.at[1]),
        pltpu.make_async_copy(reach, reach_s, local_sem.at[2]),
        pltpu.make_async_copy(tok, x.at[0, 0], local_sem.at[3]),
        pltpu.make_async_copy(w_in, w, local_sem.at[4]),
        pltpu.make_async_copy(w_out, w2.at[pl.ds(0, hd)], local_sem.at[5]),
    ]
    for copy in copies:
        copy.start()

    barrier = pltpu.get_barrier_semaphore()
    greet = [partner]
    greet += [(ctx, chip_at(d, 1) * 2 + core) for d in range(1, chips)]
    greet += [(lax.rem(ctx + e, ctxs), head) for e in range(1, ctxs)]
    for peer in greet:
        pl.semaphore_signal(barrier, inc=1, device_id=peer, device_id_type=MESH)
    pl.semaphore_wait(barrier, len(greet))

    sends = []

    def send(*args):
        copy = remote(*args)
        copy.start()
        sends.append(copy)

    def part(r):
        return pl.ds(r * rows, rows)

    for r in range(ROW_CHUNKS):
        for d in range(1, chips):
            to = (ctx, chip_at(d, 1) * 2 + core)
            send(tok.at[part(r)], x.at[d, 0, part(r)], ag_send.at[r, d], ag_recv.at[r, d], to)
        send(tok.at[part(r)], x.at[0, 1, part(r)], fw_send.at[r, 0], fw_recv.at[r, 0], partner)
    send(w_out, w2.at[pl.ds(hd, hd)], w2_sem.at[0], w2_sem.at[1], partner)

    copies[0].wait()
    copies[1].wait()
    num_codes = book_v.shape[0]
    hot = lax.broadcasted_iota(jnp.int32, (num_codes, blk), 0) == codes_v[...]
    kq[0] = lax.dot_general(
        hot.astype(F32).astype(BF16), book_v[...], (((0,), (0,)), ((), ())), preferred_element_type=F32
    ).astype(BF16)

    def later(e, src, dst, send_sem, recv_sem):
        @pl.when(ctx + e < ctxs)
        def _():
            remote(src, dst, send_sem, recv_sem, (lax.rem(ctx + e, ctxs), head)).start()

    for e in range(1, ctxs):
        later(e, kq.at[0], kq.at[e], kq_send.at[e], kq_recv.at[e])

    for copy in copies[2:]:
        copy.wait()

    for r in range(ROW_CHUNKS):
        def piece(d, other):
            source = chip_at(d, -1) * 2 + (1 - core if other else core)
            return jnp.dot(x[d, other, r * rows:(r + 1) * rows], w[source], preferred_element_type=F32)

        proj = piece(0, 0)
        arrived(x.at[0, 1, part(r)], fw_recv.at[r, 0])
        proj += piece(0, 1)
        for d in range(1, chips):
            arrived(x.at[d, 0, part(r)], ag_recv.at[r, d])
            send(x.at[d, 0, part(r)], x.at[d, 1, part(r)], fw_send.at[r, d], fw_recv.at[r, d], partner)
            proj += piece(d, 0)
        for d in range(1, chips):
            arrived(x.at[d, 1, part(r)], fw_recv.at[r, d])
            proj += piece(d, 1)
        q_s[r * rows:(r + 1) * rows] = proj[:, :hd].astype(BF16)
        kz[0, r * rows:(r + 1) * rows] = proj[:, hd:2 * hd].astype(BF16)
        vz[0, r * rows:(r + 1) * rows] = proj[:, 2 * hd:].astype(BF16)
        later(1, kz.at[0, part(r)], kz.at[1, part(r)], k_send.at[r], k_recv.at[r])
        for e in range(1, ctxs):
            later(e, vz.at[0, part(r)], vz.at[e, part(r)], v_send.at[r, e], v_recv.at[r, e])

    queries = q_s[...]
    scores = nt(queries, kz[0])
    seen = lax.broadcasted_iota(jnp.int32, scores.shape, 1) <= lax.broadcasted_iota(
        jnp.int32, scores.shape, 0
    )
    scores = jnp.where(seen, scores, -jnp.inf)
    top = jnp.max(scores, axis=1, keepdims=True)
    probs = jnp.exp((scores - top) * scale)
    top_s[...] = jnp.broadcast_to(top, top_s.shape)
    den_s[...] = jnp.broadcast_to(jnp.sum(probs, axis=1, keepdims=True), den_s.shape)
    acc_s[...] = jnp.dot(probs.astype(BF16), vz[0], preferred_element_type=F32)

    for e in range(1, ctxs):
        @pl.when(ctx >= e)
        def _():
            arrived(kq.at[e], kq_recv.at[e])
            keys = kq[e]
            if e == 1:
                for r in range(ROW_CHUNKS):
                    arrived(kz.at[1, part(r)], k_recv.at[r])
                position = lax.broadcasted_iota(jnp.int32, keys.shape, 0)
                keys = jnp.where(position >= blk - reach_s[0], kz[1], keys)
            scores = nt(q_s[...], keys)
            old = top_s[...][:, :1]
            top = jnp.maximum(old, jnp.max(scores, axis=1, keepdims=True))
            fade = jnp.exp((old - top) * scale)
            probs = jnp.exp((scores - top) * scale)
            for r in range(ROW_CHUNKS):
                arrived(vz.at[e, part(r)], v_recv.at[r, e])
            top_s[...] = jnp.broadcast_to(top, top_s.shape)
            den_s[...] = den_s[...] * fade + jnp.sum(probs, axis=1, keepdims=True)
            acc_s[...] = acc_s[...] * fade + jnp.dot(
                probs.astype(BF16), vz[e], preferred_element_type=F32
            )

    attended = acc_s[...] / den_s[...]
    for h in range(heads):
        att[h % 2, h // 2] = attended[h * rp:(h + 1) * rp].astype(BF16)
    send(att.at[1 - core], att_p, att_sem.at[0], att_sem.at[1], partner)
    mine = att[core].astype(F32).reshape(chips * rp, hd).astype(BF16)
    arrived(att_p, att_sem.at[1])
    other = att_p[...].astype(F32).reshape(chips * rp, hd).astype(BF16)
    arrived(w2.at[pl.ds(hd, hd)], w2_sem.at[1])
    both = jnp.concatenate([mine, other], axis=1)

    for j in range(COL_CHUNKS):
        block = jnp.dot(both, w2[:, j * cols:(j + 1) * cols], preferred_element_type=F32)
        for c in range(chips):
            term[j, c] = block[c * rp:(c + 1) * rp].astype(BF16)
        for d in range(1, chips):
            peer = chip_at(d, 1)
            send(term.at[j, peer], got.at[j, d], rs_send.at[j, d], rs_recv.at[j, d], (ctx, peer * 2 + core))

    for j in range(COL_CHUNKS):
        total = term[j, chip].astype(F32)
        for d in range(1, chips):
            arrived(got.at[j, d], rs_recv.at[j, d])
            total += got[j, d].astype(F32)
        out[:, j * cols:(j + 1) * cols] = total.astype(BF16)

    for copy in sends:
        copy.wait_send()
    for e in range(1, ctxs):
        @pl.when(ctx + e < ctxs)
        def _():
            remote(kq.at[0], kq.at[e], kq_send.at[e], kq_recv.at[e], partner).wait_send()
            for r in range(ROW_CHUNKS):
                if e == 1:
                    remote(kz.at[0, part(r)], kz.at[1, part(r)], k_send.at[r], k_recv.at[r], partner).wait_send()
                remote(
                    vz.at[0, part(r)], vz.at[e, part(r)], v_send.at[r, e], v_recv.at[r, e], partner
                ).wait_send()


def solution(mesh):
    ctxs, heads = mesh.shape["ctx"], mesh.shape["head"]
    chips = heads // 2

    def on_device(tokens_in, w_qkv, w_out, codebook, codes, reach):
        blk, depth = tokens_in.shape
        num_codes, hd = codebook.shape[1:]
        wide = w_out.shape[2]
        rp = blk // heads
        cols = wide // COL_CHUNKS
        dma = pltpu.SemaphoreType.DMA
        return pl.pallas_call(
            functools.partial(kernel, (ctxs, heads, blk, hd)),
            out_shape=jax.ShapeDtypeStruct((rp, wide), BF16),
            in_specs=[pl.BlockSpec(memory_space=pl.ANY)] * 6,
            out_specs=pl.BlockSpec(memory_space=pltpu.VMEM),
            scratch_shapes=[
                pltpu.VMEM((chips, 2, blk, depth), BF16),
                pltpu.VMEM((heads, depth, 3 * hd), BF16),
                pltpu.VMEM((2 * hd, wide), BF16),
                pltpu.VMEM((num_codes, hd), BF16),
                pltpu.VMEM((1, blk), jnp.int32),
                pltpu.SMEM((1,), jnp.int32),
                pltpu.VMEM((ctxs, blk, hd), BF16),
                pltpu.VMEM((2, blk, hd), BF16),
                pltpu.VMEM((ctxs, blk, hd), BF16),
                pltpu.VMEM((blk, hd), BF16),
                pltpu.VMEM((blk, hd), F32),
                pltpu.VMEM((blk, hd), F32),
                pltpu.VMEM((blk, hd), F32),
                pltpu.VMEM((2, chips, rp, hd), BF16),
                pltpu.VMEM((chips, rp, hd), BF16),
                pltpu.VMEM((COL_CHUNKS, chips, rp, cols), BF16),
                pltpu.VMEM((COL_CHUNKS, chips, rp, cols), BF16),
                dma((6,)),
                dma((ROW_CHUNKS, chips)),
                dma((ROW_CHUNKS, chips)),
                dma((ROW_CHUNKS, chips)),
                dma((ROW_CHUNKS, chips)),
                dma((2,)),
                dma((ctxs,)),
                dma((ctxs,)),
                dma((ROW_CHUNKS,)),
                dma((ROW_CHUNKS,)),
                dma((ROW_CHUNKS, ctxs)),
                dma((ROW_CHUNKS, ctxs)),
                dma((2,)),
                dma((COL_CHUNKS, chips)),
                dma((COL_CHUNKS, chips)),
            ],
            compiler_params=pltpu.CompilerParams(
                collective_id=0, has_side_effects=True, vmem_limit_bytes=48 * 1024 * 1024
            ),
            cost_estimate=pl.CostEstimate(
                flops=2 * blk * heads * depth * 3 * hd, bytes_accessed=6 * 1024 * 1024, transcendentals=blk * blk
            ),
        )(
            tokens_in, w_qkv[:, 0, :].reshape(heads, depth, 3 * hd), w_out[0], codebook[0], codes, reach
        )

    in_specs = (
        P("ctx", "head"),
        P(None, "head", None),
        P("head", None, None),
        P("head", None, None),
        P("head", "ctx"),
        P("ctx"),
    )
    return jax.shard_map(
        on_device, mesh=mesh, in_specs=in_specs, out_specs=P(("ctx", "head"), None), check_vma=False
    )
```

```python
import functools
import math

import jax
import jax.numpy as jnp
from jax import lax
from jax.experimental import pallas as pl
from jax.experimental.pallas import tpu as pltpu
from jax.sharding import PartitionSpec as P

MESH = pl.DeviceIdType.MESH
F32 = jnp.float32
BF16 = jnp.bfloat16
ROW_CHUNKS = 2
COL_CHUNKS = 4


def grid_of(chips):
    wide = 1 << ((chips.bit_length() - 1) // 2)
    return chips // wide, wide


def nt(a, b):
    return lax.dot_general(a, b, (((1,), (1,)), ((), ())), preferred_element_type=F32)


def kernel(
    sizes,
    tok, w_in, w_out, book, codes, reach, out,
    x, w, w2, book_v, codes_v, reach_s, kq, kz, vz, q_s, top_s, den_s, acc_s, att, att_p, term, got, pre,
    local_sem, ag_send, ag_recv, fw_send, fw_recv, rl_send, rl_recv, w2_sem, kq_send, kq_recv, k_send, k_recv,
    v_send, v_recv, att_sem, rs_send, rs_recv,
):
    ctxs, heads, blk, hd = sizes
    chips = heads // 2
    tall, wide = grid_of(chips)
    scale = 1.0 / math.sqrt(hd)
    rows = blk // ROW_CHUNKS
    cols = out.shape[1] // COL_CHUNKS
    rp = out.shape[0]
    ctx, head = lax.axis_index("ctx"), lax.axis_index("head")
    chip, core = head // 2, head % 2
    partner = (ctx, chip * 2 + 1 - core)

    def chip_at(d, sign):
        up, across = d // wide, d % wide
        row = lax.rem(chip // wide + (up if sign > 0 else tall - up), tall)
        col = lax.rem(chip % wide + (across if sign > 0 else wide - across), wide)
        return row * wide + col

    def remote(src, dst, send, recv, to):
        return pltpu.make_async_remote_copy(
            src_ref=src, dst_ref=dst, send_sem=send, recv_sem=recv, device_id=to, device_id_type=MESH
        )

    def arrived(dst, sem):
        remote(dst, dst, sem, sem, partner).wait_recv()

    copies = [
        pltpu.make_async_copy(codes, codes_v, local_sem.at[0]),
        pltpu.make_async_copy(book, book_v, local_sem.at[1]),
        pltpu.make_async_copy(reach, reach_s, local_sem.at[2]),
        pltpu.make_async_copy(tok, x.at[0, 0], local_sem.at[3]),
        pltpu.make_async_copy(w_in, w, local_sem.at[4]),
        pltpu.make_async_copy(w_out, w2.at[pl.ds(0, hd)], local_sem.at[5]),
    ]
    for copy in copies:
        copy.start()

    barrier = pltpu.get_barrier_semaphore()
    greet = [partner]
    greet += [(ctx, chip_at(d, 1) * 2 + core) for d in range(1, chips)]
    greet += [(lax.rem(ctx + e, ctxs), head) for e in range(1, ctxs)]
    for peer in greet:
        pl.semaphore_signal(barrier, inc=1, device_id=peer, device_id_type=MESH)
    pl.semaphore_wait(barrier, len(greet))

    relayed = (tall, wide) == (2, 2)
    direct = (1, 2) if relayed else range(1, chips)
    sends = []

    def send(*args):
        copy = remote(*args)
        copy.start()
        sends.append(copy)

    def part(r):
        return pl.ds(r * rows, rows)

    def across(d):
        return (ctx, chip_at(d, 1) * 2 + core)

    def half(r, d):
        return pl.ds(r * rows + (d - 1) * (rows // 2), rows // 2)

    def to_partner(r, d):
        send(x.at[d, 0, part(r)], x.at[d, 1, part(r)], fw_send.at[r, d], fw_recv.at[r, d], partner)

    def take_direct(r):
        for d in direct:
            arrived(x.at[d, 0, part(r)], ag_recv.at[r, d])
            if relayed:
                send(
                    x.at[d, 0, half(r, d)], x.at[3, 0, half(r, d)],
                    rl_send.at[r, d], rl_recv.at[r, d], across(3 - d),
                )
            to_partner(r, d)

    for r in range(ROW_CHUNKS):
        for d in direct:
            send(tok.at[part(r)], x.at[d, 0, part(r)], ag_send.at[r, d], ag_recv.at[r, d], across(d))
        send(tok.at[part(r)], x.at[0, 1, part(r)], fw_send.at[r, 0], fw_recv.at[r, 0], partner)
    send(w_out, w2.at[pl.ds(hd, hd)], w2_sem.at[0], w2_sem.at[1], partner)

    copies[0].wait()
    copies[1].wait()
    num_codes = book_v.shape[0]
    hot = lax.broadcasted_iota(jnp.int32, (num_codes, blk), 0) == codes_v[...]
    kq[0] = lax.dot_general(
        hot.astype(F32).astype(BF16), book_v[...], (((0,), (0,)), ((), ())), preferred_element_type=F32
    ).astype(BF16)

    def later(e, src, dst, send_sem, recv_sem):
        @pl.when(ctx + e < ctxs)
        def _():
            remote(src, dst, send_sem, recv_sem, (lax.rem(ctx + e, ctxs), head)).start()

    for e in range(1, ctxs):
        later(e, kq.at[0], kq.at[e], kq_send.at[e], kq_recv.at[e])

    for copy in copies[2:]:
        copy.wait()

    take_direct(0)
    for r in range(ROW_CHUNKS):
        def piece(d, other):
            source = chip_at(d, -1) * 2 + (1 - core if other else core)
            return jnp.dot(x[d, other, r * rows:(r + 1) * rows], w[source], preferred_element_type=F32)

        if r + 1 < ROW_CHUNKS:
            take_direct(r + 1)
        proj = piece(0, 0)
        arrived(x.at[0, 1, part(r)], fw_recv.at[r, 0])
        proj += piece(0, 1)
        for d in direct:
            proj += piece(d, 0)
        if relayed:
            for d in direct:
                arrived(x.at[3, 0, half(r, d)], rl_recv.at[r, d])
            to_partner(r, 3)
            proj += piece(3, 0)
        for d in range(1, chips):
            arrived(x.at[d, 1, part(r)], fw_recv.at[r, d])
            proj += piece(d, 1)
        q_s[r * rows:(r + 1) * rows] = proj[:, :hd].astype(BF16)
        kz[0, r * rows:(r + 1) * rows] = proj[:, hd:2 * hd].astype(BF16)
        vz[0, r * rows:(r + 1) * rows] = proj[:, 2 * hd:].astype(BF16)
        later(1, kz.at[0, part(r)], kz.at[1, part(r)], k_send.at[r], k_recv.at[r])
        for e in range(1, ctxs):
            later(e, vz.at[0, part(r)], vz.at[e, part(r)], v_send.at[r, e], v_recv.at[r, e])

    queries = q_s[...]
    scores = nt(queries, kz[0])
    seen = lax.broadcasted_iota(jnp.int32, scores.shape, 1) <= lax.broadcasted_iota(
        jnp.int32, scores.shape, 0
    )
    scores = jnp.where(seen, scores, -jnp.inf)
    top = jnp.max(scores, axis=1, keepdims=True)
    probs = jnp.exp((scores - top) * scale)
    top_s[...] = jnp.broadcast_to(top, top_s.shape)
    den_s[...] = jnp.broadcast_to(jnp.sum(probs, axis=1, keepdims=True), den_s.shape)
    acc_s[...] = jnp.dot(probs.astype(BF16), vz[0], preferred_element_type=F32)

    for e in range(1, ctxs):
        @pl.when(ctx >= e)
        def _():
            arrived(kq.at[e], kq_recv.at[e])
            keys = kq[e]
            if e == 1:
                for r in range(ROW_CHUNKS):
                    arrived(kz.at[1, part(r)], k_recv.at[r])
                position = lax.broadcasted_iota(jnp.int32, keys.shape, 0)
                keys = jnp.where(position >= blk - reach_s[0], kz[1], keys)
            scores = nt(q_s[...], keys)
            old = top_s[...][:, :1]
            top = jnp.maximum(old, jnp.max(scores, axis=1, keepdims=True))
            fade = jnp.exp((old - top) * scale)
            probs = jnp.exp((scores - top) * scale)
            for r in range(ROW_CHUNKS):
                arrived(vz.at[e, part(r)], v_recv.at[r, e])
            top_s[...] = jnp.broadcast_to(top, top_s.shape)
            den_s[...] = den_s[...] * fade + jnp.sum(probs, axis=1, keepdims=True)
            acc_s[...] = acc_s[...] * fade + jnp.dot(
                probs.astype(BF16), vz[e], preferred_element_type=F32
            )

    attended = acc_s[...] / den_s[...]
    for h in range(heads):
        att[h % 2, h // 2] = attended[h * rp:(h + 1) * rp].astype(BF16)
    send(att.at[1 - core], att_p, att_sem.at[0], att_sem.at[1], partner)
    mine = att[core].astype(F32).reshape(chips * rp, hd).astype(BF16)
    arrived(att_p, att_sem.at[1])
    other = att_p[...].astype(F32).reshape(chips * rp, hd).astype(BF16)
    arrived(w2.at[pl.ds(hd, hd)], w2_sem.at[1])
    both = jnp.concatenate([mine, other], axis=1)

    for j in range(COL_CHUNKS):
        block = jnp.dot(both, w2[:, j * cols:(j + 1) * cols], preferred_element_type=F32)
        for c in range(chips):
            term[j, c] = block[c * rp:(c + 1) * rp].astype(BF16)
        if relayed:
            first = 1 + j % 2
            send(term.at[j, chip_at(3, 1)], got.at[j, 3], rs_send.at[j, 3], rs_recv.at[j, 3], across(first))
        else:
            for d in direct:
                send(term.at[j, chip_at(d, 1)], got.at[j, d], rs_send.at[j, d], rs_recv.at[j, d], across(d))

    if relayed:
        for j in range(COL_CHUNKS):
            first = 1 + j % 2
            send(
                term.at[j, chip_at(first, 1)], got.at[j, first],
                rs_send.at[j, first], rs_recv.at[j, first], across(first),
            )
        for j in range(COL_CHUNKS):
            second = 2 - j % 2
            arrived(got.at[j, 3], rs_recv.at[j, 3])
            pair = got[j, 3].astype(F32) + term[j, chip_at(second, 1)].astype(F32)
            pre[j] = pair.astype(BF16)
            send(
                pre.at[j], got.at[j, second], rs_send.at[j, second], rs_recv.at[j, second], across(second)
            )

    for j in range(COL_CHUNKS):
        total = term[j, chip].astype(F32)
        for d in direct:
            arrived(got.at[j, d], rs_recv.at[j, d])
            total += got[j, d].astype(F32)
        out[:, j * cols:(j + 1) * cols] = total.astype(BF16)

    for copy in sends:
        copy.wait_send()
    for e in range(1, ctxs):
        @pl.when(ctx + e < ctxs)
        def _():
            remote(kq.at[0], kq.at[e], kq_send.at[e], kq_recv.at[e], partner).wait_send()
            for r in range(ROW_CHUNKS):
                if e == 1:
                    remote(kz.at[0, part(r)], kz.at[1, part(r)], k_send.at[r], k_recv.at[r], partner).wait_send()
                remote(
                    vz.at[0, part(r)], vz.at[e, part(r)], v_send.at[r, e], v_recv.at[r, e], partner
                ).wait_send()


def solution(mesh):
    ctxs, heads = mesh.shape["ctx"], mesh.shape["head"]
    chips = heads // 2

    def on_device(tokens_in, w_qkv, w_out, codebook, codes, reach):
        blk, depth = tokens_in.shape
        num_codes, hd = codebook.shape[1:]
        wide = w_out.shape[2]
        rp = blk // heads
        cols = wide // COL_CHUNKS
        dma = pltpu.SemaphoreType.DMA
        return pl.pallas_call(
            functools.partial(kernel, (ctxs, heads, blk, hd)),
            out_shape=jax.ShapeDtypeStruct((rp, wide), BF16),
            in_specs=[pl.BlockSpec(memory_space=pltpu.HBM)] * 6,
            out_specs=pl.BlockSpec(memory_space=pltpu.VMEM),
            scratch_shapes=[
                pltpu.VMEM((chips, 2, blk, depth), BF16),
                pltpu.VMEM((heads, depth, 3 * hd), BF16),
                pltpu.VMEM((2 * hd, wide), BF16),
                pltpu.VMEM((num_codes, hd), BF16),
                pltpu.VMEM((1, blk), jnp.int32),
                pltpu.SMEM((1,), jnp.int32),
                pltpu.VMEM((ctxs, blk, hd), BF16),
                pltpu.VMEM((2, blk, hd), BF16),
                pltpu.VMEM((ctxs, blk, hd), BF16),
                pltpu.VMEM((blk, hd), BF16),
                pltpu.VMEM((blk, hd), F32),
                pltpu.VMEM((blk, hd), F32),
                pltpu.VMEM((blk, hd), F32),
                pltpu.VMEM((2, chips, rp, hd), BF16),
                pltpu.VMEM((chips, rp, hd), BF16),
                pltpu.VMEM((COL_CHUNKS, chips, rp, cols), BF16),
                pltpu.VMEM((COL_CHUNKS, chips, rp, cols), BF16),
                pltpu.VMEM((COL_CHUNKS, rp, cols), BF16),
                dma((6,)),
                dma((ROW_CHUNKS, chips)),
                dma((ROW_CHUNKS, chips)),
                dma((ROW_CHUNKS, chips)),
                dma((ROW_CHUNKS, chips)),
                dma((ROW_CHUNKS, chips)),
                dma((ROW_CHUNKS, chips)),
                dma((2,)),
                dma((ctxs,)),
                dma((ctxs,)),
                dma((ROW_CHUNKS,)),
                dma((ROW_CHUNKS,)),
                dma((ROW_CHUNKS, ctxs)),
                dma((ROW_CHUNKS, ctxs)),
                dma((2,)),
                dma((COL_CHUNKS, chips)),
                dma((COL_CHUNKS, chips)),
            ],
            compiler_params=pltpu.CompilerParams(
                collective_id=0, has_side_effects=True, vmem_limit_bytes=60 * 1024 * 1024
            ),
            cost_estimate=pl.CostEstimate(
                flops=2 * blk * heads * depth * 3 * hd, bytes_accessed=6 * 1024 * 1024, transcendentals=blk * blk
            ),
        )(
            tokens_in, w_qkv[:, 0, :].reshape(heads, depth, 3 * hd), w_out[0], codebook[0], codes, reach
        )

    in_specs = (
        P("ctx", "head"),
        P(None, "head", None),
        P("head", None, None),
        P("head", None, None),
        P("head", "ctx"),
        P("ctx"),
    )
    return jax.shard_map(
        on_device, mesh=mesh, in_specs=in_specs, out_specs=P(("ctx", "head"), None), check_vma=False
    )
```

```python
import functools
import math

import jax
import jax.numpy as jnp
from jax import lax
from jax.experimental import pallas as pl
from jax.experimental.pallas import tpu as pltpu
from jax.sharding import PartitionSpec as P

MESH = pl.DeviceIdType.MESH
F32 = jnp.float32
BF16 = jnp.bfloat16
ROW_CHUNKS = 2
COL_CHUNKS = 4


def grid_of(chips):
    wide = 1 << ((chips.bit_length() - 1) // 2)
    return chips // wide, wide


def nt(a, b):
    return lax.dot_general(a, b, (((1,), (1,)), ((), ())), preferred_element_type=F32)


def kernel(
    sizes,
    tok, w_in, w_out, book, codes, reach, out,
    x, w, w2, book_v, codes_v, reach_s, kq, kz, vz, q_s, top_s, den_s, acc_s, fade_s, score_s, prob_s, out_v, att, att_p, term, got, pre,
    local_sem, ag_send, ag_recv, fw_send, fw_recv, rl_send, rl_recv, w2_sem, kq_send, kq_recv, k_send, k_recv,
    v_send, v_recv, att_sem, rs_send, rs_recv, out_sem,
):
    ctxs, heads, blk, hd = sizes
    chips = heads // 2
    tall, wide = grid_of(chips)
    scale = 1.0 / math.sqrt(hd)
    rows = blk // ROW_CHUNKS
    cols = out.shape[1] // COL_CHUNKS
    rp = out.shape[0]
    ctx, head = lax.axis_index("ctx"), lax.axis_index("head")
    chip, core = head // 2, head % 2
    partner = (ctx, chip * 2 + 1 - core)

    def chip_at(d, sign):
        up, across = d // wide, d % wide
        row = lax.rem(chip // wide + (up if sign > 0 else tall - up), tall)
        col = lax.rem(chip % wide + (across if sign > 0 else wide - across), wide)
        return row * wide + col

    def remote(src, dst, send, recv, to):
        return pltpu.make_async_remote_copy(
            src_ref=src, dst_ref=dst, send_sem=send, recv_sem=recv, device_id=to, device_id_type=MESH
        )

    def arrived(dst, sem):
        remote(dst, dst, sem, sem, partner).wait_recv()

    copies = [
        pltpu.make_async_copy(codes, codes_v, local_sem.at[0]),
        pltpu.make_async_copy(book, book_v, local_sem.at[1]),
        pltpu.make_async_copy(reach, reach_s, local_sem.at[2]),
        pltpu.make_async_copy(tok, x.at[0, 0], local_sem.at[3]),
        pltpu.make_async_copy(w_in, w, local_sem.at[4]),
        pltpu.make_async_copy(w_out, w2.at[pl.ds(0, hd)], local_sem.at[5]),
    ]
    for copy in copies:
        copy.start()

    barrier = pltpu.get_barrier_semaphore()
    greet = [partner]
    greet += [(ctx, chip_at(d, 1) * 2 + core) for d in range(1, chips)]
    greet += [(lax.rem(ctx + e, ctxs), head) for e in range(1, ctxs)]
    for peer in greet:
        pl.semaphore_signal(barrier, inc=1, device_id=peer, device_id_type=MESH)
    pl.semaphore_wait(barrier, len(greet))

    relayed = (tall, wide) == (2, 2)
    direct = (1, 2) if relayed else range(1, chips)
    sends = []

    def send(*args):
        copy = remote(*args)
        copy.start()
        sends.append(copy)

    def part(r):
        return pl.ds(r * rows, rows)

    def across(d):
        return (ctx, chip_at(d, 1) * 2 + core)

    def half(r, d):
        return pl.ds(r * rows + (d - 1) * (rows // 2), rows // 2)

    def to_partner(r, d):
        send(x.at[d, 0, part(r)], x.at[d, 1, part(r)], fw_send.at[r, d], fw_recv.at[r, d], partner)

    def take_direct(r):
        for d in direct:
            arrived(x.at[d, 0, part(r)], ag_recv.at[r, d])
            if relayed:
                send(
                    x.at[d, 0, half(r, d)], x.at[3, 0, half(r, d)],
                    rl_send.at[r, d], rl_recv.at[r, d], across(3 - d),
                )
            to_partner(r, d)

    for r in range(ROW_CHUNKS):
        for d in direct:
            send(tok.at[part(r)], x.at[d, 0, part(r)], ag_send.at[r, d], ag_recv.at[r, d], across(d))
        send(tok.at[part(r)], x.at[0, 1, part(r)], fw_send.at[r, 0], fw_recv.at[r, 0], partner)
    send(w_out, w2.at[pl.ds(hd, hd)], w2_sem.at[0], w2_sem.at[1], partner)

    copies[0].wait()
    copies[1].wait()
    num_codes = book_v.shape[0]
    hot = lax.broadcasted_iota(jnp.int32, (num_codes, blk), 0) == codes_v[...]
    kq[0] = lax.dot_general(
        hot.astype(F32).astype(BF16), book_v[...], (((0,), (0,)), ((), ())), preferred_element_type=F32
    ).astype(BF16)

    def later(e, src, dst, send_sem, recv_sem):
        @pl.when(ctx + e < ctxs)
        def _():
            remote(src, dst, send_sem, recv_sem, (lax.rem(ctx + e, ctxs), head)).start()

    for e in range(1, ctxs):
        later(e, kq.at[0], kq.at[e], kq_send.at[e], kq_recv.at[e])

    for copy in copies[2:]:
        copy.wait()

    take_direct(0)
    for r in range(ROW_CHUNKS):
        def piece(d, other):
            source = chip_at(d, -1) * 2 + (1 - core if other else core)
            return jnp.dot(x[d, other, r * rows:(r + 1) * rows], w[source], preferred_element_type=F32)

        if r + 1 < ROW_CHUNKS:
            take_direct(r + 1)
        proj = piece(0, 0)
        arrived(x.at[0, 1, part(r)], fw_recv.at[r, 0])
        proj += piece(0, 1)
        for d in direct:
            proj += piece(d, 0)
        if relayed:
            for d in direct:
                arrived(x.at[3, 0, half(r, d)], rl_recv.at[r, d])
            to_partner(r, 3)
            proj += piece(3, 0)
        for d in range(1, chips):
            arrived(x.at[d, 1, part(r)], fw_recv.at[r, d])
            proj += piece(d, 1)
        q_s[r * rows:(r + 1) * rows] = proj[:, :hd].astype(BF16)
        kz[0, r * rows:(r + 1) * rows] = proj[:, hd:2 * hd].astype(BF16)
        vz[0, r * rows:(r + 1) * rows] = proj[:, 2 * hd:].astype(BF16)
        later(1, kz.at[0, part(r)], kz.at[1, part(r)], k_send.at[r], k_recv.at[r])
        for e in range(1, ctxs):
            later(e, vz.at[0, part(r)], vz.at[e, part(r)], v_send.at[r, e], v_recv.at[r, e])

    queries = q_s[...]
    own = nt(queries, kz[0])
    seen = lax.broadcasted_iota(jnp.int32, own.shape, 1) <= lax.broadcasted_iota(jnp.int32, own.shape, 0)
    own = jnp.where(seen, own, -jnp.inf)
    top_s[...] = jnp.broadcast_to(jnp.max(own, axis=1, keepdims=True), top_s.shape)
    for e in range(2, ctxs):
        @pl.when(ctx >= e)
        def _():
            arrived(kq.at[e], kq_recv.at[e])
            scores = nt(q_s[...], kq[e])
            score_s[e - 2] = scores
            top_s[...] = jnp.maximum(top_s[...], jnp.max(scores, axis=1, keepdims=True))

    probs = jnp.exp((own - top_s[...][:, :1]) * scale)
    den_s[...] = jnp.broadcast_to(jnp.sum(probs, axis=1, keepdims=True), den_s.shape)
    acc_s[...] = jnp.dot(probs.astype(BF16), vz[0], preferred_element_type=F32)
    for e in range(2, ctxs):
        @pl.when(ctx >= e)
        def _():
            probs = jnp.exp((score_s[e - 2] - top_s[...][:, :1]) * scale)
            prob_s[e - 2] = probs.astype(BF16)
            den_s[...] += jnp.sum(probs, axis=1, keepdims=True)

    @pl.when(ctx >= 1)
    def _():
        arrived(kq.at[1], kq_recv.at[1])
        for r in range(ROW_CHUNKS):
            arrived(kz.at[1, part(r)], k_recv.at[r])
        keys = kq[1]
        position = lax.broadcasted_iota(jnp.int32, keys.shape, 0)
        keys = jnp.where(position >= blk - reach_s[0], kz[1], keys)
        scores = nt(q_s[...], keys)
        old = top_s[...]
        top = jnp.maximum(old, jnp.max(scores, axis=1, keepdims=True))
        fade = jnp.exp((old - top) * scale)
        probs = jnp.exp((scores - top[:, :1]) * scale)
        fade_s[...] = fade
        den_s[...] = den_s[...] * fade + jnp.sum(probs, axis=1, keepdims=True)
        for r in range(ROW_CHUNKS):
            arrived(vz.at[1, part(r)], v_recv.at[r, 1])
        acc_s[...] = acc_s[...] * fade + jnp.dot(
            probs.astype(BF16), vz[1], preferred_element_type=F32
        )

    for e in range(2, ctxs):
        @pl.when(ctx >= e)
        def _():
            for r in range(ROW_CHUNKS):
                arrived(vz.at[e, part(r)], v_recv.at[r, e])
            acc_s[...] += fade_s[...] * jnp.dot(prob_s[e - 2], vz[e], preferred_element_type=F32)

    attended = acc_s[...] / den_s[...]
    for h in range(heads):
        att[h % 2, h // 2] = attended[h * rp:(h + 1) * rp].astype(BF16)
    send(att.at[1 - core], att_p, att_sem.at[0], att_sem.at[1], partner)
    mine = att[core].astype(F32).reshape(chips * rp, hd).astype(BF16)
    arrived(att_p, att_sem.at[1])
    other = att_p[...].astype(F32).reshape(chips * rp, hd).astype(BF16)
    arrived(w2.at[pl.ds(hd, hd)], w2_sem.at[1])
    both = jnp.concatenate([mine, other], axis=1)

    for j in range(COL_CHUNKS):
        block = jnp.dot(both, w2[:, j * cols:(j + 1) * cols], preferred_element_type=F32)
        for c in range(chips):
            term[j, c] = block[c * rp:(c + 1) * rp].astype(BF16)
        if relayed:
            first = 1 + j % 2
            send(term.at[j, chip_at(3, 1)], got.at[j, 3], rs_send.at[j, 3], rs_recv.at[j, 3], across(first))
        else:
            for d in direct:
                send(term.at[j, chip_at(d, 1)], got.at[j, d], rs_send.at[j, d], rs_recv.at[j, d], across(d))

    if relayed:
        for j in range(COL_CHUNKS):
            first = 1 + j % 2
            send(
                term.at[j, chip_at(first, 1)], got.at[j, first],
                rs_send.at[j, first], rs_recv.at[j, first], across(first),
            )
        for j in range(COL_CHUNKS):
            second = 2 - j % 2
            arrived(got.at[j, 3], rs_recv.at[j, 3])
            pair = got[j, 3].astype(F32) + term[j, chip_at(second, 1)].astype(F32)
            pre[j] = pair.astype(BF16)
            send(
                pre.at[j], got.at[j, second], rs_send.at[j, second], rs_recv.at[j, second], across(second)
            )

    results = []
    for j in range(COL_CHUNKS):
        total = term[j, chip].astype(F32)
        for d in direct:
            arrived(got.at[j, d], rs_recv.at[j, d])
            total += got[j, d].astype(F32)
        out_v[:, j * cols:(j + 1) * cols] = total.astype(BF16)
        results.append(
            pltpu.make_async_copy(
                out_v.at[:, pl.ds(j * cols, cols)], out.at[:, pl.ds(j * cols, cols)], out_sem.at[j]
            )
        )
        results[-1].start()

    for copy in results:
        copy.wait()
    for copy in sends:
        copy.wait_send()
    for e in range(1, ctxs):
        @pl.when(ctx + e < ctxs)
        def _():
            remote(kq.at[0], kq.at[e], kq_send.at[e], kq_recv.at[e], partner).wait_send()
            for r in range(ROW_CHUNKS):
                if e == 1:
                    remote(kz.at[0, part(r)], kz.at[1, part(r)], k_send.at[r], k_recv.at[r], partner).wait_send()
                remote(
                    vz.at[0, part(r)], vz.at[e, part(r)], v_send.at[r, e], v_recv.at[r, e], partner
                ).wait_send()


def solution(mesh):
    ctxs, heads = mesh.shape["ctx"], mesh.shape["head"]
    chips = heads // 2

    def on_device(tokens_in, w_qkv, w_out, codebook, codes, reach):
        blk, depth = tokens_in.shape
        num_codes, hd = codebook.shape[1:]
        wide = w_out.shape[2]
        rp = blk // heads
        cols = wide // COL_CHUNKS
        dma = pltpu.SemaphoreType.DMA
        return pl.pallas_call(
            functools.partial(kernel, (ctxs, heads, blk, hd)),
            out_shape=jax.ShapeDtypeStruct((rp, wide), BF16),
            in_specs=[pl.BlockSpec(memory_space=pltpu.HBM)] * 6,
            out_specs=pl.BlockSpec(memory_space=pltpu.HBM),
            scratch_shapes=[
                pltpu.VMEM((chips, 2, blk, depth), BF16),
                pltpu.VMEM((heads, depth, 3 * hd), BF16),
                pltpu.VMEM((2 * hd, wide), BF16),
                pltpu.VMEM((num_codes, hd), BF16),
                pltpu.VMEM((1, blk), jnp.int32),
                pltpu.SMEM((1,), jnp.int32),
                pltpu.VMEM((ctxs, blk, hd), BF16),
                pltpu.VMEM((2, blk, hd), BF16),
                pltpu.VMEM((ctxs, blk, hd), BF16),
                pltpu.VMEM((blk, hd), BF16),
                pltpu.VMEM((blk, hd), F32),
                pltpu.VMEM((blk, hd), F32),
                pltpu.VMEM((blk, hd), F32),
                pltpu.VMEM((blk, hd), F32),
                pltpu.VMEM((max(ctxs - 2, 1), blk, blk), F32),
                pltpu.VMEM((max(ctxs - 2, 1), blk, blk), BF16),
                pltpu.VMEM((rp, wide), BF16),
                pltpu.VMEM((2, chips, rp, hd), BF16),
                pltpu.VMEM((chips, rp, hd), BF16),
                pltpu.VMEM((COL_CHUNKS, chips, rp, cols), BF16),
                pltpu.VMEM((COL_CHUNKS, chips, rp, cols), BF16),
                pltpu.VMEM((COL_CHUNKS, rp, cols), BF16),
                dma((6,)),
                dma((ROW_CHUNKS, chips)),
                dma((ROW_CHUNKS, chips)),
                dma((ROW_CHUNKS, chips)),
                dma((ROW_CHUNKS, chips)),
                dma((ROW_CHUNKS, chips)),
                dma((ROW_CHUNKS, chips)),
                dma((2,)),
                dma((ctxs,)),
                dma((ctxs,)),
                dma((ROW_CHUNKS,)),
                dma((ROW_CHUNKS,)),
                dma((ROW_CHUNKS, ctxs)),
                dma((ROW_CHUNKS, ctxs)),
                dma((2,)),
                dma((COL_CHUNKS, chips)),
                dma((COL_CHUNKS, chips)),
                dma((COL_CHUNKS,)),
            ],
            compiler_params=pltpu.CompilerParams(
                collective_id=0, has_side_effects=True, vmem_limit_bytes=60 * 1024 * 1024
            ),
            cost_estimate=pl.CostEstimate(
                flops=2 * blk * heads * depth * 3 * hd, bytes_accessed=6 * 1024 * 1024, transcendentals=blk * blk
            ),
        )(
            tokens_in, w_qkv[:, 0, :].reshape(heads, depth, 3 * hd), w_out[0], codebook[0], codes, reach
        )

    in_specs = (
        P("ctx", "head"),
        P(None, "head", None),
        P("head", None, None),
        P("head", None, None),
        P("head", "ctx"),
        P("ctx"),
    )
    return jax.shard_map(
        on_device, mesh=mesh, in_specs=in_specs, out_specs=P(("ctx", "head"), None), check_vma=False
    )
```

```python
import functools
import math

import jax
import jax.numpy as jnp
from jax import lax
from jax.experimental import pallas as pl
from jax.experimental.pallas import tpu as pltpu
from jax.sharding import PartitionSpec as P

MESH = pl.DeviceIdType.MESH
F32 = jnp.float32
BF16 = jnp.bfloat16
ROW_CHUNKS = 4
COL_CHUNKS = 8


def grid_of(chips):
    wide = 1 << ((chips.bit_length() - 1) // 2)
    return chips // wide, wide


def nt(a, b):
    return lax.dot_general(a, b, (((1,), (1,)), ((), ())), preferred_element_type=F32)


def kernel(
    sizes,
    tok, w_in, w_out, book, codes, reach, out,
    x, w, w2, book_v, codes_v, reach_s, kq, kz, vz, q_s, top_s, den_s, acc_s, fade_s, score_s, prob_s, out_v, att, att_p, term, got, pre,
    local_sem, ag_send, ag_recv, fw_send, fw_recv, rl_send, rl_recv, w2_sem, kq_send, kq_recv, k_send, k_recv,
    v_send, v_recv, att_sem, rs_send, rs_recv, out_sem,
):
    ctxs, heads, blk, hd = sizes
    chips = heads // 2
    tall, wide = grid_of(chips)
    scale = 1.0 / math.sqrt(hd)
    rows = blk // ROW_CHUNKS
    cols = out.shape[1] // COL_CHUNKS
    rp = out.shape[0]
    ctx, head = lax.axis_index("ctx"), lax.axis_index("head")
    chip, core = head // 2, head % 2
    partner = (ctx, chip * 2 + 1 - core)

    def chip_at(d, sign):
        up, across = d // wide, d % wide
        row = lax.rem(chip // wide + (up if sign > 0 else tall - up), tall)
        col = lax.rem(chip % wide + (across if sign > 0 else wide - across), wide)
        return row * wide + col

    def remote(src, dst, send, recv, to):
        return pltpu.make_async_remote_copy(
            src_ref=src, dst_ref=dst, send_sem=send, recv_sem=recv, device_id=to, device_id_type=MESH
        )

    def arrived(dst, sem):
        remote(dst, dst, sem, sem, partner).wait_recv()

    copies = [
        pltpu.make_async_copy(codes, codes_v, local_sem.at[0]),
        pltpu.make_async_copy(book, book_v, local_sem.at[1]),
        pltpu.make_async_copy(reach, reach_s, local_sem.at[2]),
        pltpu.make_async_copy(tok, x.at[0, 0], local_sem.at[3]),
        pltpu.make_async_copy(w_in, w, local_sem.at[4]),
        pltpu.make_async_copy(w_out, w2.at[pl.ds(0, hd)], local_sem.at[5]),
    ]
    for copy in copies:
        copy.start()

    barrier = pltpu.get_barrier_semaphore()
    greet = [partner]
    greet += [(ctx, chip_at(d, 1) * 2 + core) for d in range(1, chips)]
    greet += [(lax.rem(ctx + e, ctxs), head) for e in range(1, ctxs)]
    for peer in greet:
        pl.semaphore_signal(barrier, inc=1, device_id=peer, device_id_type=MESH)
    pl.semaphore_wait(barrier, len(greet))

    relayed = (tall, wide) == (2, 2)
    direct = (1, 2) if relayed else range(1, chips)
    sends = []

    def send(*args):
        copy = remote(*args)
        copy.start()
        sends.append(copy)

    def part(r):
        return pl.ds(r * rows, rows)

    def across(d):
        return (ctx, chip_at(d, 1) * 2 + core)

    def half(r, d):
        return pl.ds(r * rows + (d - 1) * (rows // 2), rows // 2)

    def to_partner(r, d):
        send(x.at[d, 0, part(r)], x.at[d, 1, part(r)], fw_send.at[r, d], fw_recv.at[r, d], partner)

    def take_direct(r):
        for d in direct:
            arrived(x.at[d, 0, part(r)], ag_recv.at[r, d])
            if relayed:
                send(
                    x.at[d, 0, half(r, d)], x.at[3, 0, half(r, d)],
                    rl_send.at[r, d], rl_recv.at[r, d], across(3 - d),
                )
            to_partner(r, d)

    for r in range(ROW_CHUNKS):
        for d in direct:
            send(tok.at[part(r)], x.at[d, 0, part(r)], ag_send.at[r, d], ag_recv.at[r, d], across(d))
        send(tok.at[part(r)], x.at[0, 1, part(r)], fw_send.at[r, 0], fw_recv.at[r, 0], partner)
    send(w_out, w2.at[pl.ds(hd, hd)], w2_sem.at[0], w2_sem.at[1], partner)

    copies[0].wait()
    copies[1].wait()
    num_codes = book_v.shape[0]
    hot = lax.broadcasted_iota(jnp.int32, (num_codes, blk), 0) == codes_v[...]
    kq[0] = lax.dot_general(
        hot.astype(F32).astype(BF16), book_v[...], (((0,), (0,)), ((), ())), preferred_element_type=F32
    ).astype(BF16)

    def later(e, src, dst, send_sem, recv_sem):
        @pl.when(ctx + e < ctxs)
        def _():
            remote(src, dst, send_sem, recv_sem, (lax.rem(ctx + e, ctxs), head)).start()

    for e in range(1, ctxs):
        later(e, kq.at[0], kq.at[e], kq_send.at[e], kq_recv.at[e])

    for copy in copies[2:]:
        copy.wait()

    take_direct(0)
    for r in range(ROW_CHUNKS):
        def piece(d, other):
            source = chip_at(d, -1) * 2 + (1 - core if other else core)
            return jnp.dot(x[d, other, r * rows:(r + 1) * rows], w[source], preferred_element_type=F32)

        if r + 1 < ROW_CHUNKS:
            take_direct(r + 1)
        proj = piece(0, 0)
        arrived(x.at[0, 1, part(r)], fw_recv.at[r, 0])
        proj += piece(0, 1)
        for d in direct:
            proj += piece(d, 0)
        if relayed:
            for d in direct:
                arrived(x.at[3, 0, half(r, d)], rl_recv.at[r, d])
            to_partner(r, 3)
            proj += piece(3, 0)
        for d in range(1, chips):
            arrived(x.at[d, 1, part(r)], fw_recv.at[r, d])
            proj += piece(d, 1)
        q_s[r * rows:(r + 1) * rows] = proj[:, :hd].astype(BF16)
        kz[0, r * rows:(r + 1) * rows] = proj[:, hd:2 * hd].astype(BF16)
        vz[0, r * rows:(r + 1) * rows] = proj[:, 2 * hd:].astype(BF16)
        later(1, kz.at[0, part(r)], kz.at[1, part(r)], k_send.at[r], k_recv.at[r])
        for e in range(1, ctxs):
            later(e, vz.at[0, part(r)], vz.at[e, part(r)], v_send.at[r, e], v_recv.at[r, e])

    queries = q_s[...]
    own = nt(queries, kz[0])
    seen = lax.broadcasted_iota(jnp.int32, own.shape, 1) <= lax.broadcasted_iota(jnp.int32, own.shape, 0)
    own = jnp.where(seen, own, -jnp.inf)
    top_s[...] = jnp.broadcast_to(jnp.max(own, axis=1, keepdims=True), top_s.shape)
    for e in range(2, ctxs):
        @pl.when(ctx >= e)
        def _():
            arrived(kq.at[e], kq_recv.at[e])
            scores = nt(q_s[...], kq[e])
            score_s[e - 2] = scores
            top_s[...] = jnp.maximum(top_s[...], jnp.max(scores, axis=1, keepdims=True))

    probs = jnp.exp((own - top_s[...][:, :1]) * scale)
    den_s[...] = jnp.broadcast_to(jnp.sum(probs, axis=1, keepdims=True), den_s.shape)
    acc_s[...] = jnp.dot(probs.astype(BF16), vz[0], preferred_element_type=F32)
    for e in range(2, ctxs):
        @pl.when(ctx >= e)
        def _():
            probs = jnp.exp((score_s[e - 2] - top_s[...][:, :1]) * scale)
            prob_s[e - 2] = probs.astype(BF16)
            den_s[...] += jnp.sum(probs, axis=1, keepdims=True)

    @pl.when(ctx >= 1)
    def _():
        arrived(kq.at[1], kq_recv.at[1])
        for r in range(ROW_CHUNKS):
            arrived(kz.at[1, part(r)], k_recv.at[r])
        keys = kq[1]
        position = lax.broadcasted_iota(jnp.int32, keys.shape, 0)
        keys = jnp.where(position >= blk - reach_s[0], kz[1], keys)
        scores = nt(q_s[...], keys)
        old = top_s[...]
        top = jnp.maximum(old, jnp.max(scores, axis=1, keepdims=True))
        fade = jnp.exp((old - top) * scale)
        probs = jnp.exp((scores - top[:, :1]) * scale)
        fade_s[...] = fade
        den_s[...] = den_s[...] * fade + jnp.sum(probs, axis=1, keepdims=True)
        for r in range(ROW_CHUNKS):
            arrived(vz.at[1, part(r)], v_recv.at[r, 1])
        acc_s[...] = acc_s[...] * fade + jnp.dot(
            probs.astype(BF16), vz[1], preferred_element_type=F32
        )

    for e in range(2, ctxs):
        @pl.when(ctx >= e)
        def _():
            for r in range(ROW_CHUNKS):
                arrived(vz.at[e, part(r)], v_recv.at[r, e])
            acc_s[...] += fade_s[...] * jnp.dot(prob_s[e - 2], vz[e], preferred_element_type=F32)

    attended = acc_s[...] / den_s[...]
    for h in range(heads):
        att[h % 2, h // 2] = attended[h * rp:(h + 1) * rp].astype(BF16)
    send(att.at[1 - core], att_p, att_sem.at[0], att_sem.at[1], partner)
    mine = att[core].astype(F32).reshape(chips * rp, hd).astype(BF16)
    arrived(att_p, att_sem.at[1])
    other = att_p[...].astype(F32).reshape(chips * rp, hd).astype(BF16)
    arrived(w2.at[pl.ds(hd, hd)], w2_sem.at[1])
    both = jnp.concatenate([mine, other], axis=1)

    for j in range(COL_CHUNKS):
        block = jnp.dot(both, w2[:, j * cols:(j + 1) * cols], preferred_element_type=F32)
        for c in range(chips):
            term[j, c] = block[c * rp:(c + 1) * rp].astype(BF16)
        if relayed:
            first = 1 + j % 2
            send(term.at[j, chip_at(3, 1)], got.at[j, 3], rs_send.at[j, 3], rs_recv.at[j, 3], across(first))
        else:
            for d in direct:
                send(term.at[j, chip_at(d, 1)], got.at[j, d], rs_send.at[j, d], rs_recv.at[j, d], across(d))

    if relayed:
        for j in range(COL_CHUNKS):
            first = 1 + j % 2
            send(
                term.at[j, chip_at(first, 1)], got.at[j, first],
                rs_send.at[j, first], rs_recv.at[j, first], across(first),
            )
        for j in range(COL_CHUNKS):
            second = 2 - j % 2
            arrived(got.at[j, 3], rs_recv.at[j, 3])
            pair = got[j, 3].astype(F32) + term[j, chip_at(second, 1)].astype(F32)
            pre[j] = pair.astype(BF16)
            send(
                pre.at[j], got.at[j, second], rs_send.at[j, second], rs_recv.at[j, second], across(second)
            )

    results = []
    for j in range(COL_CHUNKS):
        total = term[j, chip].astype(F32)
        for d in direct:
            arrived(got.at[j, d], rs_recv.at[j, d])
            total += got[j, d].astype(F32)
        out_v[:, j * cols:(j + 1) * cols] = total.astype(BF16)
        results.append(
            pltpu.make_async_copy(
                out_v.at[:, pl.ds(j * cols, cols)], out.at[:, pl.ds(j * cols, cols)], out_sem.at[j]
            )
        )
        results[-1].start()

    for copy in results:
        copy.wait()
    for copy in sends:
        copy.wait_send()
    for e in range(1, ctxs):
        @pl.when(ctx + e < ctxs)
        def _():
            remote(kq.at[0], kq.at[e], kq_send.at[e], kq_recv.at[e], partner).wait_send()
            for r in range(ROW_CHUNKS):
                if e == 1:
                    remote(kz.at[0, part(r)], kz.at[1, part(r)], k_send.at[r], k_recv.at[r], partner).wait_send()
                remote(
                    vz.at[0, part(r)], vz.at[e, part(r)], v_send.at[r, e], v_recv.at[r, e], partner
                ).wait_send()


def solution(mesh):
    ctxs, heads = mesh.shape["ctx"], mesh.shape["head"]
    chips = heads // 2

    def on_device(tokens_in, w_qkv, w_out, codebook, codes, reach):
        blk, depth = tokens_in.shape
        num_codes, hd = codebook.shape[1:]
        wide = w_out.shape[2]
        rp = blk // heads
        cols = wide // COL_CHUNKS
        dma = pltpu.SemaphoreType.DMA
        return pl.pallas_call(
            functools.partial(kernel, (ctxs, heads, blk, hd)),
            out_shape=jax.ShapeDtypeStruct((rp, wide), BF16),
            in_specs=[pl.BlockSpec(memory_space=pltpu.HBM)] * 6,
            out_specs=pl.BlockSpec(memory_space=pltpu.HBM),
            scratch_shapes=[
                pltpu.VMEM((chips, 2, blk, depth), BF16),
                pltpu.VMEM((heads, depth, 3 * hd), BF16),
                pltpu.VMEM((2 * hd, wide), BF16),
                pltpu.VMEM((num_codes, hd), BF16),
                pltpu.VMEM((1, blk), jnp.int32),
                pltpu.SMEM((1,), jnp.int32),
                pltpu.VMEM((ctxs, blk, hd), BF16),
                pltpu.VMEM((2, blk, hd), BF16),
                pltpu.VMEM((ctxs, blk, hd), BF16),
                pltpu.VMEM((blk, hd), BF16),
                pltpu.VMEM((blk, hd), F32),
                pltpu.VMEM((blk, hd), F32),
                pltpu.VMEM((blk, hd), F32),
                pltpu.VMEM((blk, hd), F32),
                pltpu.VMEM((max(ctxs - 2, 1), blk, blk), F32),
                pltpu.VMEM((max(ctxs - 2, 1), blk, blk), BF16),
                pltpu.VMEM((rp, wide), BF16),
                pltpu.VMEM((2, chips, rp, hd), BF16),
                pltpu.VMEM((chips, rp, hd), BF16),
                pltpu.VMEM((COL_CHUNKS, chips, rp, cols), BF16),
                pltpu.VMEM((COL_CHUNKS, chips, rp, cols), BF16),
                pltpu.VMEM((COL_CHUNKS, rp, cols), BF16),
                dma((6,)),
                dma((ROW_CHUNKS, chips)),
                dma((ROW_CHUNKS, chips)),
                dma((ROW_CHUNKS, chips)),
                dma((ROW_CHUNKS, chips)),
                dma((ROW_CHUNKS, chips)),
                dma((ROW_CHUNKS, chips)),
                dma((2,)),
                dma((ctxs,)),
                dma((ctxs,)),
                dma((ROW_CHUNKS,)),
                dma((ROW_CHUNKS,)),
                dma((ROW_CHUNKS, ctxs)),
                dma((ROW_CHUNKS, ctxs)),
                dma((2,)),
                dma((COL_CHUNKS, chips)),
                dma((COL_CHUNKS, chips)),
                dma((COL_CHUNKS,)),
            ],
            compiler_params=pltpu.CompilerParams(
                collective_id=0, has_side_effects=True, vmem_limit_bytes=60 * 1024 * 1024
            ),
            cost_estimate=pl.CostEstimate(
                flops=2 * blk * heads * depth * 3 * hd, bytes_accessed=6 * 1024 * 1024, transcendentals=blk * blk
            ),
        )(
            tokens_in, w_qkv[:, 0, :].reshape(heads, depth, 3 * hd), w_out[0], codebook[0], codes, reach
        )

    in_specs = (
        P("ctx", "head"),
        P(None, "head", None),
        P("head", None, None),
        P("head", None, None),
        P("head", "ctx"),
        P("ctx"),
    )
    return jax.shard_map(
        on_device, mesh=mesh, in_specs=in_specs, out_specs=P(("ctx", "head"), None), check_vma=False
    )
```

```python
import functools
import math

import jax
import jax.numpy as jnp
from jax import lax
from jax.experimental import pallas as pl
from jax.experimental.pallas import tpu as pltpu
from jax.sharding import PartitionSpec as P

MESH = pl.DeviceIdType.MESH
F32 = jnp.float32
BF16 = jnp.bfloat16
ROW_CHUNKS = 4
COL_CHUNKS = 8


def grid_of(chips):
    wide = 1 << ((chips.bit_length() - 1) // 2)
    return chips // wide, wide


def nt(a, b):
    return lax.dot_general(a, b, (((1,), (1,)), ((), ())), preferred_element_type=F32)


def kernel(
    sizes,
    tok, w_in, w_out, book, codes, reach, out,
    x, proj_s, w, w2, book_v, codes_v, reach_s, kq, kz, vz, q_s, top_s, den_s, acc_s, fade_s, score_s, prob_s, out_v, att, att_p, term, got, pre,
    local_sem, ag_send, ag_recv, fw_send, fw_recv, rl_send, rl_recv, w2_sem, kq_send, kq_recv, k_send, k_recv,
    v_send, v_recv, att_sem, rs_send, rs_recv, out_sem,
):
    ctxs, heads, blk, hd = sizes
    chips = heads // 2
    tall, wide = grid_of(chips)
    scale = 1.0 / math.sqrt(hd)
    rows = blk // ROW_CHUNKS
    cols = out.shape[1] // COL_CHUNKS
    rp = out.shape[0]
    ctx, head = lax.axis_index("ctx"), lax.axis_index("head")
    chip, core = head // 2, head % 2
    partner = (ctx, chip * 2 + 1 - core)

    def chip_at(d, sign):
        up, across = d // wide, d % wide
        row = lax.rem(chip // wide + (up if sign > 0 else tall - up), tall)
        col = lax.rem(chip % wide + (across if sign > 0 else wide - across), wide)
        return row * wide + col

    def remote(src, dst, send, recv, to):
        return pltpu.make_async_remote_copy(
            src_ref=src, dst_ref=dst, send_sem=send, recv_sem=recv, device_id=to, device_id_type=MESH
        )

    def arrived(dst, sem):
        remote(dst, dst, sem, sem, partner).wait_recv()

    copies = [
        pltpu.make_async_copy(codes, codes_v, local_sem.at[0]),
        pltpu.make_async_copy(book, book_v, local_sem.at[1]),
        pltpu.make_async_copy(reach, reach_s, local_sem.at[2]),
        pltpu.make_async_copy(tok, x.at[0, 0], local_sem.at[3]),
        pltpu.make_async_copy(w_in, w, local_sem.at[4]),
        pltpu.make_async_copy(w_out, w2.at[pl.ds(0, hd)], local_sem.at[5]),
    ]
    for copy in copies:
        copy.start()

    barrier = pltpu.get_barrier_semaphore()
    greet = [partner]
    greet += [(ctx, chip_at(d, 1) * 2 + core) for d in range(1, chips)]
    greet += [(lax.rem(ctx + e, ctxs), head) for e in range(1, ctxs)]
    for peer in greet:
        pl.semaphore_signal(barrier, inc=1, device_id=peer, device_id_type=MESH)
    pl.semaphore_wait(barrier, len(greet))

    relayed = (tall, wide) == (2, 2)
    direct = (1, 2) if relayed else range(1, chips)
    sends = []

    def send(*args):
        copy = remote(*args)
        copy.start()
        sends.append(copy)

    def part(r):
        return pl.ds(r * rows, rows)

    def across(d):
        return (ctx, chip_at(d, 1) * 2 + core)

    def half(r, d):
        return pl.ds(r * rows + (d - 1) * (rows // 2), rows // 2)

    def to_partner(r, d):
        send(x.at[d, 0, part(r)], x.at[d, 1, part(r)], fw_send.at[r, d], fw_recv.at[r, d], partner)

    def take_direct(r):
        for d in direct:
            arrived(x.at[d, 0, part(r)], ag_recv.at[r, d])
            if relayed:
                send(
                    x.at[d, 0, half(r, d)], x.at[3, 0, half(r, d)],
                    rl_send.at[r, d], rl_recv.at[r, d], across(3 - d),
                )
            to_partner(r, d)

    for r in range(ROW_CHUNKS):
        for d in direct:
            send(tok.at[part(r)], x.at[d, 0, part(r)], ag_send.at[r, d], ag_recv.at[r, d], across(d))
        send(tok.at[part(r)], x.at[0, 1, part(r)], fw_send.at[r, 0], fw_recv.at[r, 0], partner)
    send(w_out, w2.at[pl.ds(hd, hd)], w2_sem.at[0], w2_sem.at[1], partner)

    copies[0].wait()
    copies[1].wait()
    num_codes = book_v.shape[0]
    hot = lax.broadcasted_iota(jnp.int32, (num_codes, blk), 0) == codes_v[...]
    kq[0] = lax.dot_general(
        hot.astype(F32).astype(BF16), book_v[...], (((0,), (0,)), ((), ())), preferred_element_type=F32
    ).astype(BF16)

    def later(e, src, dst, send_sem, recv_sem):
        @pl.when(ctx + e < ctxs)
        def _():
            remote(src, dst, send_sem, recv_sem, (lax.rem(ctx + e, ctxs), head)).start()

    for e in range(1, ctxs):
        later(e, kq.at[0], kq.at[e], kq_send.at[e], kq_recv.at[e])

    for copy in copies[2:]:
        copy.wait()

    def piece(d, other, block):
        source = chip_at(d, -1) * 2 + (1 - core if other else core)
        return jnp.dot(x[d, other, block], w[source], preferred_element_type=F32)

    every = slice(0, blk)
    proj_s[...] = piece(0, 0, every)
    for r in range(ROW_CHUNKS):
        arrived(x.at[0, 1, part(r)], fw_recv.at[r, 0])
    proj_s[...] += piece(0, 1, every)
    for r in range(ROW_CHUNKS):
        take_direct(r)
    early = direct if relayed else range(1, chips - 1)
    last = chips - 1

    def take_last(r):
        if relayed:
            for d in direct:
                arrived(x.at[3, 0, half(r, d)], rl_recv.at[r, d])
            to_partner(r, 3)

    for d in early:
        proj_s[...] += piece(d, 0, every)
    take_last(0)
    for d in early:
        for r in range(ROW_CHUNKS):
            arrived(x.at[d, 1, part(r)], fw_recv.at[r, d])
        proj_s[...] += piece(d, 1, every)

    for r in range(ROW_CHUNKS):
        block = slice(r * rows, (r + 1) * rows)
        if r + 1 < ROW_CHUNKS:
            take_last(r + 1)
        proj = proj_s[block] + piece(last, 0, block)
        arrived(x.at[last, 1, part(r)], fw_recv.at[r, last])
        proj += piece(last, 1, block)
        q_s[block] = proj[:, :hd].astype(BF16)
        kz[0, block] = proj[:, hd:2 * hd].astype(BF16)
        vz[0, block] = proj[:, 2 * hd:].astype(BF16)
        later(1, kz.at[0, part(r)], kz.at[1, part(r)], k_send.at[r], k_recv.at[r])
        for e in range(1, ctxs):
            later(e, vz.at[0, part(r)], vz.at[e, part(r)], v_send.at[r, e], v_recv.at[r, e])

    queries = q_s[...]
    own = nt(queries, kz[0])
    seen = lax.broadcasted_iota(jnp.int32, own.shape, 1) <= lax.broadcasted_iota(jnp.int32, own.shape, 0)
    own = jnp.where(seen, own, -jnp.inf)
    top_s[...] = jnp.broadcast_to(jnp.max(own, axis=1, keepdims=True), top_s.shape)
    for e in range(2, ctxs):
        @pl.when(ctx >= e)
        def _():
            arrived(kq.at[e], kq_recv.at[e])
            scores = nt(q_s[...], kq[e])
            score_s[e - 2] = scores
            top_s[...] = jnp.maximum(top_s[...], jnp.max(scores, axis=1, keepdims=True))

    probs = jnp.exp((own - top_s[...][:, :1]) * scale)
    den_s[...] = jnp.broadcast_to(jnp.sum(probs, axis=1, keepdims=True), den_s.shape)
    acc_s[...] = jnp.dot(probs.astype(BF16), vz[0], preferred_element_type=F32)
    for e in range(2, ctxs):
        @pl.when(ctx >= e)
        def _():
            probs = jnp.exp((score_s[e - 2] - top_s[...][:, :1]) * scale)
            prob_s[e - 2] = probs.astype(BF16)
            den_s[...] += jnp.sum(probs, axis=1, keepdims=True)

    @pl.when(ctx >= 1)
    def _():
        arrived(kq.at[1], kq_recv.at[1])
        for r in range(ROW_CHUNKS):
            arrived(kz.at[1, part(r)], k_recv.at[r])
        keys = kq[1]
        position = lax.broadcasted_iota(jnp.int32, keys.shape, 0)
        keys = jnp.where(position >= blk - reach_s[0], kz[1], keys)
        scores = nt(q_s[...], keys)
        old = top_s[...]
        top = jnp.maximum(old, jnp.max(scores, axis=1, keepdims=True))
        fade = jnp.exp((old - top) * scale)
        probs = jnp.exp((scores - top[:, :1]) * scale)
        fade_s[...] = fade
        den_s[...] = den_s[...] * fade + jnp.sum(probs, axis=1, keepdims=True)
        for r in range(ROW_CHUNKS):
            arrived(vz.at[1, part(r)], v_recv.at[r, 1])
        acc_s[...] = acc_s[...] * fade + jnp.dot(
            probs.astype(BF16), vz[1], preferred_element_type=F32
        )

    for e in range(2, ctxs):
        @pl.when(ctx >= e)
        def _():
            for r in range(ROW_CHUNKS):
                arrived(vz.at[e, part(r)], v_recv.at[r, e])
            acc_s[...] += fade_s[...] * jnp.dot(prob_s[e - 2], vz[e], preferred_element_type=F32)

    attended = acc_s[...] / den_s[...]
    for h in range(heads):
        att[h % 2, h // 2] = attended[h * rp:(h + 1) * rp].astype(BF16)
    send(att.at[1 - core], att_p, att_sem.at[0], att_sem.at[1], partner)
    mine = att[core].astype(F32).reshape(chips * rp, hd).astype(BF16)
    arrived(att_p, att_sem.at[1])
    other = att_p[...].astype(F32).reshape(chips * rp, hd).astype(BF16)
    arrived(w2.at[pl.ds(hd, hd)], w2_sem.at[1])
    both = jnp.concatenate([mine, other], axis=1)

    for j in range(COL_CHUNKS):
        block = jnp.dot(both, w2[:, j * cols:(j + 1) * cols], preferred_element_type=F32)
        for c in range(chips):
            term[j, c] = block[c * rp:(c + 1) * rp].astype(BF16)
        if relayed:
            first = 1 + j % 2
            send(term.at[j, chip_at(3, 1)], got.at[j, 3], rs_send.at[j, 3], rs_recv.at[j, 3], across(first))
        else:
            for d in direct:
                send(term.at[j, chip_at(d, 1)], got.at[j, d], rs_send.at[j, d], rs_recv.at[j, d], across(d))

    if relayed:
        for j in range(COL_CHUNKS):
            first = 1 + j % 2
            send(
                term.at[j, chip_at(first, 1)], got.at[j, first],
                rs_send.at[j, first], rs_recv.at[j, first], across(first),
            )
        for j in range(COL_CHUNKS):
            second = 2 - j % 2
            arrived(got.at[j, 3], rs_recv.at[j, 3])
            pair = got[j, 3].astype(F32) + term[j, chip_at(second, 1)].astype(F32)
            pre[j] = pair.astype(BF16)
            send(
                pre.at[j], got.at[j, second], rs_send.at[j, second], rs_recv.at[j, second], across(second)
            )

    results = []
    for j in range(COL_CHUNKS):
        total = term[j, chip].astype(F32)
        for d in direct:
            arrived(got.at[j, d], rs_recv.at[j, d])
            total += got[j, d].astype(F32)
        out_v[:, j * cols:(j + 1) * cols] = total.astype(BF16)
        results.append(
            pltpu.make_async_copy(
                out_v.at[:, pl.ds(j * cols, cols)], out.at[:, pl.ds(j * cols, cols)], out_sem.at[j]
            )
        )
        results[-1].start()

    for copy in results:
        copy.wait()
    for copy in sends:
        copy.wait_send()
    for e in range(1, ctxs):
        @pl.when(ctx + e < ctxs)
        def _():
            remote(kq.at[0], kq.at[e], kq_send.at[e], kq_recv.at[e], partner).wait_send()
            for r in range(ROW_CHUNKS):
                if e == 1:
                    remote(kz.at[0, part(r)], kz.at[1, part(r)], k_send.at[r], k_recv.at[r], partner).wait_send()
                remote(
                    vz.at[0, part(r)], vz.at[e, part(r)], v_send.at[r, e], v_recv.at[r, e], partner
                ).wait_send()


def solution(mesh):
    ctxs, heads = mesh.shape["ctx"], mesh.shape["head"]
    chips = heads // 2

    def on_device(tokens_in, w_qkv, w_out, codebook, codes, reach):
        blk, depth = tokens_in.shape
        num_codes, hd = codebook.shape[1:]
        wide = w_out.shape[2]
        rp = blk // heads
        cols = wide // COL_CHUNKS
        dma = pltpu.SemaphoreType.DMA
        return pl.pallas_call(
            functools.partial(kernel, (ctxs, heads, blk, hd)),
            out_shape=jax.ShapeDtypeStruct((rp, wide), BF16),
            in_specs=[pl.BlockSpec(memory_space=pltpu.HBM)] * 6,
            out_specs=pl.BlockSpec(memory_space=pltpu.HBM),
            scratch_shapes=[
                pltpu.VMEM((chips, 2, blk, depth), BF16),
                pltpu.VMEM((blk, 3 * hd), F32),
                pltpu.VMEM((heads, depth, 3 * hd), BF16),
                pltpu.VMEM((2 * hd, wide), BF16),
                pltpu.VMEM((num_codes, hd), BF16),
                pltpu.VMEM((1, blk), jnp.int32),
                pltpu.SMEM((1,), jnp.int32),
                pltpu.VMEM((ctxs, blk, hd), BF16),
                pltpu.VMEM((2, blk, hd), BF16),
                pltpu.VMEM((ctxs, blk, hd), BF16),
                pltpu.VMEM((blk, hd), BF16),
                pltpu.VMEM((blk, hd), F32),
                pltpu.VMEM((blk, hd), F32),
                pltpu.VMEM((blk, hd), F32),
                pltpu.VMEM((blk, hd), F32),
                pltpu.VMEM((max(ctxs - 2, 1), blk, blk), F32),
                pltpu.VMEM((max(ctxs - 2, 1), blk, blk), BF16),
                pltpu.VMEM((rp, wide), BF16),
                pltpu.VMEM((2, chips, rp, hd), BF16),
                pltpu.VMEM((chips, rp, hd), BF16),
                pltpu.VMEM((COL_CHUNKS, chips, rp, cols), BF16),
                pltpu.VMEM((COL_CHUNKS, chips, rp, cols), BF16),
                pltpu.VMEM((COL_CHUNKS, rp, cols), BF16),
                dma((6,)),
                dma((ROW_CHUNKS, chips)),
                dma((ROW_CHUNKS, chips)),
                dma((ROW_CHUNKS, chips)),
                dma((ROW_CHUNKS, chips)),
                dma((ROW_CHUNKS, chips)),
                dma((ROW_CHUNKS, chips)),
                dma((2,)),
                dma((ctxs,)),
                dma((ctxs,)),
                dma((ROW_CHUNKS,)),
                dma((ROW_CHUNKS,)),
                dma((ROW_CHUNKS, ctxs)),
                dma((ROW_CHUNKS, ctxs)),
                dma((2,)),
                dma((COL_CHUNKS, chips)),
                dma((COL_CHUNKS, chips)),
                dma((COL_CHUNKS,)),
            ],
            compiler_params=pltpu.CompilerParams(
                collective_id=0, has_side_effects=True, vmem_limit_bytes=60 * 1024 * 1024
            ),
            cost_estimate=pl.CostEstimate(
                flops=2 * blk * heads * depth * 3 * hd, bytes_accessed=6 * 1024 * 1024, transcendentals=blk * blk
            ),
        )(
            tokens_in, w_qkv[:, 0, :].reshape(heads, depth, 3 * hd), w_out[0], codebook[0], codes, reach
        )

    in_specs = (
        P("ctx", "head"),
        P(None, "head", None),
        P("head", None, None),
        P("head", None, None),
        P("head", "ctx"),
        P("ctx"),
    )
    return jax.shard_map(
        on_device, mesh=mesh, in_specs=in_specs, out_specs=P(("ctx", "head"), None), check_vma=False
    )
```

```python
import functools
import math

import jax
import jax.numpy as jnp
from jax import lax
from jax.experimental import pallas as pl
from jax.experimental.pallas import tpu as pltpu
from jax.sharding import PartitionSpec as P

MESH = pl.DeviceIdType.MESH
F32 = jnp.float32
BF16 = jnp.bfloat16
ROW_CHUNKS = 4
COL_CHUNKS = 8
AHEAD = 2
GROUPS = ((0,), (1,), (2, 3))


def grid_of(chips):
    wide = 1 << ((chips.bit_length() - 1) // 2)
    return chips // wide, wide


def nt(a, b):
    return lax.dot_general(a, b, (((1,), (1,)), ((), ())), preferred_element_type=F32)


def kernel(
    sizes,
    tok, w_in, w_out, book, codes, reach, out,
    x, proj_s, w, w2, book_v, codes_v, reach_s, kq, kz, vz, q_s, top_s, den_s, acc_s, fade_s, score_s, prob_s, out_v, att, att_p, term, got, pre,
    local_sem, ag_send, ag_recv, fw_send, fw_recv, rl_send, rl_recv, w2_sem, kq_send, kq_recv, k_send, k_recv,
    v_send, v_recv, att_sem, rs_send, rs_recv, out_sem,
):
    ctxs, heads, blk, hd = sizes
    chips = heads // 2
    tall, wide = grid_of(chips)
    scale = 1.0 / math.sqrt(hd)
    rows = blk // ROW_CHUNKS
    cols = out.shape[1] // COL_CHUNKS
    rp = out.shape[0]
    ctx, head = lax.axis_index("ctx"), lax.axis_index("head")
    chip, core = head // 2, head % 2
    partner = (ctx, chip * 2 + 1 - core)

    def chip_at(d, sign):
        up, across = d // wide, d % wide
        row = lax.rem(chip // wide + (up if sign > 0 else tall - up), tall)
        col = lax.rem(chip % wide + (across if sign > 0 else wide - across), wide)
        return row * wide + col

    def remote(src, dst, send, recv, to):
        return pltpu.make_async_remote_copy(
            src_ref=src, dst_ref=dst, send_sem=send, recv_sem=recv, device_id=to, device_id_type=MESH
        )

    def arrived(dst, sem):
        remote(dst, dst, sem, sem, partner).wait_recv()

    copies = [
        pltpu.make_async_copy(codes, codes_v, local_sem.at[0]),
        pltpu.make_async_copy(book, book_v, local_sem.at[1]),
        pltpu.make_async_copy(reach, reach_s, local_sem.at[2]),
        pltpu.make_async_copy(tok, x.at[0, 0], local_sem.at[3]),
        pltpu.make_async_copy(w_in, w, local_sem.at[4]),
        pltpu.make_async_copy(w_out, w2.at[pl.ds(0, hd)], local_sem.at[5]),
    ]
    for copy in copies:
        copy.start()

    barrier = pltpu.get_barrier_semaphore()
    greet = [partner]
    greet += [(ctx, chip_at(d, 1) * 2 + core) for d in range(1, chips)]
    greet += [(lax.rem(ctx + e, ctxs), head) for e in range(1, ctxs)]
    for peer in greet:
        pl.semaphore_signal(barrier, inc=1, device_id=peer, device_id_type=MESH)
    pl.semaphore_wait(barrier, len(greet))

    relayed = (tall, wide) == (2, 2)
    direct = (1, 2) if relayed else range(1, chips)
    sends = []

    def send(*args):
        copy = remote(*args)
        copy.start()
        sends.append(copy)

    def part(r):
        return pl.ds(r * rows, rows)

    def across(d):
        return (ctx, chip_at(d, 1) * 2 + core)

    def half(r, d):
        return pl.ds(r * rows + (d - 1) * (rows // 2), rows // 2)

    def to_partner(r, d):
        send(x.at[d, 0, part(r)], x.at[d, 1, part(r)], fw_send.at[r, d], fw_recv.at[r, d], partner)

    def take_direct(r):
        for d in direct:
            arrived(x.at[d, 0, part(r)], ag_recv.at[r, d])
            if relayed:
                send(
                    x.at[d, 0, half(r, d)], x.at[3, 0, half(r, d)],
                    rl_send.at[r, d], rl_recv.at[r, d], across(3 - d),
                )
            to_partner(r, d)
        if r + AHEAD < ROW_CHUNKS:
            send_direct(r + AHEAD)

    def send_direct(r):
        for d in direct:
            send(tok.at[part(r)], x.at[d, 0, part(r)], ag_send.at[r, d], ag_recv.at[r, d], across(d))

    for r in range(AHEAD):
        send_direct(r)
    for r in range(ROW_CHUNKS):
        send(tok.at[part(r)], x.at[0, 1, part(r)], fw_send.at[r, 0], fw_recv.at[r, 0], partner)
    send(w_out, w2.at[pl.ds(hd, hd)], w2_sem.at[0], w2_sem.at[1], partner)

    copies[0].wait()
    copies[1].wait()
    num_codes = book_v.shape[0]
    hot = lax.broadcasted_iota(jnp.int32, (num_codes, blk), 0) == codes_v[...]
    kq[0] = lax.dot_general(
        hot.astype(F32).astype(BF16), book_v[...], (((0,), (0,)), ((), ())), preferred_element_type=F32
    ).astype(BF16)

    def later(e, src, dst, send_sem, recv_sem):
        @pl.when(ctx + e < ctxs)
        def _():
            remote(src, dst, send_sem, recv_sem, (lax.rem(ctx + e, ctxs), head)).start()

    for e in range(1, ctxs):
        later(e, kq.at[0], kq.at[e], kq_send.at[e], kq_recv.at[e])

    for copy in copies[2:]:
        copy.wait()

    def piece(d, other, block):
        source = chip_at(d, -1) * 2 + (1 - core if other else core)
        return jnp.dot(x[d, other, block], w[source], preferred_element_type=F32)

    early = direct if relayed else range(1, chips - 1)
    last = chips - 1

    def take_last(r):
        if relayed:
            for d in direct:
                arrived(x.at[3, 0, half(r, d)], rl_recv.at[r, d])
            to_partner(r, 3)

    def project_early(chunks):
        block = slice(chunks[0] * rows, (chunks[-1] + 1) * rows)
        for d in early:
            proj_s[block] += piece(d, 0, block)
        take_last(chunks[0])
        for d in early:
            for r in chunks:
                arrived(x.at[d, 1, part(r)], fw_recv.at[r, d])
            proj_s[block] += piece(d, 1, block)

    def project_last(r):
        block = slice(r * rows, (r + 1) * rows)
        proj = proj_s[block] + piece(last, 0, block)
        arrived(x.at[last, 1, part(r)], fw_recv.at[r, last])
        proj += piece(last, 1, block)
        q_s[block] = proj[:, :hd].astype(BF16)
        kz[0, block] = proj[:, hd:2 * hd].astype(BF16)
        vz[0, block] = proj[:, 2 * hd:].astype(BF16)
        later(1, kz.at[0, part(r)], kz.at[1, part(r)], k_send.at[r], k_recv.at[r])
        for e in range(1, ctxs):
            later(e, vz.at[0, part(r)], vz.at[e, part(r)], v_send.at[r, e], v_recv.at[r, e])

    every = slice(0, blk)
    proj_s[...] = piece(0, 0, every)
    for r in range(ROW_CHUNKS):
        arrived(x.at[0, 1, part(r)], fw_recv.at[r, 0])
    proj_s[...] += piece(0, 1, every)
    for r in range(AHEAD):
        take_direct(r)
    taken = AHEAD
    for chunks in GROUPS:
        while taken <= chunks[-1]:
            take_direct(taken)
            taken += 1
        project_early(chunks)
        if taken < ROW_CHUNKS:
            take_direct(taken)
            taken += 1
        for r in chunks:
            if r > chunks[0]:
                take_last(r)
            project_last(r)

    queries = q_s[...]
    own = nt(queries, kz[0])
    seen = lax.broadcasted_iota(jnp.int32, own.shape, 1) <= lax.broadcasted_iota(jnp.int32, own.shape, 0)
    own = jnp.where(seen, own, -jnp.inf)
    top_s[...] = jnp.broadcast_to(jnp.max(own, axis=1, keepdims=True), top_s.shape)
    for e in range(2, ctxs):
        @pl.when(ctx >= e)
        def _():
            arrived(kq.at[e], kq_recv.at[e])
            scores = nt(q_s[...], kq[e])
            score_s[e - 2] = scores
            top_s[...] = jnp.maximum(top_s[...], jnp.max(scores, axis=1, keepdims=True))

    probs = jnp.exp((own - top_s[...][:, :1]) * scale)
    den_s[...] = jnp.broadcast_to(jnp.sum(probs, axis=1, keepdims=True), den_s.shape)
    acc_s[...] = jnp.dot(probs.astype(BF16), vz[0], preferred_element_type=F32)
    for e in range(2, ctxs):
        @pl.when(ctx >= e)
        def _():
            probs = jnp.exp((score_s[e - 2] - top_s[...][:, :1]) * scale)
            prob_s[e - 2] = probs.astype(BF16)
            den_s[...] += jnp.sum(probs, axis=1, keepdims=True)

    @pl.when(ctx >= 1)
    def _():
        arrived(kq.at[1], kq_recv.at[1])
        for r in range(ROW_CHUNKS):
            arrived(kz.at[1, part(r)], k_recv.at[r])
        keys = kq[1]
        position = lax.broadcasted_iota(jnp.int32, keys.shape, 0)
        keys = jnp.where(position >= blk - reach_s[0], kz[1], keys)
        scores = nt(q_s[...], keys)
        old = top_s[...]
        top = jnp.maximum(old, jnp.max(scores, axis=1, keepdims=True))
        fade = jnp.exp((old - top) * scale)
        probs = jnp.exp((scores - top[:, :1]) * scale)
        fade_s[...] = fade
        den_s[...] = den_s[...] * fade + jnp.sum(probs, axis=1, keepdims=True)
        for r in range(ROW_CHUNKS):
            arrived(vz.at[1, part(r)], v_recv.at[r, 1])
        acc_s[...] = acc_s[...] * fade + jnp.dot(
            probs.astype(BF16), vz[1], preferred_element_type=F32
        )

    for e in range(2, ctxs):
        @pl.when(ctx >= e)
        def _():
            for r in range(ROW_CHUNKS):
                arrived(vz.at[e, part(r)], v_recv.at[r, e])
            acc_s[...] += fade_s[...] * jnp.dot(prob_s[e - 2], vz[e], preferred_element_type=F32)

    attended = acc_s[...] / den_s[...]
    for h in range(heads):
        att[h % 2, h // 2] = attended[h * rp:(h + 1) * rp].astype(BF16)
    send(att.at[1 - core], att_p, att_sem.at[0], att_sem.at[1], partner)
    mine = att[core].astype(F32).reshape(chips * rp, hd).astype(BF16)
    arrived(att_p, att_sem.at[1])
    other = att_p[...].astype(F32).reshape(chips * rp, hd).astype(BF16)
    arrived(w2.at[pl.ds(hd, hd)], w2_sem.at[1])
    both = jnp.concatenate([mine, other], axis=1)

    for j in range(COL_CHUNKS):
        block = jnp.dot(both, w2[:, j * cols:(j + 1) * cols], preferred_element_type=F32)
        for c in range(chips):
            term[j, c] = block[c * rp:(c + 1) * rp].astype(BF16)
        if relayed:
            first = 1 + j % 2
            send(term.at[j, chip_at(3, 1)], got.at[j, 3], rs_send.at[j, 3], rs_recv.at[j, 3], across(first))
        else:
            for d in direct:
                send(term.at[j, chip_at(d, 1)], got.at[j, d], rs_send.at[j, d], rs_recv.at[j, d], across(d))

    if relayed:
        for j in range(COL_CHUNKS):
            first = 1 + j % 2
            send(
                term.at[j, chip_at(first, 1)], got.at[j, first],
                rs_send.at[j, first], rs_recv.at[j, first], across(first),
            )
        for j in range(COL_CHUNKS):
            second = 2 - j % 2
            arrived(got.at[j, 3], rs_recv.at[j, 3])
            pair = got[j, 3].astype(F32) + term[j, chip_at(second, 1)].astype(F32)
            pre[j] = pair.astype(BF16)
            send(
                pre.at[j], got.at[j, second], rs_send.at[j, second], rs_recv.at[j, second], across(second)
            )

    results = []
    for j in range(COL_CHUNKS):
        total = term[j, chip].astype(F32)
        for d in direct:
            arrived(got.at[j, d], rs_recv.at[j, d])
            total += got[j, d].astype(F32)
        out_v[:, j * cols:(j + 1) * cols] = total.astype(BF16)
        results.append(
            pltpu.make_async_copy(
                out_v.at[:, pl.ds(j * cols, cols)], out.at[:, pl.ds(j * cols, cols)], out_sem.at[j]
            )
        )
        results[-1].start()

    for copy in results:
        copy.wait()
    for copy in sends:
        copy.wait_send()
    for e in range(1, ctxs):
        @pl.when(ctx + e < ctxs)
        def _():
            remote(kq.at[0], kq.at[e], kq_send.at[e], kq_recv.at[e], partner).wait_send()
            for r in range(ROW_CHUNKS):
                if e == 1:
                    remote(kz.at[0, part(r)], kz.at[1, part(r)], k_send.at[r], k_recv.at[r], partner).wait_send()
                remote(
                    vz.at[0, part(r)], vz.at[e, part(r)], v_send.at[r, e], v_recv.at[r, e], partner
                ).wait_send()


def solution(mesh):
    ctxs, heads = mesh.shape["ctx"], mesh.shape["head"]
    chips = heads // 2

    def on_device(tokens_in, w_qkv, w_out, codebook, codes, reach):
        blk, depth = tokens_in.shape
        num_codes, hd = codebook.shape[1:]
        wide = w_out.shape[2]
        rp = blk // heads
        cols = wide // COL_CHUNKS
        dma = pltpu.SemaphoreType.DMA
        return pl.pallas_call(
            functools.partial(kernel, (ctxs, heads, blk, hd)),
            out_shape=jax.ShapeDtypeStruct((rp, wide), BF16),
            in_specs=[pl.BlockSpec(memory_space=pltpu.HBM)] * 6,
            out_specs=pl.BlockSpec(memory_space=pltpu.HBM),
            scratch_shapes=[
                pltpu.VMEM((chips, 2, blk, depth), BF16),
                pltpu.VMEM((blk, 3 * hd), F32),
                pltpu.VMEM((heads, depth, 3 * hd), BF16),
                pltpu.VMEM((2 * hd, wide), BF16),
                pltpu.VMEM((num_codes, hd), BF16),
                pltpu.VMEM((1, blk), jnp.int32),
                pltpu.SMEM((1,), jnp.int32),
                pltpu.VMEM((ctxs, blk, hd), BF16),
                pltpu.VMEM((2, blk, hd), BF16),
                pltpu.VMEM((ctxs, blk, hd), BF16),
                pltpu.VMEM((blk, hd), BF16),
                pltpu.VMEM((blk, hd), F32),
                pltpu.VMEM((blk, hd), F32),
                pltpu.VMEM((blk, hd), F32),
                pltpu.VMEM((blk, hd), F32),
                pltpu.VMEM((max(ctxs - 2, 1), blk, blk), F32),
                pltpu.VMEM((max(ctxs - 2, 1), blk, blk), BF16),
                pltpu.VMEM((rp, wide), BF16),
                pltpu.VMEM((2, chips, rp, hd), BF16),
                pltpu.VMEM((chips, rp, hd), BF16),
                pltpu.VMEM((COL_CHUNKS, chips, rp, cols), BF16),
                pltpu.VMEM((COL_CHUNKS, chips, rp, cols), BF16),
                pltpu.VMEM((COL_CHUNKS, rp, cols), BF16),
                dma((6,)),
                dma((ROW_CHUNKS, chips)),
                dma((ROW_CHUNKS, chips)),
                dma((ROW_CHUNKS, chips)),
                dma((ROW_CHUNKS, chips)),
                dma((ROW_CHUNKS, chips)),
                dma((ROW_CHUNKS, chips)),
                dma((2,)),
                dma((ctxs,)),
                dma((ctxs,)),
                dma((ROW_CHUNKS,)),
                dma((ROW_CHUNKS,)),
                dma((ROW_CHUNKS, ctxs)),
                dma((ROW_CHUNKS, ctxs)),
                dma((2,)),
                dma((COL_CHUNKS, chips)),
                dma((COL_CHUNKS, chips)),
                dma((COL_CHUNKS,)),
            ],
            compiler_params=pltpu.CompilerParams(
                collective_id=0, has_side_effects=True, vmem_limit_bytes=60 * 1024 * 1024
            ),
            cost_estimate=pl.CostEstimate(
                flops=2 * blk * heads * depth * 3 * hd, bytes_accessed=6 * 1024 * 1024, transcendentals=blk * blk
            ),
        )(
            tokens_in, w_qkv[:, 0, :].reshape(heads, depth, 3 * hd), w_out[0], codebook[0], codes, reach
        )

    in_specs = (
        P("ctx", "head"),
        P(None, "head", None),
        P("head", None, None),
        P("head", None, None),
        P("head", "ctx"),
        P("ctx"),
    )
    return jax.shard_map(
        on_device, mesh=mesh, in_specs=in_specs, out_specs=P(("ctx", "head"), None), check_vma=False
    )
```

```python
import functools
import math

import jax
import jax.numpy as jnp
from jax import lax
from jax.experimental import pallas as pl
from jax.experimental.pallas import tpu as pltpu
from jax.sharding import PartitionSpec as P

MESH = pl.DeviceIdType.MESH
F32 = jnp.float32
BF16 = jnp.bfloat16
ROW_CHUNKS = 4
COL_CHUNKS = 8
AHEAD = 2
GROUPS = ((0,), (1,), (2, 3))


def grid_of(chips):
    wide = 1 << ((chips.bit_length() - 1) // 2)
    return chips // wide, wide


def nt(a, b):
    return lax.dot_general(a, b, (((1,), (1,)), ((), ())), preferred_element_type=F32)


def kernel(
    sizes,
    tok, w_in, w_out, book, codes, reach, out,
    x, proj_s, w, w2, book_v, codes_v, reach_s, kq, kz, vz, q_s, top_s, den_s, acc_s, fade_s, score_s, prob_s, out_v, att, att_p, term, got, pre,
    local_sem, ag_send, ag_recv, fw_send, fw_recv, rl_send, rl_recv, w2_sem, kq_send, kq_recv, k_send, k_recv,
    v_send, v_recv, att_sem, rs_send, rs_recv, out_sem,
):
    ctxs, heads, blk, hd = sizes
    chips = heads // 2
    tall, wide = grid_of(chips)
    scale = 1.0 / math.sqrt(hd)
    rows = blk // ROW_CHUNKS
    cols = out.shape[1] // COL_CHUNKS
    rp = out.shape[0]
    ctx, head = lax.axis_index("ctx"), lax.axis_index("head")
    chip, core = head // 2, head % 2
    partner = (ctx, chip * 2 + 1 - core)

    def chip_at(d, sign):
        up, across = d // wide, d % wide
        row = lax.rem(chip // wide + (up if sign > 0 else tall - up), tall)
        col = lax.rem(chip % wide + (across if sign > 0 else wide - across), wide)
        return row * wide + col

    def remote(src, dst, send, recv, to):
        return pltpu.make_async_remote_copy(
            src_ref=src, dst_ref=dst, send_sem=send, recv_sem=recv, device_id=to, device_id_type=MESH
        )

    def arrived(dst, sem):
        remote(dst, dst, sem, sem, partner).wait_recv()

    copies = [
        pltpu.make_async_copy(codes, codes_v, local_sem.at[0]),
        pltpu.make_async_copy(book, book_v, local_sem.at[1]),
        pltpu.make_async_copy(reach, reach_s, local_sem.at[2]),
        pltpu.make_async_copy(tok, x.at[0, 0], local_sem.at[3]),
        pltpu.make_async_copy(w_in, w, local_sem.at[4]),
        pltpu.make_async_copy(w_out, w2.at[pl.ds(0, hd)], local_sem.at[5]),
    ]
    for copy in copies:
        copy.start()

    barrier = pltpu.get_barrier_semaphore()
    greet = [partner]
    greet += [(ctx, chip_at(d, 1) * 2 + core) for d in range(1, chips)]
    greet += [(lax.rem(ctx + e, ctxs), head) for e in range(1, ctxs)]
    for peer in greet:
        pl.semaphore_signal(barrier, inc=1, device_id=peer, device_id_type=MESH)
    pl.semaphore_wait(barrier, len(greet))

    relayed = (tall, wide) == (2, 2)
    direct = (1, 2) if relayed else range(1, chips)
    sends = []

    def send(*args):
        copy = remote(*args)
        copy.start()
        sends.append(copy)

    def part(r):
        return pl.ds(r * rows, rows)

    def across(d):
        return (ctx, chip_at(d, 1) * 2 + core)

    def half(r, d):
        return pl.ds(r * rows + (d - 1) * (rows // 2), rows // 2)

    def to_partner(r, d):
        send(x.at[d, 0, part(r)], x.at[d, 1, part(r)], fw_send.at[r, d], fw_recv.at[r, d], partner)

    def take_direct(r):
        for d in direct:
            arrived(x.at[d, 0, part(r)], ag_recv.at[r, d])
            if relayed:
                send(
                    x.at[d, 0, half(r, d)], x.at[3, 0, half(r, d)],
                    rl_send.at[r, d], rl_recv.at[r, d], across(3 - d),
                )
            to_partner(r, d)
        if r + AHEAD < ROW_CHUNKS:
            send_direct(r + AHEAD)

    def send_direct(r):
        for d in direct:
            send(tok.at[part(r)], x.at[d, 0, part(r)], ag_send.at[r, d], ag_recv.at[r, d], across(d))

    for r in range(AHEAD):
        send_direct(r)
    for r in range(ROW_CHUNKS):
        send(tok.at[part(r)], x.at[0, 1, part(r)], fw_send.at[r, 0], fw_recv.at[r, 0], partner)
    send(w_out, w2.at[pl.ds(hd, hd)], w2_sem.at[0], w2_sem.at[1], partner)

    copies[0].wait()
    copies[1].wait()
    num_codes = book_v.shape[0]
    hot = lax.broadcasted_iota(jnp.int32, (num_codes, blk), 0) == codes_v[...]
    kq[0] = lax.dot_general(
        hot.astype(F32).astype(BF16), book_v[...], (((0,), (0,)), ((), ())), preferred_element_type=F32
    ).astype(BF16)

    def later(e, src, dst, send_sem, recv_sem):
        @pl.when(ctx + e < ctxs)
        def _():
            remote(src, dst, send_sem, recv_sem, (lax.rem(ctx + e, ctxs), head)).start()

    for e in range(1, ctxs):
        later(e, kq.at[0], kq.at[e], kq_send.at[e], kq_recv.at[e])

    for copy in copies[2:]:
        copy.wait()

    def piece(d, other, block):
        source = chip_at(d, -1) * 2 + (1 - core if other else core)
        return jnp.dot(x[d, other, block], w[source], preferred_element_type=F32)

    early = direct if relayed else range(1, chips - 1)
    last = chips - 1

    def take_last(r):
        if relayed:
            for d in direct:
                arrived(x.at[3, 0, half(r, d)], rl_recv.at[r, d])
            to_partner(r, 3)

    def project_early(chunks):
        block = slice(chunks[0] * rows, (chunks[-1] + 1) * rows)
        for d in early:
            proj_s[block] += piece(d, 0, block)
        take_last(chunks[0])
        for d in early:
            for r in chunks:
                arrived(x.at[d, 1, part(r)], fw_recv.at[r, d])
            proj_s[block] += piece(d, 1, block)

    def project_last(r):
        block = slice(r * rows, (r + 1) * rows)
        proj = proj_s[block] + piece(last, 0, block)
        arrived(x.at[last, 1, part(r)], fw_recv.at[r, last])
        proj += piece(last, 1, block)
        q_s[block] = proj[:, :hd].astype(BF16)
        kz[0, block] = proj[:, hd:2 * hd].astype(BF16)
        vz[0, block] = proj[:, 2 * hd:].astype(BF16)
        later(1, kz.at[0, part(r)], kz.at[1, part(r)], k_send.at[r], k_recv.at[r])
        for e in range(1, ctxs):
            later(e, vz.at[0, part(r)], vz.at[e, part(r)], v_send.at[r, e], v_recv.at[r, e])

    def begin(chunks):
        low, high = chunks[0] * rows, (chunks[-1] + 1) * rows
        block = slice(low, high)
        own = nt(q_s[block], kz[0, :high])
        seen = lax.broadcasted_iota(jnp.int32, own.shape, 1) <= low + lax.broadcasted_iota(
            jnp.int32, own.shape, 0
        )
        own = jnp.where(seen, own, -jnp.inf)
        top_s[block] = jnp.broadcast_to(jnp.max(own, axis=1, keepdims=True), (high - low, hd))
        for e in range(2, ctxs):
            @pl.when(ctx >= e)
            def _():
                if low == 0:
                    arrived(kq.at[e], kq_recv.at[e])
                scores = nt(q_s[block], kq[e])
                score_s[e - 2, block] = scores
                top_s[block] = jnp.maximum(top_s[block], jnp.max(scores, axis=1, keepdims=True))

        probs = jnp.exp((own - top_s[block][:, :1]) * scale)
        den_s[block] = jnp.broadcast_to(jnp.sum(probs, axis=1, keepdims=True), (high - low, hd))
        acc_s[block] = jnp.dot(probs.astype(BF16), vz[0, :high], preferred_element_type=F32)
        for e in range(2, ctxs):
            @pl.when(ctx >= e)
            def _():
                probs = jnp.exp((score_s[e - 2, block] - top_s[block][:, :1]) * scale)
                prob_s[e - 2, block] = probs.astype(BF16)
                den_s[block] += jnp.sum(probs, axis=1, keepdims=True)

    every = slice(0, blk)
    proj_s[...] = piece(0, 0, every)
    for r in range(ROW_CHUNKS):
        arrived(x.at[0, 1, part(r)], fw_recv.at[r, 0])
    proj_s[...] += piece(0, 1, every)
    for r in range(AHEAD):
        take_direct(r)
    taken = AHEAD
    for chunks in GROUPS:
        while taken <= chunks[-1]:
            take_direct(taken)
            taken += 1
        project_early(chunks)
        if taken < ROW_CHUNKS:
            take_direct(taken)
            taken += 1
        for r in chunks:
            if r > chunks[0]:
                take_last(r)
            project_last(r)
        begin(chunks)

    @pl.when(ctx >= 1)
    def _():
        arrived(kq.at[1], kq_recv.at[1])
        for r in range(ROW_CHUNKS):
            arrived(kz.at[1, part(r)], k_recv.at[r])
        keys = kq[1]
        position = lax.broadcasted_iota(jnp.int32, keys.shape, 0)
        keys = jnp.where(position >= blk - reach_s[0], kz[1], keys)
        scores = nt(q_s[...], keys)
        old = top_s[...]
        top = jnp.maximum(old, jnp.max(scores, axis=1, keepdims=True))
        fade = jnp.exp((old - top) * scale)
        probs = jnp.exp((scores - top[:, :1]) * scale)
        fade_s[...] = fade
        den_s[...] = den_s[...] * fade + jnp.sum(probs, axis=1, keepdims=True)
        for r in range(ROW_CHUNKS):
            arrived(vz.at[1, part(r)], v_recv.at[r, 1])
        acc_s[...] = acc_s[...] * fade + jnp.dot(
            probs.astype(BF16), vz[1], preferred_element_type=F32
        )

    for e in range(2, ctxs):
        @pl.when(ctx >= e)
        def _():
            for r in range(ROW_CHUNKS):
                arrived(vz.at[e, part(r)], v_recv.at[r, e])
            acc_s[...] += fade_s[...] * jnp.dot(prob_s[e - 2], vz[e], preferred_element_type=F32)

    attended = acc_s[...] / den_s[...]
    for h in range(heads):
        att[h % 2, h // 2] = attended[h * rp:(h + 1) * rp].astype(BF16)
    send(att.at[1 - core], att_p, att_sem.at[0], att_sem.at[1], partner)
    mine = att[core].astype(F32).reshape(chips * rp, hd).astype(BF16)
    arrived(att_p, att_sem.at[1])
    other = att_p[...].astype(F32).reshape(chips * rp, hd).astype(BF16)
    arrived(w2.at[pl.ds(hd, hd)], w2_sem.at[1])
    both = jnp.concatenate([mine, other], axis=1)

    for j in range(COL_CHUNKS):
        block = jnp.dot(both, w2[:, j * cols:(j + 1) * cols], preferred_element_type=F32)
        for c in range(chips):
            term[j, c] = block[c * rp:(c + 1) * rp].astype(BF16)
        if relayed:
            first = 1 + j % 2
            send(term.at[j, chip_at(3, 1)], got.at[j, 3], rs_send.at[j, 3], rs_recv.at[j, 3], across(first))
        else:
            for d in direct:
                send(term.at[j, chip_at(d, 1)], got.at[j, d], rs_send.at[j, d], rs_recv.at[j, d], across(d))

    if relayed:
        for j in range(COL_CHUNKS):
            first = 1 + j % 2
            send(
                term.at[j, chip_at(first, 1)], got.at[j, first],
                rs_send.at[j, first], rs_recv.at[j, first], across(first),
            )
        for j in range(COL_CHUNKS):
            second = 2 - j % 2
            arrived(got.at[j, 3], rs_recv.at[j, 3])
            pair = got[j, 3].astype(F32) + term[j, chip_at(second, 1)].astype(F32)
            pre[j] = pair.astype(BF16)
            send(
                pre.at[j], got.at[j, second], rs_send.at[j, second], rs_recv.at[j, second], across(second)
            )

    results = []
    for j in range(COL_CHUNKS):
        total = term[j, chip].astype(F32)
        for d in direct:
            arrived(got.at[j, d], rs_recv.at[j, d])
            total += got[j, d].astype(F32)
        out_v[:, j * cols:(j + 1) * cols] = total
        results.append(
            pltpu.make_async_copy(
                out_v.at[:, pl.ds(j * cols, cols)], out.at[:, pl.ds(j * cols, cols)], out_sem.at[j]
            )
        )
        results[-1].start()

    for copy in results:
        copy.wait()
    for copy in sends:
        copy.wait_send()
    for e in range(1, ctxs):
        @pl.when(ctx + e < ctxs)
        def _():
            remote(kq.at[0], kq.at[e], kq_send.at[e], kq_recv.at[e], partner).wait_send()
            for r in range(ROW_CHUNKS):
                if e == 1:
                    remote(kz.at[0, part(r)], kz.at[1, part(r)], k_send.at[r], k_recv.at[r], partner).wait_send()
                remote(
                    vz.at[0, part(r)], vz.at[e, part(r)], v_send.at[r, e], v_recv.at[r, e], partner
                ).wait_send()


def solution(mesh):
    ctxs, heads = mesh.shape["ctx"], mesh.shape["head"]
    chips = heads // 2

    def on_device(tokens_in, w_qkv, w_out, codebook, codes, reach):
        blk, depth = tokens_in.shape
        num_codes, hd = codebook.shape[1:]
        wide = w_out.shape[2]
        rp = blk // heads
        cols = wide // COL_CHUNKS
        dma = pltpu.SemaphoreType.DMA
        return pl.pallas_call(
            functools.partial(kernel, (ctxs, heads, blk, hd)),
            out_shape=jax.ShapeDtypeStruct((rp, wide), F32),
            in_specs=[pl.BlockSpec(memory_space=pltpu.HBM)] * 6,
            out_specs=pl.BlockSpec(memory_space=pltpu.HBM),
            scratch_shapes=[
                pltpu.VMEM((chips, 2, blk, depth), BF16),
                pltpu.VMEM((blk, 3 * hd), F32),
                pltpu.VMEM((heads, depth, 3 * hd), BF16),
                pltpu.VMEM((2 * hd, wide), BF16),
                pltpu.VMEM((num_codes, hd), BF16),
                pltpu.VMEM((1, blk), jnp.int32),
                pltpu.SMEM((1,), jnp.int32),
                pltpu.VMEM((ctxs, blk, hd), BF16),
                pltpu.VMEM((2, blk, hd), BF16),
                pltpu.VMEM((ctxs, blk, hd), BF16),
                pltpu.VMEM((blk, hd), BF16),
                pltpu.VMEM((blk, hd), F32),
                pltpu.VMEM((blk, hd), F32),
                pltpu.VMEM((blk, hd), F32),
                pltpu.VMEM((blk, hd), F32),
                pltpu.VMEM((max(ctxs - 2, 1), blk, blk), F32),
                pltpu.VMEM((max(ctxs - 2, 1), blk, blk), BF16),
                pltpu.VMEM((rp, wide), F32),
                pltpu.VMEM((2, chips, rp, hd), BF16),
                pltpu.VMEM((chips, rp, hd), BF16),
                pltpu.VMEM((COL_CHUNKS, chips, rp, cols), BF16),
                pltpu.VMEM((COL_CHUNKS, chips, rp, cols), BF16),
                pltpu.VMEM((COL_CHUNKS, rp, cols), BF16),
                dma((6,)),
                dma((ROW_CHUNKS, chips)),
                dma((ROW_CHUNKS, chips)),
                dma((ROW_CHUNKS, chips)),
                dma((ROW_CHUNKS, chips)),
                dma((ROW_CHUNKS, chips)),
                dma((ROW_CHUNKS, chips)),
                dma((2,)),
                dma((ctxs,)),
                dma((ctxs,)),
                dma((ROW_CHUNKS,)),
                dma((ROW_CHUNKS,)),
                dma((ROW_CHUNKS, ctxs)),
                dma((ROW_CHUNKS, ctxs)),
                dma((2,)),
                dma((COL_CHUNKS, chips)),
                dma((COL_CHUNKS, chips)),
                dma((COL_CHUNKS,)),
            ],
            compiler_params=pltpu.CompilerParams(
                collective_id=0, has_side_effects=True, vmem_limit_bytes=60 * 1024 * 1024
            ),
            cost_estimate=pl.CostEstimate(
                flops=2 * blk * heads * depth * 3 * hd, bytes_accessed=6 * 1024 * 1024, transcendentals=blk * blk
            ),
        )(
            tokens_in, w_qkv[:, 0, :].reshape(heads, depth, 3 * hd), w_out[0], codebook[0], codes, reach
        ).astype(BF16)

    in_specs = (
        P("ctx", "head"),
        P(None, "head", None),
        P("head", None, None),
        P("head", None, None),
        P("head", "ctx"),
        P("ctx"),
    )
    return jax.shard_map(
        on_device, mesh=mesh, in_specs=in_specs, out_specs=P(("ctx", "head"), None), check_vma=False
    )
```

```python
import functools
import math

import jax
import jax.numpy as jnp
from jax import lax
from jax.experimental import pallas as pl
from jax.experimental.pallas import tpu as pltpu
from jax.sharding import PartitionSpec as P

MESH = pl.DeviceIdType.MESH
F32 = jnp.float32
BF16 = jnp.bfloat16
ROW_CHUNKS = 4
COL_CHUNKS = 8
AHEAD = 2
GROUPS = (((0, 1),), ((2,), (3,)))


def grid_of(chips):
    wide = 1 << ((chips.bit_length() - 1) // 2)
    return chips // wide, wide


def nt(a, b):
    return lax.dot_general(a, b, (((1,), (1,)), ((), ())), preferred_element_type=F32)


def kernel(
    sizes,
    tok, w_in, w_out, book, codes, reach, out,
    x, proj_s, w, w2, book_v, codes_v, reach_s, kq, kz, vz, q_s, top_s, den_s, acc_s, fade_s, score_s, prob_s, out_v, att, att_p, term, got, pre,
    local_sem, ag_send, ag_recv, fw_send, fw_recv, rl_send, rl_recv, w2_sem, kq_send, kq_recv, k_send, k_recv,
    v_send, v_recv, att_sem, rs_send, rs_recv, out_sem,
):
    ctxs, heads, blk, hd = sizes
    chips = heads // 2
    tall, wide = grid_of(chips)
    scale = 1.0 / math.sqrt(hd)
    rows = blk // ROW_CHUNKS
    cols = out.shape[1] // COL_CHUNKS
    rp = out.shape[0]
    ctx, head = lax.axis_index("ctx"), lax.axis_index("head")
    chip, core = head // 2, head % 2
    partner = (ctx, chip * 2 + 1 - core)

    def chip_at(d, sign):
        up, across = d // wide, d % wide
        row = lax.rem(chip // wide + (up if sign > 0 else tall - up), tall)
        col = lax.rem(chip % wide + (across if sign > 0 else wide - across), wide)
        return row * wide + col

    def remote(src, dst, send, recv, to):
        return pltpu.make_async_remote_copy(
            src_ref=src, dst_ref=dst, send_sem=send, recv_sem=recv, device_id=to, device_id_type=MESH
        )

    def arrived(dst, sem):
        remote(dst, dst, sem, sem, partner).wait_recv()

    copies = [
        pltpu.make_async_copy(codes, codes_v, local_sem.at[0]),
        pltpu.make_async_copy(book, book_v, local_sem.at[1]),
        pltpu.make_async_copy(reach, reach_s, local_sem.at[2]),
        pltpu.make_async_copy(tok, x.at[0, 0], local_sem.at[3]),
        pltpu.make_async_copy(w_in, w, local_sem.at[4]),
        pltpu.make_async_copy(w_out, w2.at[pl.ds(0, hd)], local_sem.at[5]),
    ]
    for copy in copies:
        copy.start()

    barrier = pltpu.get_barrier_semaphore()
    greet = [partner]
    greet += [(ctx, chip_at(d, 1) * 2 + core) for d in range(1, chips)]
    greet += [(lax.rem(ctx + e, ctxs), head) for e in range(1, ctxs)]
    for peer in greet:
        pl.semaphore_signal(barrier, inc=1, device_id=peer, device_id_type=MESH)
    pl.semaphore_wait(barrier, len(greet))

    relayed = (tall, wide) == (2, 2)
    direct = (1, 2) if relayed else range(1, chips)
    sends = []

    def send(*args):
        copy = remote(*args)
        copy.start()
        sends.append(copy)

    def part(r):
        return pl.ds(r * rows, rows)

    def across(d):
        return (ctx, chip_at(d, 1) * 2 + core)

    def half(r, d):
        return pl.ds(r * rows + (d - 1) * (rows // 2), rows // 2)

    def to_partner(r, d):
        send(x.at[d, 0, part(r)], x.at[d, 1, part(r)], fw_send.at[r, d], fw_recv.at[r, d], partner)

    def take_direct(r):
        for d in direct:
            arrived(x.at[d, 0, part(r)], ag_recv.at[r, d])
            if relayed:
                send(
                    x.at[d, 0, half(r, d)], x.at[3, 0, half(r, d)],
                    rl_send.at[r, d], rl_recv.at[r, d], across(3 - d),
                )
            to_partner(r, d)
        if r + AHEAD < ROW_CHUNKS:
            send_direct(r + AHEAD)

    def send_direct(r):
        for d in direct:
            send(tok.at[part(r)], x.at[d, 0, part(r)], ag_send.at[r, d], ag_recv.at[r, d], across(d))

    for r in range(AHEAD):
        send_direct(r)
    for r in range(ROW_CHUNKS):
        send(tok.at[part(r)], x.at[0, 1, part(r)], fw_send.at[r, 0], fw_recv.at[r, 0], partner)
    send(w_out, w2.at[pl.ds(hd, hd)], w2_sem.at[0], w2_sem.at[1], partner)

    copies[0].wait()
    copies[1].wait()
    num_codes = book_v.shape[0]
    hot = lax.broadcasted_iota(jnp.int32, (num_codes, blk), 0) == codes_v[...]
    kq[0] = lax.dot_general(
        hot.astype(F32).astype(BF16), book_v[...], (((0,), (0,)), ((), ())), preferred_element_type=F32
    ).astype(BF16)

    def later(e, src, dst, send_sem, recv_sem):
        @pl.when(ctx + e < ctxs)
        def _():
            remote(src, dst, send_sem, recv_sem, (lax.rem(ctx + e, ctxs), head)).start()

    for e in range(1, ctxs):
        later(e, kq.at[0], kq.at[e], kq_send.at[e], kq_recv.at[e])

    for copy in copies[2:]:
        copy.wait()

    def piece(d, other, block):
        source = chip_at(d, -1) * 2 + (1 - core if other else core)
        return jnp.dot(x[d, other, block], w[source], preferred_element_type=F32)

    early = direct if relayed else range(1, chips - 1)
    last = chips - 1

    def take_last(r):
        if relayed:
            for d in direct:
                arrived(x.at[3, 0, half(r, d)], rl_recv.at[r, d])
            to_partner(r, 3)

    def project_early(chunks):
        block = slice(chunks[0] * rows, (chunks[-1] + 1) * rows)
        for d in early:
            proj_s[block] += piece(d, 0, block)
        take_last(chunks[0])
        for d in early:
            for r in chunks:
                arrived(x.at[d, 1, part(r)], fw_recv.at[r, d])
            proj_s[block] += piece(d, 1, block)

    def project_last(chunks):
        block = slice(chunks[0] * rows, (chunks[-1] + 1) * rows)
        proj = proj_s[block] + piece(last, 0, block)
        for r in chunks:
            arrived(x.at[last, 1, part(r)], fw_recv.at[r, last])
        proj += piece(last, 1, block)
        q_s[block] = proj[:, :hd].astype(BF16)
        kz[0, block] = proj[:, hd:2 * hd].astype(BF16)
        vz[0, block] = proj[:, 2 * hd:].astype(BF16)
        for r in chunks:
            later(1, kz.at[0, part(r)], kz.at[1, part(r)], k_send.at[r], k_recv.at[r])
            later(1, vz.at[0, part(r)], vz.at[1, part(r)], v_send.at[r, 1], v_recv.at[r, 1])
        for e in range(2, ctxs):
            for r in chunks:
                later(e, vz.at[0, part(r)], vz.at[e, part(r)], v_send.at[r, e], v_recv.at[r, e])

    every = slice(0, blk)
    proj_s[...] = piece(0, 0, every)
    for r in range(ROW_CHUNKS):
        arrived(x.at[0, 1, part(r)], fw_recv.at[r, 0])
    proj_s[...] += piece(0, 1, every)
    for r in range(AHEAD):
        take_direct(r)
    taken = AHEAD
    for group in GROUPS:
        chunks = sum(group, ())
        while taken <= chunks[-1]:
            take_direct(taken)
            taken += 1
        project_early(chunks)
        if taken < ROW_CHUNKS:
            take_direct(taken)
            taken += 1
        for some in group:
            for r in some:
                if r > chunks[0]:
                    take_last(r)
            project_last(some)

    queries = q_s[...]
    own = nt(queries, kz[0])
    seen = lax.broadcasted_iota(jnp.int32, own.shape, 1) <= lax.broadcasted_iota(jnp.int32, own.shape, 0)
    own = jnp.where(seen, own, -jnp.inf)
    top_s[...] = jnp.broadcast_to(jnp.max(own, axis=1, keepdims=True), top_s.shape)
    for e in range(2, ctxs):
        @pl.when(ctx >= e)
        def _():
            arrived(kq.at[e], kq_recv.at[e])
            scores = nt(q_s[...], kq[e])
            score_s[e - 2] = scores
            top_s[...] = jnp.maximum(top_s[...], jnp.max(scores, axis=1, keepdims=True))

    probs = jnp.exp((own - top_s[...][:, :1]) * scale)
    den_s[...] = jnp.broadcast_to(jnp.sum(probs, axis=1, keepdims=True), den_s.shape)
    acc_s[...] = jnp.dot(probs.astype(BF16), vz[0], preferred_element_type=F32)
    for e in range(2, ctxs):
        @pl.when(ctx >= e)
        def _():
            probs = jnp.exp((score_s[e - 2] - top_s[...][:, :1]) * scale)
            prob_s[e - 2] = probs.astype(BF16)
            den_s[...] += jnp.sum(probs, axis=1, keepdims=True)

    @pl.when(ctx >= 1)
    def _():
        arrived(kq.at[1], kq_recv.at[1])
        for r in range(ROW_CHUNKS):
            arrived(kz.at[1, part(r)], k_recv.at[r])
        keys = kq[1]
        position = lax.broadcasted_iota(jnp.int32, keys.shape, 0)
        keys = jnp.where(position >= blk - reach_s[0], kz[1], keys)
        scores = nt(q_s[...], keys)
        old = top_s[...]
        top = jnp.maximum(old, jnp.max(scores, axis=1, keepdims=True))
        fade = jnp.exp((old - top) * scale)
        probs = jnp.exp((scores - top[:, :1]) * scale)
        fade_s[...] = fade
        den_s[...] = den_s[...] * fade + jnp.sum(probs, axis=1, keepdims=True)
        for r in range(ROW_CHUNKS):
            arrived(vz.at[1, part(r)], v_recv.at[r, 1])
        acc_s[...] = acc_s[...] * fade + jnp.dot(
            probs.astype(BF16), vz[1], preferred_element_type=F32
        )

    for e in range(2, ctxs):
        @pl.when(ctx >= e)
        def _():
            for r in range(ROW_CHUNKS):
                arrived(vz.at[e, part(r)], v_recv.at[r, e])
            acc_s[...] += fade_s[...] * jnp.dot(prob_s[e - 2], vz[e], preferred_element_type=F32)

    attended = acc_s[...] / den_s[...]
    for h in range(heads):
        att[h % 2, h // 2] = attended[h * rp:(h + 1) * rp].astype(BF16)
    send(att.at[1 - core], att_p, att_sem.at[0], att_sem.at[1], partner)
    mine = att[core].astype(F32).reshape(chips * rp, hd).astype(BF16)
    arrived(att_p, att_sem.at[1])
    other = att_p[...].astype(F32).reshape(chips * rp, hd).astype(BF16)
    arrived(w2.at[pl.ds(hd, hd)], w2_sem.at[1])
    both = jnp.concatenate([mine, other], axis=1)

    for j in range(COL_CHUNKS):
        block = jnp.dot(both, w2[:, j * cols:(j + 1) * cols], preferred_element_type=F32)
        for c in range(chips):
            term[j, c] = block[c * rp:(c + 1) * rp].astype(BF16)
        if relayed:
            first = 1 + j % 2
            send(term.at[j, chip_at(3, 1)], got.at[j, 3], rs_send.at[j, 3], rs_recv.at[j, 3], across(first))
        else:
            for d in direct:
                send(term.at[j, chip_at(d, 1)], got.at[j, d], rs_send.at[j, d], rs_recv.at[j, d], across(d))

    if relayed:
        for j in range(COL_CHUNKS):
            first = 1 + j % 2
            send(
                term.at[j, chip_at(first, 1)], got.at[j, first],
                rs_send.at[j, first], rs_recv.at[j, first], across(first),
            )
        for j in range(COL_CHUNKS):
            second = 2 - j % 2
            arrived(got.at[j, 3], rs_recv.at[j, 3])
            pair = got[j, 3].astype(F32) + term[j, chip_at(second, 1)].astype(F32)
            pre[j] = pair.astype(BF16)
            send(
                pre.at[j], got.at[j, second], rs_send.at[j, second], rs_recv.at[j, second], across(second)
            )

    results = []
    for j in range(COL_CHUNKS):
        total = term[j, chip].astype(F32)
        for d in direct:
            arrived(got.at[j, d], rs_recv.at[j, d])
            total += got[j, d].astype(F32)
        out_v[:, j * cols:(j + 1) * cols] = total.astype(BF16)
        results.append(
            pltpu.make_async_copy(
                out_v.at[:, pl.ds(j * cols, cols)], out.at[:, pl.ds(j * cols, cols)], out_sem.at[j]
            )
        )
        results[-1].start()

    for copy in results:
        copy.wait()
    for copy in sends:
        copy.wait_send()
    for e in range(1, ctxs):
        @pl.when(ctx + e < ctxs)
        def _():
            remote(kq.at[0], kq.at[e], kq_send.at[e], kq_recv.at[e], partner).wait_send()
            for r in range(ROW_CHUNKS):
                if e == 1:
                    remote(kz.at[0, part(r)], kz.at[1, part(r)], k_send.at[r], k_recv.at[r], partner).wait_send()
                remote(
                    vz.at[0, part(r)], vz.at[e, part(r)], v_send.at[r, e], v_recv.at[r, e], partner
                ).wait_send()


def solution(mesh):
    ctxs, heads = mesh.shape["ctx"], mesh.shape["head"]
    chips = heads // 2

    def on_device(tokens_in, w_qkv, w_out, codebook, codes, reach):
        blk, depth = tokens_in.shape
        num_codes, hd = codebook.shape[1:]
        wide = w_out.shape[2]
        rp = blk // heads
        cols = wide // COL_CHUNKS
        dma = pltpu.SemaphoreType.DMA
        return pl.pallas_call(
            functools.partial(kernel, (ctxs, heads, blk, hd)),
            out_shape=jax.ShapeDtypeStruct((rp, wide), BF16),
            in_specs=[pl.BlockSpec(memory_space=pltpu.HBM)] * 6,
            out_specs=pl.BlockSpec(memory_space=pltpu.HBM),
            scratch_shapes=[
                pltpu.VMEM((chips, 2, blk, depth), BF16),
                pltpu.VMEM((blk, 3 * hd), F32),
                pltpu.VMEM((heads, depth, 3 * hd), BF16),
                pltpu.VMEM((2 * hd, wide), BF16),
                pltpu.VMEM((num_codes, hd), BF16),
                pltpu.VMEM((1, blk), jnp.int32),
                pltpu.SMEM((1,), jnp.int32),
                pltpu.VMEM((ctxs, blk, hd), BF16),
                pltpu.VMEM((2, blk, hd), BF16),
                pltpu.VMEM((ctxs, blk, hd), BF16),
                pltpu.VMEM((blk, hd), BF16),
                pltpu.VMEM((blk, hd), F32),
                pltpu.VMEM((blk, hd), F32),
                pltpu.VMEM((blk, hd), F32),
                pltpu.VMEM((blk, hd), F32),
                pltpu.VMEM((max(ctxs - 2, 1), blk, blk), F32),
                pltpu.VMEM((max(ctxs - 2, 1), blk, blk), BF16),
                pltpu.VMEM((rp, wide), BF16),
                pltpu.VMEM((2, chips, rp, hd), BF16),
                pltpu.VMEM((chips, rp, hd), BF16),
                pltpu.VMEM((COL_CHUNKS, chips, rp, cols), BF16),
                pltpu.VMEM((COL_CHUNKS, chips, rp, cols), BF16),
                pltpu.VMEM((COL_CHUNKS, rp, cols), BF16),
                dma((6,)),
                dma((ROW_CHUNKS, chips)),
                dma((ROW_CHUNKS, chips)),
                dma((ROW_CHUNKS, chips)),
                dma((ROW_CHUNKS, chips)),
                dma((ROW_CHUNKS, chips)),
                dma((ROW_CHUNKS, chips)),
                dma((2,)),
                dma((ctxs,)),
                dma((ctxs,)),
                dma((ROW_CHUNKS,)),
                dma((ROW_CHUNKS,)),
                dma((ROW_CHUNKS, ctxs)),
                dma((ROW_CHUNKS, ctxs)),
                dma((2,)),
                dma((COL_CHUNKS, chips)),
                dma((COL_CHUNKS, chips)),
                dma((COL_CHUNKS,)),
            ],
            compiler_params=pltpu.CompilerParams(
                collective_id=0, has_side_effects=True, vmem_limit_bytes=60 * 1024 * 1024
            ),
            cost_estimate=pl.CostEstimate(
                flops=2 * blk * heads * depth * 3 * hd, bytes_accessed=6 * 1024 * 1024, transcendentals=blk * blk
            ),
        )(
            tokens_in, w_qkv[:, 0, :].reshape(heads, depth, 3 * hd), w_out[0], codebook[0], codes, reach
        )

    in_specs = (
        P("ctx", "head"),
        P(None, "head", None),
        P("head", None, None),
        P("head", None, None),
        P("head", "ctx"),
        P("ctx"),
    )
    return jax.shard_map(
        on_device, mesh=mesh, in_specs=in_specs, out_specs=P(("ctx", "head"), None), check_vma=False
    )
```

```python
import functools
import math

import jax
import jax.numpy as jnp
from jax import lax
from jax.experimental import pallas as pl
from jax.experimental.pallas import tpu as pltpu
from jax.sharding import PartitionSpec as P

MESH = pl.DeviceIdType.MESH
F32 = jnp.float32
BF16 = jnp.bfloat16
ROW_CHUNKS = 4
COL_CHUNKS = 4
AHEAD = 2
GROUPS = ((0,), (1,), (2, 3))


def grid_of(chips):
    wide = 1 << ((chips.bit_length() - 1) // 2)
    return chips // wide, wide


def parts_of(rp):
    return 2 if rp % 32 == 0 else 1


def nt(a, b):
    return lax.dot_general(a, b, (((1,), (1,)), ((), ())), preferred_element_type=F32)


def kernel(
    sizes,
    tok, w_in, w_out, book, codes, reach, out,
    x, proj_s, w, w2, book_v, codes_v, reach_s, kq, kz, vz, q_s, top_s, den_s, acc_s, fade_s, score_s, prob_s, out_v, att, att_p, term, got, pre,
    local_sem, ag_send, ag_recv, fw_send, fw_recv, rl_send, rl_recv, w2_sem, kq_send, kq_recv, k_send, k_recv,
    v_send, v_recv, att_sem, rs_send, rs_recv, out_sem,
):
    ctxs, heads, blk, hd = sizes
    chips = heads // 2
    tall, wide = grid_of(chips)
    scale = 1.0 / math.sqrt(hd)
    rows = blk // ROW_CHUNKS
    cols = out.shape[1] // COL_CHUNKS
    rp = out.shape[0]
    parts = parts_of(rp)
    hs, length = rp // parts, blk // parts
    ctx, head = lax.axis_index("ctx"), lax.axis_index("head")
    chip, core = head // 2, head % 2
    partner = (ctx, chip * 2 + 1 - core)

    def chip_at(d, sign):
        up, across = d // wide, d % wide
        row = lax.rem(chip // wide + (up if sign > 0 else tall - up), tall)
        col = lax.rem(chip % wide + (across if sign > 0 else wide - across), wide)
        return row * wide + col

    def remote(src, dst, send, recv, to):
        return pltpu.make_async_remote_copy(
            src_ref=src, dst_ref=dst, send_sem=send, recv_sem=recv, device_id=to, device_id_type=MESH
        )

    def arrived(dst, sem):
        remote(dst, dst, sem, sem, partner).wait_recv()

    copies = [
        pltpu.make_async_copy(codes, codes_v, local_sem.at[0]),
        pltpu.make_async_copy(book, book_v, local_sem.at[1]),
        pltpu.make_async_copy(reach, reach_s, local_sem.at[2]),
        pltpu.make_async_copy(tok, x.at[0, 0], local_sem.at[3]),
        pltpu.make_async_copy(w_in, w, local_sem.at[4]),
        pltpu.make_async_copy(w_out, w2.at[pl.ds(0, hd)], local_sem.at[5]),
    ]
    for copy in copies:
        copy.start()

    barrier = pltpu.get_barrier_semaphore()
    greet = [partner]
    greet += [(ctx, chip_at(d, 1) * 2 + core) for d in range(1, chips)]
    greet += [(lax.rem(ctx + e, ctxs), head) for e in range(1, ctxs)]
    for peer in greet:
        pl.semaphore_signal(barrier, inc=1, device_id=peer, device_id_type=MESH)
    pl.semaphore_wait(barrier, len(greet))

    relayed = (tall, wide) == (2, 2)
    direct = (1, 2) if relayed else range(1, chips)
    sends = []

    def send(*args):
        copy = remote(*args)
        copy.start()
        sends.append(copy)

    def part(r):
        return pl.ds(r * rows, rows)

    def across(d):
        return (ctx, chip_at(d, 1) * 2 + core)

    def half(r, d):
        return pl.ds(r * rows + (d - 1) * (rows // 2), rows // 2)

    def to_partner(r, d):
        send(x.at[d, 0, part(r)], x.at[d, 1, part(r)], fw_send.at[r, d], fw_recv.at[r, d], partner)

    def take_direct(r):
        for d in direct:
            arrived(x.at[d, 0, part(r)], ag_recv.at[r, d])
            if relayed:
                send(
                    x.at[d, 0, half(r, d)], x.at[3, 0, half(r, d)],
                    rl_send.at[r, d], rl_recv.at[r, d], across(3 - d),
                )
            to_partner(r, d)
        if r + AHEAD < ROW_CHUNKS:
            send_direct(r + AHEAD)

    def send_direct(r):
        for d in direct:
            send(tok.at[part(r)], x.at[d, 0, part(r)], ag_send.at[r, d], ag_recv.at[r, d], across(d))

    for r in range(AHEAD):
        send_direct(r)
    for r in range(ROW_CHUNKS):
        send(tok.at[part(r)], x.at[0, 1, part(r)], fw_send.at[r, 0], fw_recv.at[r, 0], partner)
    send(w_out, w2.at[pl.ds(hd, hd)], w2_sem.at[0], w2_sem.at[1], partner)

    copies[0].wait()
    copies[1].wait()
    num_codes = book_v.shape[0]
    hot = lax.broadcasted_iota(jnp.int32, (num_codes, blk), 0) == codes_v[...]
    kq[0] = lax.dot_general(
        hot.astype(F32).astype(BF16), book_v[...], (((0,), (0,)), ((), ())), preferred_element_type=F32
    ).astype(BF16)

    def later(e, src, dst, send_sem, recv_sem):
        @pl.when(ctx + e < ctxs)
        def _():
            remote(src, dst, send_sem, recv_sem, (lax.rem(ctx + e, ctxs), head)).start()

    for e in range(1, ctxs):
        later(e, kq.at[0], kq.at[e], kq_send.at[e], kq_recv.at[e])

    for copy in copies[2:]:
        copy.wait()

    def piece(d, other, block):
        source = chip_at(d, -1) * 2 + (1 - core if other else core)
        return jnp.dot(x[d, other, block], w[source], preferred_element_type=F32)

    early = direct if relayed else range(1, chips - 1)
    last = chips - 1

    def take_last(r):
        if relayed:
            for d in direct:
                arrived(x.at[3, 0, half(r, d)], rl_recv.at[r, d])
            to_partner(r, 3)

    def project_early(chunks):
        block = slice(chunks[0] * rows, (chunks[-1] + 1) * rows)
        for d in early:
            proj_s[block] += piece(d, 0, block)
        take_last(chunks[0])
        for d in early:
            for r in chunks:
                arrived(x.at[d, 1, part(r)], fw_recv.at[r, d])
            proj_s[block] += piece(d, 1, block)

    def project_last(r):
        block = slice(r * rows, (r + 1) * rows)
        proj = proj_s[block] + piece(last, 0, block)
        arrived(x.at[last, 1, part(r)], fw_recv.at[r, last])
        proj += piece(last, 1, block)
        for h in range(r * rows // rp, (r + 1) * rows // rp):
            for p in range(parts):
                low = h * rp + p * hs - r * rows
                q_s[p * length + h * hs:p * length + (h + 1) * hs] = proj[low:low + hs, :hd].astype(BF16)
        kz[0, block] = proj[:, hd:2 * hd].astype(BF16)
        vz[0, block] = proj[:, 2 * hd:].astype(BF16)
        later(1, kz.at[0, part(r)], kz.at[1, part(r)], k_send.at[r], k_recv.at[r])
        for e in range(1, ctxs):
            later(e, vz.at[0, part(r)], vz.at[e, part(r)], v_send.at[r, e], v_recv.at[r, e])

    every = slice(0, blk)
    proj_s[...] = piece(0, 0, every)
    for r in range(ROW_CHUNKS):
        arrived(x.at[0, 1, part(r)], fw_recv.at[r, 0])
    proj_s[...] += piece(0, 1, every)
    for r in range(AHEAD):
        take_direct(r)
    taken = AHEAD
    for chunks in GROUPS:
        while taken <= chunks[-1]:
            take_direct(taken)
            taken += 1
        project_early(chunks)
        if taken < ROW_CHUNKS:
            take_direct(taken)
            taken += 1
        for r in chunks:
            if r > chunks[0]:
                take_last(r)
            project_last(r)

    def begin(p):
        block = slice(p * length, (p + 1) * length)
        own = nt(q_s[block], kz[0])
        line = lax.broadcasted_iota(jnp.int32, own.shape, 0)
        line = line + lax.div(line, hs) * (rp - hs) + p * hs
        own = jnp.where(lax.broadcasted_iota(jnp.int32, own.shape, 1) <= line, own, -jnp.inf)
        top_s[block] = jnp.broadcast_to(jnp.max(own, axis=1, keepdims=True), (length, hd))
        for e in range(2, ctxs):
            @pl.when(ctx >= e)
            def _():
                if p == 0:
                    arrived(kq.at[e], kq_recv.at[e])
                scores = nt(q_s[block], kq[e])
                score_s[e - 2, block] = scores
                top_s[block] = jnp.maximum(top_s[block], jnp.max(scores, axis=1, keepdims=True))

        probs = jnp.exp((own - top_s[block][:, :1]) * scale)
        den_s[block] = jnp.broadcast_to(jnp.sum(probs, axis=1, keepdims=True), (length, hd))
        acc_s[block] = jnp.dot(probs.astype(BF16), vz[0], preferred_element_type=F32)
        for e in range(2, ctxs):
            @pl.when(ctx >= e)
            def _():
                probs = jnp.exp((score_s[e - 2, block] - top_s[block][:, :1]) * scale)
                prob_s[e - 2, block] = probs.astype(BF16)
                den_s[block] += jnp.sum(probs, axis=1, keepdims=True)

    def finish(p):
        block = slice(p * length, (p + 1) * length)

        @pl.when(ctx >= 1)
        def _():
            if p == 0:
                arrived(kq.at[1], kq_recv.at[1])
                for r in range(ROW_CHUNKS):
                    arrived(kz.at[1, part(r)], k_recv.at[r])
                position = lax.broadcasted_iota(jnp.int32, (blk, hd), 0)
                kq[1] = jnp.where(position >= blk - reach_s[0], kz[1], kq[1])
            scores = nt(q_s[block], kq[1])
            old = top_s[block]
            top = jnp.maximum(old, jnp.max(scores, axis=1, keepdims=True))
            fade = jnp.exp((old - top) * scale)
            probs = jnp.exp((scores - top[:, :1]) * scale)
            fade_s[block] = fade
            den_s[block] = den_s[block] * fade + jnp.sum(probs, axis=1, keepdims=True)
            if p == 0:
                for r in range(ROW_CHUNKS):
                    arrived(vz.at[1, part(r)], v_recv.at[r, 1])
            acc_s[block] = acc_s[block] * fade + jnp.dot(
                probs.astype(BF16), vz[1], preferred_element_type=F32
            )

        for e in range(2, ctxs):
            @pl.when(ctx >= e)
            def _():
                if p == 0:
                    for r in range(ROW_CHUNKS):
                        arrived(vz.at[e, part(r)], v_recv.at[r, e])
                acc_s[block] += fade_s[block] * jnp.dot(
                    prob_s[e - 2, block], vz[e], preferred_element_type=F32
                )

        attended = acc_s[block] / den_s[block]
        for h in range(heads):
            att[p, h % 2, h // 2] = attended[h * hs:(h + 1) * hs].astype(BF16)
        send(att.at[p, 1 - core], att_p.at[p], att_sem.at[p, 0], att_sem.at[p, 1], partner)

    def project_out(p):
        mine = att[p, core].astype(F32).reshape(chips * hs, hd).astype(BF16)
        arrived(att_p.at[p], att_sem.at[p, 1])
        other = att_p[p].astype(F32).reshape(chips * hs, hd).astype(BF16)
        if p == 0:
            arrived(w2.at[pl.ds(hd, hd)], w2_sem.at[1])
        both = jnp.concatenate([mine, other], axis=1)
        for j in range(COL_CHUNKS):
            i = p * COL_CHUNKS + j
            block = jnp.dot(both, w2[:, j * cols:(j + 1) * cols], preferred_element_type=F32)
            for c in range(chips):
                term[i, c] = block[c * hs:(c + 1) * hs].astype(BF16)
            if relayed:
                first = 1 + j % 2
                send(term.at[i, chip_at(3, 1)], got.at[i, 3], rs_send.at[i, 3], rs_recv.at[i, 3], across(first))
            else:
                for d in direct:
                    send(term.at[i, chip_at(d, 1)], got.at[i, d], rs_send.at[i, d], rs_recv.at[i, d], across(d))
        if relayed:
            for j in range(COL_CHUNKS):
                i, first = p * COL_CHUNKS + j, 1 + j % 2
                send(
                    term.at[i, chip_at(first, 1)], got.at[i, first],
                    rs_send.at[i, first], rs_recv.at[i, first], across(first),
                )

    def pass_on(p):
        if relayed:
            for j in range(COL_CHUNKS):
                i, second = p * COL_CHUNKS + j, 2 - j % 2
                arrived(got.at[i, 3], rs_recv.at[i, 3])
                pair = got[i, 3].astype(F32) + term[i, chip_at(second, 1)].astype(F32)
                pre[i] = pair.astype(BF16)
                send(
                    pre.at[i], got.at[i, second], rs_send.at[i, second], rs_recv.at[i, second], across(second)
                )

    results = []

    def add_up(p):
        lines = slice(p * hs, (p + 1) * hs)
        for j in range(COL_CHUNKS):
            i = p * COL_CHUNKS + j
            total = term[i, chip].astype(F32)
            for d in direct:
                arrived(got.at[i, d], rs_recv.at[i, d])
                total += got[i, d].astype(F32)
            out_v[lines, j * cols:(j + 1) * cols] = total.astype(BF16)
            here = (pl.ds(p * hs, hs), pl.ds(j * cols, cols))
            results.append(pltpu.make_async_copy(out_v.at[here], out.at[here], out_sem.at[i]))
            results[-1].start()

    begin(0)
    finish(0)
    for p in range(1, parts):
        begin(p)
        project_out(p - 1)
        finish(p)
        pass_on(p - 1)
    project_out(parts - 1)
    pass_on(parts - 1)
    for p in range(parts):
        add_up(p)

    for copy in results:
        copy.wait()
    for copy in sends:
        copy.wait_send()
    for e in range(1, ctxs):
        @pl.when(ctx + e < ctxs)
        def _():
            remote(kq.at[0], kq.at[e], kq_send.at[e], kq_recv.at[e], partner).wait_send()
            for r in range(ROW_CHUNKS):
                if e == 1:
                    remote(kz.at[0, part(r)], kz.at[1, part(r)], k_send.at[r], k_recv.at[r], partner).wait_send()
                remote(
                    vz.at[0, part(r)], vz.at[e, part(r)], v_send.at[r, e], v_recv.at[r, e], partner
                ).wait_send()


def solution(mesh):
    ctxs, heads = mesh.shape["ctx"], mesh.shape["head"]
    chips = heads // 2

    def on_device(tokens_in, w_qkv, w_out, codebook, codes, reach):
        blk, depth = tokens_in.shape
        num_codes, hd = codebook.shape[1:]
        wide = w_out.shape[2]
        rp = blk // heads
        cols = wide // COL_CHUNKS
        parts = parts_of(rp)
        hs, pieces = rp // parts, parts * COL_CHUNKS
        dma = pltpu.SemaphoreType.DMA
        return pl.pallas_call(
            functools.partial(kernel, (ctxs, heads, blk, hd)),
            out_shape=jax.ShapeDtypeStruct((rp, wide), BF16),
            in_specs=[pl.BlockSpec(memory_space=pltpu.HBM)] * 6,
            out_specs=pl.BlockSpec(memory_space=pltpu.HBM),
            scratch_shapes=[
                pltpu.VMEM((chips, 2, blk, depth), BF16),
                pltpu.VMEM((blk, 3 * hd), F32),
                pltpu.VMEM((heads, depth, 3 * hd), BF16),
                pltpu.VMEM((2 * hd, wide), BF16),
                pltpu.VMEM((num_codes, hd), BF16),
                pltpu.VMEM((1, blk), jnp.int32),
                pltpu.SMEM((1,), jnp.int32),
                pltpu.VMEM((ctxs, blk, hd), BF16),
                pltpu.VMEM((2, blk, hd), BF16),
                pltpu.VMEM((ctxs, blk, hd), BF16),
                pltpu.VMEM((blk, hd), BF16),
                pltpu.VMEM((blk, hd), F32),
                pltpu.VMEM((blk, hd), F32),
                pltpu.VMEM((blk, hd), F32),
                pltpu.VMEM((blk, hd), F32),
                pltpu.VMEM((max(ctxs - 2, 1), blk, blk), F32),
                pltpu.VMEM((max(ctxs - 2, 1), blk, blk), BF16),
                pltpu.VMEM((rp, wide), BF16),
                pltpu.VMEM((parts, 2, chips, hs, hd), BF16),
                pltpu.VMEM((parts, chips, hs, hd), BF16),
                pltpu.VMEM((pieces, chips, hs, cols), BF16),
                pltpu.VMEM((pieces, chips, hs, cols), BF16),
                pltpu.VMEM((pieces, hs, cols), BF16),
                dma((6,)),
                dma((ROW_CHUNKS, chips)),
                dma((ROW_CHUNKS, chips)),
                dma((ROW_CHUNKS, chips)),
                dma((ROW_CHUNKS, chips)),
                dma((ROW_CHUNKS, chips)),
                dma((ROW_CHUNKS, chips)),
                dma((2,)),
                dma((ctxs,)),
                dma((ctxs,)),
                dma((ROW_CHUNKS,)),
                dma((ROW_CHUNKS,)),
                dma((ROW_CHUNKS, ctxs)),
                dma((ROW_CHUNKS, ctxs)),
                dma((parts, 2)),
                dma((pieces, chips)),
                dma((pieces, chips)),
                dma((pieces,)),
            ],
            compiler_params=pltpu.CompilerParams(
                collective_id=0, has_side_effects=True, vmem_limit_bytes=60 * 1024 * 1024
            ),
            cost_estimate=pl.CostEstimate(
                flops=2 * blk * heads * depth * 3 * hd, bytes_accessed=6 * 1024 * 1024, transcendentals=blk * blk
            ),
        )(
            tokens_in, w_qkv[:, 0, :].reshape(heads, depth, 3 * hd), w_out[0], codebook[0], codes, reach
        )

    in_specs = (
        P("ctx", "head"),
        P(None, "head", None),
        P("head", None, None),
        P("head", None, None),
        P("head", "ctx"),
        P("ctx"),
    )
    return jax.shard_map(
        on_device, mesh=mesh, in_specs=in_specs, out_specs=P(("ctx", "head"), None), check_vma=False
    )
```

```python
import functools
import math

import jax
import jax.numpy as jnp
from jax import lax
from jax.experimental import pallas as pl
from jax.experimental.pallas import tpu as pltpu
from jax.sharding import PartitionSpec as P

MESH = pl.DeviceIdType.MESH
F32 = jnp.float32
BF16 = jnp.bfloat16
ROW_CHUNKS = 4
COL_CHUNKS = 4
AHEAD = 2
GROUPS = ((0,), (1,), (2, 3))


def grid_of(chips):
    wide = 1 << ((chips.bit_length() - 1) // 2)
    return chips // wide, wide


def nt(a, b):
    return lax.dot_general(a, b, (((1,), (1,)), ((), ())), preferred_element_type=F32)


def kernel(
    sizes,
    tok, w_in, w_out, book, codes, reach, out,
    x, proj_s, w, w2, book_v, codes_v, reach_s, kq, kz, vz, q_s, top_s, den_s, acc_s, fade_s, score_s, prob_s, out_v, att, att_p, term, got, pre,
    local_sem, ag_send, ag_recv, fw_send, fw_recv, rl_send, rl_recv, w2_sem, kq_send, kq_recv, k_send, k_recv,
    v_send, v_recv, att_sem, rs_send, rs_recv, out_sem,
):
    ctxs, heads, blk, hd = sizes
    chips = heads // 2
    tall, wide = grid_of(chips)
    scale = 1.0 / math.sqrt(hd)
    rows = blk // ROW_CHUNKS
    cols = out.shape[1] // COL_CHUNKS
    rp = out.shape[0]
    ctx, head = lax.axis_index("ctx"), lax.axis_index("head")
    chip, core = head // 2, head % 2
    partner = (ctx, chip * 2 + 1 - core)

    def chip_at(d, sign):
        up, across = d // wide, d % wide
        row = lax.rem(chip // wide + (up if sign > 0 else tall - up), tall)
        col = lax.rem(chip % wide + (across if sign > 0 else wide - across), wide)
        return row * wide + col

    def remote(src, dst, send, recv, to):
        return pltpu.make_async_remote_copy(
            src_ref=src, dst_ref=dst, send_sem=send, recv_sem=recv, device_id=to, device_id_type=MESH
        )

    def arrived(dst, sem):
        remote(dst, dst, sem, sem, partner).wait_recv()

    copies = [
        pltpu.make_async_copy(codes, codes_v, local_sem.at[0]),
        pltpu.make_async_copy(book, book_v, local_sem.at[1]),
        pltpu.make_async_copy(reach, reach_s, local_sem.at[2]),
        pltpu.make_async_copy(tok, x.at[0, 0], local_sem.at[3]),
        pltpu.make_async_copy(w_in, w, local_sem.at[4]),
        pltpu.make_async_copy(w_out, w2.at[pl.ds(0, hd)], local_sem.at[5]),
    ]
    for copy in copies:
        copy.start()

    relayed = (tall, wide) == (2, 2)
    direct = (1, 2) if relayed else range(1, chips)
    barrier = pltpu.get_barrier_semaphore()
    greet = [partner]
    greet += [(ctx, chip_at(d, 1) * 2 + core) for d in direct]
    greet += [(lax.rem(ctx + e, ctxs), head) for e in range(1, ctxs)]
    for peer in greet:
        pl.semaphore_signal(barrier, inc=1, device_id=peer, device_id_type=MESH)
    pl.semaphore_wait(barrier, len(greet))

    sends = []

    def send(*args):
        copy = remote(*args)
        copy.start()
        sends.append(copy)

    def part(r):
        return pl.ds(r * rows, rows)

    def across(d):
        return (ctx, chip_at(d, 1) * 2 + core)

    def half(r, d):
        return pl.ds(r * rows + (d - 1) * (rows // 2), rows // 2)

    def to_partner(r, d):
        send(x.at[d, 0, part(r)], x.at[d, 1, part(r)], fw_send.at[r, d], fw_recv.at[r, d], partner)

    def take_direct(r):
        for d in direct:
            arrived(x.at[d, 0, part(r)], ag_recv.at[r, d])
            if relayed:
                send(
                    x.at[d, 0, half(r, d)], x.at[3, 0, half(r, d)],
                    rl_send.at[r, d], rl_recv.at[r, d], across(3 - d),
                )
            to_partner(r, d)
        if r + AHEAD < ROW_CHUNKS:
            send_direct(r + AHEAD)

    def send_direct(r):
        for d in direct:
            send(tok.at[part(r)], x.at[d, 0, part(r)], ag_send.at[r, d], ag_recv.at[r, d], across(d))

    for r in range(AHEAD):
        send_direct(r)
    send(tok, x.at[0, 1], fw_send.at[0, 0], fw_recv.at[0, 0], partner)
    send(w_out, w2.at[pl.ds(hd, hd)], w2_sem.at[0], w2_sem.at[1], partner)

    copies[0].wait()
    copies[1].wait()
    num_codes = book_v.shape[0]
    hot = lax.broadcasted_iota(jnp.int32, (num_codes, blk), 0) == codes_v[...]
    kq[0] = lax.dot_general(
        hot.astype(F32).astype(BF16), book_v[...], (((0,), (0,)), ((), ())), preferred_element_type=F32
    ).astype(BF16)

    def later(e, src, dst, send_sem, recv_sem):
        @pl.when(ctx + e < ctxs)
        def _():
            remote(src, dst, send_sem, recv_sem, (lax.rem(ctx + e, ctxs), head)).start()

    for e in range(1, ctxs):
        later(e, kq.at[0], kq.at[e], kq_send.at[e], kq_recv.at[e])

    for copy in copies[2:]:
        copy.wait()

    def piece(d, other, block):
        source = chip_at(d, -1) * 2 + (1 - core if other else core)
        return jnp.dot(x[d, other, block], w[source], preferred_element_type=F32)

    early = direct if relayed else range(1, chips - 1)
    last = chips - 1

    def take_last(r):
        if relayed:
            for d in direct:
                arrived(x.at[3, 0, half(r, d)], rl_recv.at[r, d])
            to_partner(r, 3)

    def project_early(chunks):
        block = slice(chunks[0] * rows, (chunks[-1] + 1) * rows)
        proj = proj_s[block]
        for d in early:
            proj += piece(d, 0, block)
        take_last(chunks[0])
        for d in early:
            for r in chunks:
                arrived(x.at[d, 1, part(r)], fw_recv.at[r, d])
            proj += piece(d, 1, block)
        proj_s[block] = proj

    def project_last(r):
        block = slice(r * rows, (r + 1) * rows)
        proj = proj_s[block] + piece(last, 0, block)
        arrived(x.at[last, 1, part(r)], fw_recv.at[r, last])
        proj += piece(last, 1, block)
        q_s[block] = proj[:, :hd].astype(BF16)
        kz[0, block] = proj[:, hd:2 * hd].astype(BF16)
        vz[0, block] = proj[:, 2 * hd:].astype(BF16)
        later(1, kz.at[0, part(r)], kz.at[1, part(r)], k_send.at[r], k_recv.at[r])
        for e in range(1, ctxs):
            later(e, vz.at[0, part(r)], vz.at[e, part(r)], v_send.at[r, e], v_recv.at[r, e])

    every = slice(0, blk)
    arrived(x.at[0, 1], fw_recv.at[0, 0])
    proj_s[...] = piece(0, 0, every) + piece(0, 1, every)
    for r in range(AHEAD):
        take_direct(r)
    taken = AHEAD
    for chunks in GROUPS:
        while taken <= chunks[-1]:
            take_direct(taken)
            taken += 1
        project_early(chunks)
        if taken < ROW_CHUNKS:
            take_direct(taken)
            taken += 1
        for r in chunks:
            if r > chunks[0]:
                take_last(r)
            project_last(r)

    queries = q_s[...]
    own = nt(queries, kz[0])
    seen = lax.broadcasted_iota(jnp.int32, own.shape, 1) <= lax.broadcasted_iota(jnp.int32, own.shape, 0)
    own = jnp.where(seen, own, -jnp.inf)
    top_s[...] = jnp.broadcast_to(jnp.max(own, axis=1, keepdims=True), top_s.shape)
    for e in range(2, ctxs):
        @pl.when(ctx >= e)
        def _():
            arrived(kq.at[e], kq_recv.at[e])
            scores = nt(q_s[...], kq[e])
            score_s[e - 2] = scores
            top_s[...] = jnp.maximum(top_s[...], jnp.max(scores, axis=1, keepdims=True))

    probs = jnp.exp((own - top_s[...][:, :1]) * scale)
    den_s[...] = jnp.broadcast_to(jnp.sum(probs, axis=1, keepdims=True), den_s.shape)
    acc_s[...] = jnp.dot(probs.astype(BF16), vz[0], preferred_element_type=F32)
    for e in range(2, ctxs):
        @pl.when(ctx >= e)
        def _():
            probs = jnp.exp((score_s[e - 2] - top_s[...][:, :1]) * scale)
            prob_s[e - 2] = probs.astype(BF16)
            den_s[...] += jnp.sum(probs, axis=1, keepdims=True)

    @pl.when(ctx >= 1)
    def _():
        arrived(kq.at[1], kq_recv.at[1])
        for r in range(ROW_CHUNKS):
            arrived(kz.at[1, part(r)], k_recv.at[r])
        keys = kq[1]
        position = lax.broadcasted_iota(jnp.int32, keys.shape, 0)
        keys = jnp.where(position >= blk - reach_s[0], kz[1], keys)
        scores = nt(q_s[...], keys)
        old = top_s[...]
        top = jnp.maximum(old, jnp.max(scores, axis=1, keepdims=True))
        fade = jnp.exp((old - top) * scale)
        probs = jnp.exp((scores - top[:, :1]) * scale)
        fade_s[...] = fade
        den_s[...] = den_s[...] * fade + jnp.sum(probs, axis=1, keepdims=True)
        for r in range(ROW_CHUNKS):
            arrived(vz.at[1, part(r)], v_recv.at[r, 1])
        acc_s[...] = acc_s[...] * fade + jnp.dot(
            probs.astype(BF16), vz[1], preferred_element_type=F32
        )

    for e in range(2, ctxs):
        @pl.when(ctx >= e)
        def _():
            for r in range(ROW_CHUNKS):
                arrived(vz.at[e, part(r)], v_recv.at[r, e])
            acc_s[...] += fade_s[...] * jnp.dot(prob_s[e - 2], vz[e], preferred_element_type=F32)

    attended = acc_s[...] / den_s[...]
    for h in range(heads):
        att[h % 2, h // 2] = attended[h * rp:(h + 1) * rp].astype(BF16)
    send(att.at[1 - core], att_p, att_sem.at[0], att_sem.at[1], partner)
    mine = att[core].astype(F32).reshape(chips * rp, hd).astype(BF16)
    arrived(att_p, att_sem.at[1])
    other = att_p[...].astype(F32).reshape(chips * rp, hd).astype(BF16)
    arrived(w2.at[pl.ds(hd, hd)], w2_sem.at[1])
    both = jnp.concatenate([mine, other], axis=1)

    before = len(sends)
    for j in range(COL_CHUNKS):
        block = jnp.dot(both, w2[:, j * cols:(j + 1) * cols], preferred_element_type=F32)
        for c in range(chips):
            term[j, c] = block[c * rp:(c + 1) * rp].astype(BF16)
        if relayed:
            first = 1 + j % 2
            send(term.at[j, chip_at(3, 1)], got.at[j, 3], rs_send.at[j, 3], rs_recv.at[j, 3], across(first))
        else:
            for d in direct:
                send(term.at[j, chip_at(d, 1)], got.at[j, d], rs_send.at[j, d], rs_recv.at[j, d], across(d))

    if relayed:
        for j in range(COL_CHUNKS):
            first = 1 + j % 2
            send(
                term.at[j, chip_at(first, 1)], got.at[j, first],
                rs_send.at[j, first], rs_recv.at[j, first], across(first),
            )
    for copy in sends[:before]:
        copy.wait_send()
    for e in range(1, ctxs):
        @pl.when(ctx + e < ctxs)
        def _():
            remote(kq.at[0], kq.at[e], kq_send.at[e], kq_recv.at[e], partner).wait_send()
            for r in range(ROW_CHUNKS):
                if e == 1:
                    remote(kz.at[0, part(r)], kz.at[1, part(r)], k_send.at[r], k_recv.at[r], partner).wait_send()
                remote(
                    vz.at[0, part(r)], vz.at[e, part(r)], v_send.at[r, e], v_recv.at[r, e], partner
                ).wait_send()

    if relayed:
        for j in range(COL_CHUNKS):
            second = 2 - j % 2
            arrived(got.at[j, 3], rs_recv.at[j, 3])
            pair = got[j, 3].astype(F32) + term[j, chip_at(second, 1)].astype(F32)
            pre[j] = pair.astype(BF16)
            send(
                pre.at[j], got.at[j, second], rs_send.at[j, second], rs_recv.at[j, second], across(second)
            )

    results = []
    for j in range(COL_CHUNKS):
        total = term[j, chip].astype(F32)
        for d in direct:
            arrived(got.at[j, d], rs_recv.at[j, d])
            total += got[j, d].astype(F32)
        out_v[:, j * cols:(j + 1) * cols] = total.astype(BF16)
        results.append(
            pltpu.make_async_copy(
                out_v.at[:, pl.ds(j * cols, cols)], out.at[:, pl.ds(j * cols, cols)], out_sem.at[j]
            )
        )
        results[-1].start()

    for copy in results:
        copy.wait()
    for copy in sends[before:]:
        copy.wait_send()


def solution(mesh):
    ctxs, heads = mesh.shape["ctx"], mesh.shape["head"]
    chips = heads // 2

    def on_device(tokens_in, w_qkv, w_out, codebook, codes, reach):
        blk, depth = tokens_in.shape
        num_codes, hd = codebook.shape[1:]
        wide = w_out.shape[2]
        rp = blk // heads
        cols = wide // COL_CHUNKS
        dma = pltpu.SemaphoreType.DMA
        return pl.pallas_call(
            functools.partial(kernel, (ctxs, heads, blk, hd)),
            out_shape=jax.ShapeDtypeStruct((rp, wide), BF16),
            in_specs=[pl.BlockSpec(memory_space=pltpu.HBM)] * 6,
            out_specs=pl.BlockSpec(memory_space=pltpu.HBM),
            scratch_shapes=[
                pltpu.VMEM((chips, 2, blk, depth), BF16),
                pltpu.VMEM((blk, 3 * hd), F32),
                pltpu.VMEM((heads, depth, 3 * hd), BF16),
                pltpu.VMEM((2 * hd, wide), BF16),
                pltpu.VMEM((num_codes, hd), BF16),
                pltpu.VMEM((1, blk), jnp.int32),
                pltpu.SMEM((1,), jnp.int32),
                pltpu.VMEM((ctxs, blk, hd), BF16),
                pltpu.VMEM((2, blk, hd), BF16),
                pltpu.VMEM((ctxs, blk, hd), BF16),
                pltpu.VMEM((blk, hd), BF16),
                pltpu.VMEM((blk, hd), F32),
                pltpu.VMEM((blk, hd), F32),
                pltpu.VMEM((blk, hd), F32),
                pltpu.VMEM((blk, hd), F32),
                pltpu.VMEM((max(ctxs - 2, 1), blk, blk), F32),
                pltpu.VMEM((max(ctxs - 2, 1), blk, blk), BF16),
                pltpu.VMEM((rp, wide), BF16),
                pltpu.VMEM((2, chips, rp, hd), BF16),
                pltpu.VMEM((chips, rp, hd), BF16),
                pltpu.VMEM((COL_CHUNKS, chips, rp, cols), BF16),
                pltpu.VMEM((COL_CHUNKS, chips, rp, cols), BF16),
                pltpu.VMEM((COL_CHUNKS, rp, cols), BF16),
                dma((6,)),
                dma((ROW_CHUNKS, chips)),
                dma((ROW_CHUNKS, chips)),
                dma((ROW_CHUNKS, chips)),
                dma((ROW_CHUNKS, chips)),
                dma((ROW_CHUNKS, chips)),
                dma((ROW_CHUNKS, chips)),
                dma((2,)),
                dma((ctxs,)),
                dma((ctxs,)),
                dma((ROW_CHUNKS,)),
                dma((ROW_CHUNKS,)),
                dma((ROW_CHUNKS, ctxs)),
                dma((ROW_CHUNKS, ctxs)),
                dma((2,)),
                dma((COL_CHUNKS, chips)),
                dma((COL_CHUNKS, chips)),
                dma((COL_CHUNKS,)),
            ],
            compiler_params=pltpu.CompilerParams(
                collective_id=0, has_side_effects=True, vmem_limit_bytes=60 * 1024 * 1024
            ),
            cost_estimate=pl.CostEstimate(
                flops=2 * blk * heads * depth * 3 * hd, bytes_accessed=6 * 1024 * 1024, transcendentals=blk * blk
            ),
        )(
            tokens_in, w_qkv[:, 0, :].reshape(heads, depth, 3 * hd), w_out[0], codebook[0], codes, reach
        )

    in_specs = (
        P("ctx", "head"),
        P(None, "head", None),
        P("head", None, None),
        P("head", None, None),
        P("head", "ctx"),
        P("ctx"),
    )
    return jax.shard_map(
        on_device, mesh=mesh, in_specs=in_specs, out_specs=P(("ctx", "head"), None), check_vma=False
    )
```

```python
import functools
import math

import jax
import jax.numpy as jnp
from jax import lax
from jax.experimental import pallas as pl
from jax.experimental.pallas import tpu as pltpu
from jax.sharding import PartitionSpec as P

MESH = pl.DeviceIdType.MESH
F32 = jnp.float32
BF16 = jnp.bfloat16
ROW_CHUNKS = 4
COL_CHUNKS = 4
AHEAD = 2
COPIES = 8
GROUPS = ((0,), (1,), (2, 3))


def grid_of(chips):
    wide = 1 << ((chips.bit_length() - 1) // 2)
    return chips // wide, wide


def nt(a, b):
    return lax.dot_general(a, b, (((1,), (1,)), ((), ())), preferred_element_type=F32)


def kernel(
    sizes,
    tok, w_in, w_out, book, codes, reach, out,
    x, proj_s, w, w2, book_v, codes_v, reach_s, kq, kz, vz, q_s, top_s, den_s, acc_s, fade_s, score_s, prob_s, out_v, att, att_p, term, got, pre,
    local_sem, ag_send, ag_recv, fw_send, fw_recv, rl_send, rl_recv, w2_sem, kq_send, kq_recv, k_send, k_recv,
    v_send, v_recv, att_sem, rs_send, rs_recv, out_sem,
):
    ctxs, heads, blk, hd = sizes
    chips = heads // 2
    tall, wide = grid_of(chips)
    scale = 1.0 / math.sqrt(hd)
    rows = blk // ROW_CHUNKS
    cols = out.shape[1] // COL_CHUNKS
    rp = out.shape[0]
    ctx, head = lax.axis_index("ctx"), lax.axis_index("head")
    chip, core = head // 2, head % 2
    partner = (ctx, chip * 2 + 1 - core)

    def chip_at(d, sign):
        up, across = d // wide, d % wide
        row = lax.rem(chip // wide + (up if sign > 0 else tall - up), tall)
        col = lax.rem(chip % wide + (across if sign > 0 else wide - across), wide)
        return row * wide + col

    def remote(src, dst, send, recv, to):
        return pltpu.make_async_remote_copy(
            src_ref=src, dst_ref=dst, send_sem=send, recv_sem=recv, device_id=to, device_id_type=MESH
        )

    def arrived(dst, sem):
        remote(dst, dst, sem, sem, partner).wait_recv()

    copies = [
        pltpu.make_async_copy(codes, codes_v, local_sem.at[0]),
        pltpu.make_async_copy(book, book_v, local_sem.at[1]),
        pltpu.make_async_copy(reach, reach_s, local_sem.at[2]),
        pltpu.make_async_copy(tok, x.at[0, 0], local_sem.at[3]),
        pltpu.make_async_copy(w_in, w, local_sem.at[4]),
        pltpu.make_async_copy(w_out, w2.at[pl.ds(0, hd)], local_sem.at[5]),
    ]
    for copy in copies:
        copy.start()

    relayed = (tall, wide) == (2, 2)
    direct = (1, 2) if relayed else range(1, chips)
    barrier = pltpu.get_barrier_semaphore()
    greet = [partner]
    greet += [(ctx, chip_at(d, 1) * 2 + core) for d in direct]
    greet += [(lax.rem(ctx + e, ctxs), head) for e in range(1, ctxs)]
    for peer in greet:
        pl.semaphore_signal(barrier, inc=1, device_id=peer, device_id_type=MESH)
    pl.semaphore_wait(barrier, len(greet))

    sends = []

    def send(*args):
        copy = remote(*args)
        copy.start()
        sends.append(copy)

    def part(r):
        return pl.ds(r * rows, rows)

    def across(d):
        return (ctx, chip_at(d, 1) * 2 + core)

    def half(r, d):
        return pl.ds(r * rows + (d - 1) * (rows // 2), rows // 2)

    def to_partner(r, d):
        send(x.at[d, 0, part(r)], x.at[d, 1, part(r)], fw_send.at[r, d], fw_recv.at[r, d], partner)

    def take_direct(r):
        for d in direct:
            arrived(x.at[d, 0, part(r)], ag_recv.at[r, d])
            if relayed:
                send(
                    x.at[d, 0, half(r, d)], x.at[3, 0, half(r, d)],
                    rl_send.at[r, d], rl_recv.at[r, d], across(3 - d),
                )
            to_partner(r, d)
        if r + AHEAD < ROW_CHUNKS:
            send_direct(r + AHEAD)

    def send_direct(r):
        for d in direct:
            send(tok.at[part(r)], x.at[d, 0, part(r)], ag_send.at[r, d], ag_recv.at[r, d], across(d))

    for r in range(AHEAD):
        send_direct(r)
    send(tok, x.at[0, 1], fw_send.at[0, 0], fw_recv.at[0, 0], partner)
    send(w_out, w2.at[pl.ds(hd, hd)], w2_sem.at[0], w2_sem.at[1], partner)

    copies[0].wait()
    copies[1].wait()
    num_codes = book_v.shape[0]
    hot = lax.broadcasted_iota(jnp.int32, (num_codes, blk), 0) == codes_v[...]
    kq[0] = lax.dot_general(
        hot.astype(F32).astype(BF16), book_v[...], (((0,), (0,)), ((), ())), preferred_element_type=F32
    ).astype(BF16)

    def later(e, src, dst, send_sem, recv_sem):
        @pl.when(ctx + e < ctxs)
        def _():
            remote(src, dst, send_sem, recv_sem, (lax.rem(ctx + e, ctxs), head)).start()

    for e in range(1, ctxs):
        later(e, kq.at[0], kq.at[e], kq_send.at[e], kq_recv.at[e])

    for copy in copies[2:]:
        copy.wait()

    def piece(d, other, block):
        source = chip_at(d, -1) * 2 + (1 - core if other else core)
        return jnp.dot(x[d, other, block], w[source], preferred_element_type=F32)

    early = direct if relayed else range(1, chips - 1)
    last = chips - 1

    def take_last(r):
        if relayed:
            for d in direct:
                arrived(x.at[3, 0, half(r, d)], rl_recv.at[r, d])
            to_partner(r, 3)

    def project_early(chunks):
        block = slice(chunks[0] * rows, (chunks[-1] + 1) * rows)
        proj = proj_s[block]
        for d in early:
            proj += piece(d, 0, block)
        take_last(chunks[0])
        for d in early:
            for r in chunks:
                arrived(x.at[d, 1, part(r)], fw_recv.at[r, d])
            proj += piece(d, 1, block)
        proj_s[block] = proj

    def project_last(r):
        block = slice(r * rows, (r + 1) * rows)
        proj = proj_s[block] + piece(last, 0, block)
        arrived(x.at[last, 1, part(r)], fw_recv.at[r, last])
        proj += piece(last, 1, block)
        q_s[block] = proj[:, :hd].astype(BF16)
        kz[0, block] = proj[:, hd:2 * hd].astype(BF16)
        vz[0, block] = proj[:, 2 * hd:].astype(BF16)
        later(1, kz.at[0, part(r)], kz.at[1, part(r)], k_send.at[r], k_recv.at[r])
        for e in range(1, ctxs):
            later(e, vz.at[0, part(r)], vz.at[e, part(r)], v_send.at[r, e], v_recv.at[r, e])

    every = slice(0, blk)
    arrived(x.at[0, 1], fw_recv.at[0, 0])
    proj_s[...] = piece(0, 0, every) + piece(0, 1, every)
    for r in range(AHEAD):
        take_direct(r)
    taken = AHEAD
    for chunks in GROUPS:
        while taken <= chunks[-1]:
            take_direct(taken)
            taken += 1
        project_early(chunks)
        if taken < ROW_CHUNKS:
            take_direct(taken)
            taken += 1
        for r in chunks:
            if r > chunks[0]:
                take_last(r)
            project_last(r)

    queries = q_s[...]
    own = nt(queries, kz[0])
    seen = lax.broadcasted_iota(jnp.int32, own.shape, 1) <= lax.broadcasted_iota(jnp.int32, own.shape, 0)
    own = jnp.where(seen, own, -jnp.inf)
    top_s[...] = jnp.broadcast_to(jnp.max(own, axis=1, keepdims=True), top_s.shape)
    for e in range(2, ctxs):
        @pl.when(ctx >= e)
        def _():
            arrived(kq.at[e], kq_recv.at[e])
            scores = nt(q_s[...], kq[e])
            score_s[e - 2] = scores
            top_s[...] = jnp.maximum(top_s[...], jnp.max(scores, axis=1, keepdims=True))

    probs = jnp.exp((own - top_s[...][:, :1]) * scale)
    den_s[...] = jnp.broadcast_to(jnp.sum(probs, axis=1, keepdims=True), den_s.shape)
    acc_s[...] = jnp.dot(probs.astype(BF16), vz[0], preferred_element_type=F32)
    for e in range(2, ctxs):
        @pl.when(ctx >= e)
        def _():
            probs = jnp.exp((score_s[e - 2] - top_s[...][:, :1]) * scale)
            prob_s[e - 2] = probs.astype(BF16)
            den_s[...] += jnp.sum(probs, axis=1, keepdims=True)

    @pl.when(ctx >= 1)
    def _():
        arrived(kq.at[1], kq_recv.at[1])
        for r in range(ROW_CHUNKS):
            arrived(kz.at[1, part(r)], k_recv.at[r])
        keys = kq[1]
        position = lax.broadcasted_iota(jnp.int32, keys.shape, 0)
        keys = jnp.where(position >= blk - reach_s[0], kz[1], keys)
        scores = nt(q_s[...], keys)
        old = top_s[...]
        top = jnp.maximum(old, jnp.max(scores, axis=1, keepdims=True))
        fade = jnp.exp((old - top) * scale)
        probs = jnp.exp((scores - top[:, :1]) * scale)
        fade_s[...] = fade
        den_s[...] = den_s[...] * fade + jnp.sum(probs, axis=1, keepdims=True)
        for r in range(ROW_CHUNKS):
            arrived(vz.at[1, part(r)], v_recv.at[r, 1])
        acc_s[...] = acc_s[...] * fade + jnp.dot(
            probs.astype(BF16), vz[1], preferred_element_type=F32
        )

    for e in range(2, ctxs):
        @pl.when(ctx >= e)
        def _():
            for r in range(ROW_CHUNKS):
                arrived(vz.at[e, part(r)], v_recv.at[r, e])
            acc_s[...] += fade_s[...] * jnp.dot(prob_s[e - 2], vz[e], preferred_element_type=F32)

    attended = acc_s[...] / den_s[...]
    for h in range(heads):
        att[h % 2, h // 2] = attended[h * rp:(h + 1) * rp].astype(BF16)
    send(att.at[1 - core], att_p, att_sem.at[0], att_sem.at[1], partner)
    mine = att[core].astype(F32).reshape(chips * rp, hd).astype(BF16)
    arrived(att_p, att_sem.at[1])
    other = att_p[...].astype(F32).reshape(chips * rp, hd).astype(BF16)
    arrived(w2.at[pl.ds(hd, hd)], w2_sem.at[1])
    both = jnp.concatenate([mine, other], axis=1)

    before = len(sends)
    for j in range(COL_CHUNKS):
        block = jnp.dot(both, w2[:, j * cols:(j + 1) * cols], preferred_element_type=F32)
        for c in range(chips):
            term[j, c] = block[c * rp:(c + 1) * rp].astype(BF16)
        if relayed:
            first = 1 + j % 2
            send(term.at[j, chip_at(3, 1)], got.at[j, 3], rs_send.at[j, 3], rs_recv.at[j, 3], across(first))
        else:
            for d in direct:
                send(term.at[j, chip_at(d, 1)], got.at[j, d], rs_send.at[j, d], rs_recv.at[j, d], across(d))

    if relayed:
        for j in range(COL_CHUNKS):
            first = 1 + j % 2
            send(
                term.at[j, chip_at(first, 1)], got.at[j, first],
                rs_send.at[j, first], rs_recv.at[j, first], across(first),
            )
    for copy in sends[:before]:
        copy.wait_send()
    for e in range(1, ctxs):
        @pl.when(ctx + e < ctxs)
        def _():
            remote(kq.at[0], kq.at[e], kq_send.at[e], kq_recv.at[e], partner).wait_send()
            for r in range(ROW_CHUNKS):
                if e == 1:
                    remote(kz.at[0, part(r)], kz.at[1, part(r)], k_send.at[r], k_recv.at[r], partner).wait_send()
                remote(
                    vz.at[0, part(r)], vz.at[e, part(r)], v_send.at[r, e], v_recv.at[r, e], partner
                ).wait_send()

    if relayed:
        for j in range(COL_CHUNKS):
            second = 2 - j % 2
            arrived(got.at[j, 3], rs_recv.at[j, 3])
            pair = got[j, 3].astype(F32) + term[j, chip_at(second, 1)].astype(F32)
            pre[j] = pair.astype(BF16)
            send(
                pre.at[j], got.at[j, second], rs_send.at[j, second], rs_recv.at[j, second], across(second)
            )

    results = []
    for j in range(COL_CHUNKS):
        total = term[j, chip].astype(F32)
        for d in direct:
            arrived(got.at[j, d], rs_recv.at[j, d])
            total += got[j, d].astype(F32)
        out_v[:, j * cols:(j + 1) * cols] = total.astype(BF16)
        results.append(
            pltpu.make_async_copy(
                out_v.at[:, pl.ds(j * cols, cols)], out.at[:, pl.ds(j * cols, cols)], out_sem.at[j]
            )
        )
        results[-1].start()

    for copy in results:
        copy.wait()
    for copy in sends[before:]:
        copy.wait_send()


def hand_over(src, dst, sems):
    width = src.shape[1] // COPIES
    copies = [
        pltpu.make_async_copy(
            src.at[:, pl.ds(i * width, width)], dst.at[:, pl.ds(i * width, width)], sems.at[i]
        )
        for i in range(COPIES)
    ]
    for copy in copies:
        copy.start()
    for copy in copies:
        copy.wait()


def solution(mesh):
    ctxs, heads = mesh.shape["ctx"], mesh.shape["head"]
    chips = heads // 2

    def on_device(tokens_in, w_qkv, w_out, codebook, codes, reach):
        blk, depth = tokens_in.shape
        num_codes, hd = codebook.shape[1:]
        wide = w_out.shape[2]
        rp = blk // heads
        cols = wide // COL_CHUNKS
        dma = pltpu.SemaphoreType.DMA
        mixed = pl.pallas_call(
            functools.partial(kernel, (ctxs, heads, blk, hd)),
            out_shape=jax.ShapeDtypeStruct((rp, wide), BF16),
            in_specs=[pl.BlockSpec(memory_space=pltpu.HBM)] * 6,
            out_specs=pl.BlockSpec(memory_space=pltpu.HBM),
            scratch_shapes=[
                pltpu.VMEM((chips, 2, blk, depth), BF16),
                pltpu.VMEM((blk, 3 * hd), F32),
                pltpu.VMEM((heads, depth, 3 * hd), BF16),
                pltpu.VMEM((2 * hd, wide), BF16),
                pltpu.VMEM((num_codes, hd), BF16),
                pltpu.VMEM((1, blk), jnp.int32),
                pltpu.SMEM((1,), jnp.int32),
                pltpu.VMEM((ctxs, blk, hd), BF16),
                pltpu.VMEM((2, blk, hd), BF16),
                pltpu.VMEM((ctxs, blk, hd), BF16),
                pltpu.VMEM((blk, hd), BF16),
                pltpu.VMEM((blk, hd), F32),
                pltpu.VMEM((blk, hd), F32),
                pltpu.VMEM((blk, hd), F32),
                pltpu.VMEM((blk, hd), F32),
                pltpu.VMEM((max(ctxs - 2, 1), blk, blk), F32),
                pltpu.VMEM((max(ctxs - 2, 1), blk, blk), BF16),
                pltpu.VMEM((rp, wide), BF16),
                pltpu.VMEM((2, chips, rp, hd), BF16),
                pltpu.VMEM((chips, rp, hd), BF16),
                pltpu.VMEM((COL_CHUNKS, chips, rp, cols), BF16),
                pltpu.VMEM((COL_CHUNKS, chips, rp, cols), BF16),
                pltpu.VMEM((COL_CHUNKS, rp, cols), BF16),
                dma((6,)),
                dma((ROW_CHUNKS, chips)),
                dma((ROW_CHUNKS, chips)),
                dma((ROW_CHUNKS, chips)),
                dma((ROW_CHUNKS, chips)),
                dma((ROW_CHUNKS, chips)),
                dma((ROW_CHUNKS, chips)),
                dma((2,)),
                dma((ctxs,)),
                dma((ctxs,)),
                dma((ROW_CHUNKS,)),
                dma((ROW_CHUNKS,)),
                dma((ROW_CHUNKS, ctxs)),
                dma((ROW_CHUNKS, ctxs)),
                dma((2,)),
                dma((COL_CHUNKS, chips)),
                dma((COL_CHUNKS, chips)),
                dma((COL_CHUNKS,)),
            ],
            compiler_params=pltpu.CompilerParams(
                collective_id=0, has_side_effects=True, vmem_limit_bytes=60 * 1024 * 1024
            ),
            cost_estimate=pl.CostEstimate(
                flops=2 * blk * heads * depth * 3 * hd, bytes_accessed=6 * 1024 * 1024, transcendentals=blk * blk
            ),
        )(
            tokens_in, w_qkv[:, 0, :].reshape(heads, depth, 3 * hd), w_out[0], codebook[0], codes, reach
        )
        return pl.pallas_call(
            hand_over,
            out_shape=jax.ShapeDtypeStruct((rp, wide), BF16),
            in_specs=[pl.BlockSpec(memory_space=pltpu.HBM)],
            out_specs=pl.BlockSpec(memory_space=pltpu.HBM),
            scratch_shapes=[dma((COPIES,))],
            compiler_params=pltpu.CompilerParams(vmem_limit_bytes=60 * 1024 * 1024),
        )(mixed)

    in_specs = (
        P("ctx", "head"),
        P(None, "head", None),
        P("head", None, None),
        P("head", None, None),
        P("head", "ctx"),
        P("ctx"),
    )
    return jax.shard_map(
        on_device, mesh=mesh, in_specs=in_specs, out_specs=P(("ctx", "head"), None), check_vma=False
    )
```

```python
import functools
import math

import jax
import jax.numpy as jnp
from jax import lax
from jax.experimental import pallas as pl
from jax.experimental.pallas import tpu as pltpu
from jax.sharding import PartitionSpec as P

MESH = pl.DeviceIdType.MESH
F32 = jnp.float32
BF16 = jnp.bfloat16
ROW_CHUNKS = 4
COL_CHUNKS = 4
AHEAD = 2
GROUPS = ((0,), (1,), (2, 3))


def grid_of(chips):
    wide = 1 << ((chips.bit_length() - 1) // 2)
    return chips // wide, wide


def nt(a, b):
    return lax.dot_general(a, b, (((1,), (1,)), ((), ())), preferred_element_type=F32)


def kernel(
    sizes,
    tok, w_in, w_out, book, codes, reach, out,
    x, proj_s, w, w2, book_v, codes_v, reach_s, kq, kz, vz, q_s, top_s, den_s, acc_s, fade_s, score_s, prob_s, out_v, att, att_p, term, got, pre,
    local_sem, ag_send, ag_recv, fw_send, fw_recv, rl_send, rl_recv, w2_sem, kq_send, kq_recv, k_send, k_recv,
    v_send, v_recv, att_sem, rs_send, rs_recv, out_sem,
):
    ctxs, heads, blk, hd = sizes
    chips = heads // 2
    tall, wide = grid_of(chips)
    scale = 1.0 / math.sqrt(hd)
    rows = blk // ROW_CHUNKS
    cols = out.shape[1] // COL_CHUNKS
    rp = out.shape[0]
    ctx, head = lax.axis_index("ctx"), lax.axis_index("head")
    chip, core = head // 2, head % 2
    partner = (ctx, chip * 2 + 1 - core)

    def chip_at(d, sign):
        up, across = d // wide, d % wide
        row = lax.rem(chip // wide + (up if sign > 0 else tall - up), tall)
        col = lax.rem(chip % wide + (across if sign > 0 else wide - across), wide)
        return row * wide + col

    def remote(src, dst, send, recv, to):
        return pltpu.make_async_remote_copy(
            src_ref=src, dst_ref=dst, send_sem=send, recv_sem=recv, device_id=to, device_id_type=MESH
        )

    def arrived(dst, sem):
        remote(dst, dst, sem, sem, partner).wait_recv()

    copies = [
        pltpu.make_async_copy(codes, codes_v, local_sem.at[0]),
        pltpu.make_async_copy(book, book_v, local_sem.at[1]),
        pltpu.make_async_copy(reach, reach_s, local_sem.at[2]),
        pltpu.make_async_copy(tok, x.at[0, 0], local_sem.at[3]),
        pltpu.make_async_copy(w_in, w, local_sem.at[4]),
        pltpu.make_async_copy(w_out, w2.at[pl.ds(0, hd)], local_sem.at[5]),
    ]
    for copy in copies:
        copy.start()

    relayed = (tall, wide) == (2, 2)
    direct = (1, 2) if relayed else range(1, chips)
    barrier = pltpu.get_barrier_semaphore()
    greet = [partner]
    greet += [(ctx, chip_at(d, 1) * 2 + core) for d in direct]
    greet += [(lax.rem(ctx + e, ctxs), head) for e in range(1, ctxs)]
    for peer in greet:
        pl.semaphore_signal(barrier, inc=1, device_id=peer, device_id_type=MESH)
    pl.semaphore_wait(barrier, len(greet))

    sends = []

    def send(*args):
        copy = remote(*args)
        copy.start()
        sends.append(copy)

    def part(r):
        return pl.ds(r * rows, rows)

    def across(d):
        return (ctx, chip_at(d, 1) * 2 + core)

    def half(r, d):
        return pl.ds(r * rows + (d - 1) * (rows // 2), rows // 2)

    def to_partner(r, d):
        send(x.at[d, 0, part(r)], x.at[d, 1, part(r)], fw_send.at[r, d], fw_recv.at[r, d], partner)

    def take_direct(r):
        for d in direct:
            arrived(x.at[d, 0, part(r)], ag_recv.at[r, d])
            if relayed:
                send(
                    x.at[d, 0, half(r, d)], x.at[3, 0, half(r, d)],
                    rl_send.at[r, d], rl_recv.at[r, d], across(3 - d),
                )
            to_partner(r, d)
        if r + AHEAD < ROW_CHUNKS:
            send_direct(r + AHEAD)

    def send_direct(r):
        for d in direct:
            own = tok if r < AHEAD else x.at[0, 0]
            send(own.at[part(r)], x.at[d, 0, part(r)], ag_send.at[r, d], ag_recv.at[r, d], across(d))

    for r in range(AHEAD):
        send_direct(r)
    send(tok, x.at[0, 1], fw_send.at[0, 0], fw_recv.at[0, 0], partner)
    send(w_out, w2.at[pl.ds(hd, hd)], w2_sem.at[0], w2_sem.at[1], partner)

    copies[0].wait()
    copies[1].wait()
    num_codes = book_v.shape[0]
    hot = lax.broadcasted_iota(jnp.int32, (num_codes, blk), 0) == codes_v[...]
    kq[0] = lax.dot_general(
        hot.astype(F32).astype(BF16), book_v[...], (((0,), (0,)), ((), ())), preferred_element_type=F32
    ).astype(BF16)

    def later(e, src, dst, send_sem, recv_sem):
        @pl.when(ctx + e < ctxs)
        def _():
            remote(src, dst, send_sem, recv_sem, (lax.rem(ctx + e, ctxs), head)).start()

    for e in range(1, ctxs):
        later(e, kq.at[0], kq.at[e], kq_send.at[e], kq_recv.at[e])

    for copy in copies[2:]:
        copy.wait()

    def piece(d, other, block):
        source = chip_at(d, -1) * 2 + (1 - core if other else core)
        return jnp.dot(x[d, other, block], w[source], preferred_element_type=F32)

    early = direct if relayed else range(1, chips - 1)
    last = chips - 1

    def take_last(r):
        if relayed:
            for d in direct:
                arrived(x.at[3, 0, half(r, d)], rl_recv.at[r, d])
            to_partner(r, 3)

    def project_early(chunks):
        block = slice(chunks[0] * rows, (chunks[-1] + 1) * rows)
        proj = proj_s[block]
        for d in early:
            proj += piece(d, 0, block)
        take_last(chunks[0])
        for d in early:
            for r in chunks:
                arrived(x.at[d, 1, part(r)], fw_recv.at[r, d])
            proj += piece(d, 1, block)
        proj_s[block] = proj

    def project_last(r):
        block = slice(r * rows, (r + 1) * rows)
        proj = proj_s[block] + piece(last, 0, block)
        arrived(x.at[last, 1, part(r)], fw_recv.at[r, last])
        proj += piece(last, 1, block)
        q_s[block] = proj[:, :hd].astype(BF16)
        kz[0, block] = proj[:, hd:2 * hd].astype(BF16)
        vz[0, block] = proj[:, 2 * hd:].astype(BF16)
        later(1, kz.at[0, part(r)], kz.at[1, part(r)], k_send.at[r], k_recv.at[r])
        for e in range(1, ctxs):
            later(e, vz.at[0, part(r)], vz.at[e, part(r)], v_send.at[r, e], v_recv.at[r, e])

    every = slice(0, blk)
    arrived(x.at[0, 1], fw_recv.at[0, 0])
    proj_s[...] = piece(0, 0, every) + piece(0, 1, every)
    for r in range(AHEAD):
        take_direct(r)
    taken = AHEAD
    for chunks in GROUPS:
        while taken <= chunks[-1]:
            take_direct(taken)
            taken += 1
        project_early(chunks)
        if taken < ROW_CHUNKS:
            take_direct(taken)
            taken += 1
        for r in chunks:
            if r > chunks[0]:
                take_last(r)
            project_last(r)

    queries = q_s[...]
    own = nt(queries, kz[0])
    seen = lax.broadcasted_iota(jnp.int32, own.shape, 1) <= lax.broadcasted_iota(jnp.int32, own.shape, 0)
    own = jnp.where(seen, own, -jnp.inf)
    top_s[...] = jnp.broadcast_to(jnp.max(own, axis=1, keepdims=True), top_s.shape)
    for e in range(2, ctxs):
        @pl.when(ctx >= e)
        def _():
            arrived(kq.at[e], kq_recv.at[e])
            scores = nt(q_s[...], kq[e])
            score_s[e - 2] = scores
            top_s[...] = jnp.maximum(top_s[...], jnp.max(scores, axis=1, keepdims=True))

    probs = jnp.exp((own - top_s[...][:, :1]) * scale)
    den_s[...] = jnp.broadcast_to(jnp.sum(probs, axis=1, keepdims=True), den_s.shape)
    acc_s[...] = jnp.dot(probs.astype(BF16), vz[0], preferred_element_type=F32)
    for e in range(2, ctxs):
        @pl.when(ctx >= e)
        def _():
            probs = jnp.exp((score_s[e - 2] - top_s[...][:, :1]) * scale)
            prob_s[e - 2] = probs.astype(BF16)
            den_s[...] += jnp.sum(probs, axis=1, keepdims=True)

    @pl.when(ctx >= 1)
    def _():
        arrived(kq.at[1], kq_recv.at[1])
        for r in range(ROW_CHUNKS):
            arrived(kz.at[1, part(r)], k_recv.at[r])
        keys = kq[1]
        position = lax.broadcasted_iota(jnp.int32, keys.shape, 0)
        keys = jnp.where(position >= blk - reach_s[0], kz[1], keys)
        scores = nt(q_s[...], keys)
        old = top_s[...]
        top = jnp.maximum(old, jnp.max(scores, axis=1, keepdims=True))
        fade = jnp.exp((old - top) * scale)
        probs = jnp.exp((scores - top[:, :1]) * scale)
        fade_s[...] = fade
        den_s[...] = den_s[...] * fade + jnp.sum(probs, axis=1, keepdims=True)
        for r in range(ROW_CHUNKS):
            arrived(vz.at[1, part(r)], v_recv.at[r, 1])
        acc_s[...] = acc_s[...] * fade + jnp.dot(
            probs.astype(BF16), vz[1], preferred_element_type=F32
        )

    for e in range(2, ctxs):
        @pl.when(ctx >= e)
        def _():
            for r in range(ROW_CHUNKS):
                arrived(vz.at[e, part(r)], v_recv.at[r, e])
            acc_s[...] += fade_s[...] * jnp.dot(prob_s[e - 2], vz[e], preferred_element_type=F32)

    attended = acc_s[...] / den_s[...]
    for h in range(heads):
        att[h % 2, h // 2] = attended[h * rp:(h + 1) * rp].astype(BF16)
    send(att.at[1 - core], att_p, att_sem.at[0], att_sem.at[1], partner)
    mine = att[core].astype(F32).reshape(chips * rp, hd).astype(BF16)
    arrived(att_p, att_sem.at[1])
    other = att_p[...].astype(F32).reshape(chips * rp, hd).astype(BF16)
    arrived(w2.at[pl.ds(hd, hd)], w2_sem.at[1])
    both = jnp.concatenate([mine, other], axis=1)

    before = len(sends)
    for j in range(COL_CHUNKS):
        block = jnp.dot(both, w2[:, j * cols:(j + 1) * cols], preferred_element_type=F32)
        for c in range(chips):
            term[j, c] = block[c * rp:(c + 1) * rp].astype(BF16)
        if relayed:
            first = 1 + j % 2
            send(term.at[j, chip_at(3, 1)], got.at[j, 3], rs_send.at[j, 3], rs_recv.at[j, 3], across(first))
        else:
            for d in direct:
                send(term.at[j, chip_at(d, 1)], got.at[j, d], rs_send.at[j, d], rs_recv.at[j, d], across(d))

    if relayed:
        for j in range(COL_CHUNKS):
            first = 1 + j % 2
            send(
                term.at[j, chip_at(first, 1)], got.at[j, first],
                rs_send.at[j, first], rs_recv.at[j, first], across(first),
            )
    for copy in sends[:before]:
        copy.wait_send()
    for e in range(1, ctxs):
        @pl.when(ctx + e < ctxs)
        def _():
            remote(kq.at[0], kq.at[e], kq_send.at[e], kq_recv.at[e], partner).wait_send()
            for r in range(ROW_CHUNKS):
                if e == 1:
                    remote(kz.at[0, part(r)], kz.at[1, part(r)], k_send.at[r], k_recv.at[r], partner).wait_send()
                remote(
                    vz.at[0, part(r)], vz.at[e, part(r)], v_send.at[r, e], v_recv.at[r, e], partner
                ).wait_send()

    if relayed:
        for j in range(COL_CHUNKS):
            second = 2 - j % 2
            arrived(got.at[j, 3], rs_recv.at[j, 3])
            pair = got[j, 3].astype(F32) + term[j, chip_at(second, 1)].astype(F32)
            pre[j] = pair.astype(BF16)
            send(
                pre.at[j], got.at[j, second], rs_send.at[j, second], rs_recv.at[j, second], across(second)
            )

    results = []
    for j in range(COL_CHUNKS):
        total = term[j, chip].astype(F32)
        for d in direct:
            arrived(got.at[j, d], rs_recv.at[j, d])
            total += got[j, d].astype(F32)
        out_v[:, j * cols:(j + 1) * cols] = total.astype(BF16)
        results.append(
            pltpu.make_async_copy(
                out_v.at[:, pl.ds(j * cols, cols)], out.at[:, pl.ds(j * cols, cols)], out_sem.at[j]
            )
        )
        results[-1].start()

    for copy in results:
        copy.wait()
    for copy in sends[before:]:
        copy.wait_send()


def solution(mesh):
    ctxs, heads = mesh.shape["ctx"], mesh.shape["head"]
    chips = heads // 2

    def on_device(tokens_in, w_qkv, w_out, codebook, codes, reach):
        blk, depth = tokens_in.shape
        num_codes, hd = codebook.shape[1:]
        wide = w_out.shape[2]
        rp = blk // heads
        cols = wide // COL_CHUNKS
        dma = pltpu.SemaphoreType.DMA
        return pl.pallas_call(
            functools.partial(kernel, (ctxs, heads, blk, hd)),
            out_shape=jax.ShapeDtypeStruct((rp, wide), BF16),
            in_specs=[pl.BlockSpec(memory_space=pltpu.HBM)] * 6,
            out_specs=pl.BlockSpec(memory_space=pltpu.HBM),
            scratch_shapes=[
                pltpu.VMEM((chips, 2, blk, depth), BF16),
                pltpu.VMEM((blk, 3 * hd), F32),
                pltpu.VMEM((heads, depth, 3 * hd), BF16),
                pltpu.VMEM((2 * hd, wide), BF16),
                pltpu.VMEM((num_codes, hd), BF16),
                pltpu.VMEM((1, blk), jnp.int32),
                pltpu.SMEM((1,), jnp.int32),
                pltpu.VMEM((ctxs, blk, hd), BF16),
                pltpu.VMEM((2, blk, hd), BF16),
                pltpu.VMEM((ctxs, blk, hd), BF16),
                pltpu.VMEM((blk, hd), BF16),
                pltpu.VMEM((blk, hd), F32),
                pltpu.VMEM((blk, hd), F32),
                pltpu.VMEM((blk, hd), F32),
                pltpu.VMEM((blk, hd), F32),
                pltpu.VMEM((max(ctxs - 2, 1), blk, blk), F32),
                pltpu.VMEM((max(ctxs - 2, 1), blk, blk), BF16),
                pltpu.VMEM((rp, wide), BF16),
                pltpu.VMEM((2, chips, rp, hd), BF16),
                pltpu.VMEM((chips, rp, hd), BF16),
                pltpu.VMEM((COL_CHUNKS, chips, rp, cols), BF16),
                pltpu.VMEM((COL_CHUNKS, chips, rp, cols), BF16),
                pltpu.VMEM((COL_CHUNKS, rp, cols), BF16),
                dma((6,)),
                dma((ROW_CHUNKS, chips)),
                dma((ROW_CHUNKS, chips)),
                dma((ROW_CHUNKS, chips)),
                dma((ROW_CHUNKS, chips)),
                dma((ROW_CHUNKS, chips)),
                dma((ROW_CHUNKS, chips)),
                dma((2,)),
                dma((ctxs,)),
                dma((ctxs,)),
                dma((ROW_CHUNKS,)),
                dma((ROW_CHUNKS,)),
                dma((ROW_CHUNKS, ctxs)),
                dma((ROW_CHUNKS, ctxs)),
                dma((2,)),
                dma((COL_CHUNKS, chips)),
                dma((COL_CHUNKS, chips)),
                dma((COL_CHUNKS,)),
            ],
            compiler_params=pltpu.CompilerParams(
                collective_id=0, has_side_effects=True, vmem_limit_bytes=60 * 1024 * 1024
            ),
            cost_estimate=pl.CostEstimate(
                flops=2 * blk * heads * depth * 3 * hd, bytes_accessed=6 * 1024 * 1024, transcendentals=blk * blk
            ),
        )(
            tokens_in, w_qkv[:, 0, :].reshape(heads, depth, 3 * hd), w_out[0], codebook[0], codes, reach
        )

    in_specs = (
        P("ctx", "head"),
        P(None, "head", None),
        P("head", None, None),
        P("head", None, None),
        P("head", "ctx"),
        P("ctx"),
    )
    return jax.shard_map(
        on_device, mesh=mesh, in_specs=in_specs, out_specs=P(("ctx", "head"), None), check_vma=False
    )
```
